256 devices in a mesh: gx: 4 (over y), gy: 8 (over z), gz: 8 (over x, core).
Axes of the slice: x: 4, y: 4, z: 8, core: 2. Of those that a mesh axis runs over, the one named last changes fastest.
Arguments:
- populations: float32 [19, 16, 128, 1024], P(None, 'gx', 'gy', 'gz'), may hold values from 0 to 0.6, as said below
- design: float32 [16, 128, 1024], P('gx', 'gy', 'gz'), may hold values from 0 to 1
- labels: int32 [16, 128, 1024], P('gx', 'gy', 'gz'), may hold values from 1 to 4, as said below
Outputs:
- adjoint: float32 [19, 16, 128, 1024], P(None, 'gx', 'gy', 'gz')
- sensitivity: float32 [16, 128, 1024], P('gx', 'gy', 'gz')
- objective: float32 [], replicated
The draws below stay inside these ranges and needn't reach their ends.
Inputs may be any that keep to these rules, and one draw needn't show every extreme that they name: `labels`: cells on the four side faces (x or y first or last) are 2; otherwise the first z layer is 3 and the last is 4; inside, cells are 1 or 2. Positive populations near equilibrium with density near 1 and speeds below 0.2.
All inputs are finite; a program needn't handle non-finite values.
Results may differ from the reference program's by a relative error of at most 0.0003.
Values sent between devices are 32-bit elements; how exact they have to be, the bound alone decides.
A program may use at most 64 MiB of HBM per device.

```python
import jax
import jax.numpy as jnp
from jax import lax

NX = 16
NY = 128
NZ = 1024


LATTICE = [(0, 0, 0), (1, 0, 0), (-1, 0, 0), (0, 1, 0), (0, -1, 0), (0, 0, 1), (0, 0, -1), (1, 1, 0), (-1, -1, 0), (1, -1, 0), (-1, 1, 0), (1, 0, 1), (-1, 0, -1), (1, 0, -1), (-1, 0, 1), (0, 1, 1), (0, -1, -1), (0, 1, -1), (0, -1, 1)]


LATTICE_WEIGHTS = [1.0 / 3.0] + [1.0 / 18.0] * 6 + [1.0 / 36.0] * 12


def draw_labels(key, part):
    key = jax.random.fold_in(key, 11)
    shape = (NX, NY, NZ)
    xpos = lax.broadcasted_iota(jnp.int32, shape, 0)
    ypos = lax.broadcasted_iota(jnp.int32, shape, 1)
    zpos = lax.broadcasted_iota(jnp.int32, shape, 2)
    rough = jax.random.randint(key, shape, 0, 10)
    result = jnp.where(rough == 0, 2, 1)
    result = jnp.where(zpos == 0, 3, result)
    result = jnp.where(zpos == NZ - 1, 4, result)
    side = (xpos == 0) | (xpos == NX - 1) | (ypos == 0) | (ypos == NY - 1)
    return jnp.where(side, 2, result).astype(jnp.int32)


def draw_design(key, part):
    key = jax.random.fold_in(key, 12)
    shape = (NX, NY, NZ)
    zpos = lax.broadcasted_iota(jnp.int32, shape, 2).astype(jnp.float32)
    drawn = jax.random.uniform(key, shape, jnp.float32)
    ramp = 0.2 + 0.8 * (zpos + 0.5) / NZ
    return (drawn * ramp).astype(jnp.float32)


def draw_populations(key, part):
    key = jax.random.fold_in(key, 13)
    shape = (NX, NY, NZ)
    keys = jax.random.split(key, 5)
    density = 1.0 + 0.05 * jax.random.uniform(keys[0], shape, jnp.float32, -1.0, 1.0)
    speed = [jax.random.uniform(keys[1 + a], shape, jnp.float32, -0.06, 0.06) for a in range(3)]
    speed[2] = speed[2] + 0.04
    square = speed[0] * speed[0] + speed[1] * speed[1] + speed[2] * speed[2]
    rows = []
    for index in range(19):
        along = LATTICE[index][0] * speed[0] + LATTICE[index][1] * speed[1] + LATTICE[index][2] * speed[2]
        rows.append(LATTICE_WEIGHTS[index] * density * (1.0 + 3.0 * along + 4.5 * along * along - 1.5 * square))
    noise = 1.0 + 0.05 * jax.random.uniform(keys[4], (19,) + shape, jnp.float32, -1.0, 1.0)
    return (jnp.stack(rows) * noise).astype(jnp.float32)


def setup_inputs(seed: int = 0) -> dict:
    streams_of = jax.random.split(jax.random.key(seed), 4)
    populations = draw_populations(jax.random.fold_in(streams_of[3], 71), 0)
    design = draw_design(jax.random.fold_in(streams_of[3], 71), 0)
    labels = draw_labels(jax.random.fold_in(streams_of[3], 71), 0)
    return {"populations": populations, "design": design, "labels": labels}


VELOCITY = [(0, 0, 0), (1, 0, 0), (-1, 0, 0), (0, 1, 0), (0, -1, 0), (0, 0, 1), (0, 0, -1), (1, 1, 0), (-1, -1, 0), (1, -1, 0), (-1, 1, 0), (1, 0, 1), (-1, 0, -1), (1, 0, -1), (-1, 0, 1), (0, 1, 1), (0, -1, -1), (0, 1, -1), (0, -1, 1)]
WEIGHTS = [1.0 / 3.0] + [1.0 / 18.0] * 6 + [1.0 / 36.0] * 12
OPPOSITE = [0, 2, 1, 4, 3, 6, 5, 8, 7, 10, 9, 12, 11, 14, 13, 16, 15, 18, 17]
RELAX = 1.6
INFLOW = 0.05

def equilibrium(density, speed):
    square = speed[0] * speed[0] + speed[1] * speed[1] + speed[2] * speed[2]
    rows = []
    for index in range(19):
        along = VELOCITY[index][0] * speed[0] + VELOCITY[index][1] * speed[1] + VELOCITY[index][2] * speed[2]
        rows.append(WEIGHTS[index] * density * (1.0 + 3.0 * along + 4.5 * along * along - 1.5 * square))
    return jnp.stack(rows)

def velocity(field, safe):
    result = []
    for axis in range(3):
        total = jnp.zeros_like(safe)
        for index in range(19):
            if VELOCITY[index][axis] != 0:
                total = total + VELOCITY[index][axis] * field[index]
        result.append(total / safe)
    return result

def collide(field, design, labels):
    density = lax.optimization_barrier(jnp.sum(field, axis=0))
    safe = jnp.where(labels > 0, density, 1.0)
    speed = velocity(field, safe)
    damping = 1.0 / (1.0 + design)
    relaxed = field - RELAX * (field - equilibrium(safe, [s * damping for s in speed]))
    bounce = jnp.stack([field[j] for j in OPPOSITE])
    ones = jnp.ones_like(density)
    zeros = jnp.zeros_like(density)
    inlet = equilibrium(ones, [zeros, zeros, zeros + INFLOW])
    outlet = equilibrium(ones, speed)
    marks = labels[None]
    result = jnp.where(marks == 1, relaxed, 0.0)
    result = jnp.where(marks == 2, bounce, result)
    result = jnp.where(marks == 3, inlet, result)
    return jnp.where(marks == 4, outlet, result)

def stream(field, sign):
    padded = jnp.pad(field, ((0, 0), (1, 1), (1, 1), (1, 1)))
    sizes = field.shape[1:]
    rows = []
    for index in range(19):
        start = [1 - sign * VELOCITY[index][a] for a in range(3)]
        rows.append(padded[index, start[0]:start[0] + sizes[0], start[1]:start[1] + sizes[1], start[2]:start[2] + sizes[2]])
    return jnp.stack(rows)

def dissipation(field, design, labels):
    density = lax.optimization_barrier(jnp.sum(field, axis=0))
    safe = jnp.where(labels > 0, density, 1.0)
    speed = velocity(field, safe)
    square = speed[0] * speed[0] + speed[1] * speed[1] + speed[2] * speed[2]
    return 10.0 * jnp.sum(jnp.where(labels == 1, design * safe * square, 0.0))

def reference(populations, design, labels):
    middle = stream(collide(populations, design, labels), 1)
    final = stream(collide(middle, design, labels), 1)
    total, (final_grad, direct) = jax.value_and_grad(dissipation, argnums=(0, 1))(final, design, labels)
    _, back_two = jax.vjp(lambda f, d: collide(f, d, labels), middle, design)
    back_mid, sens_two = back_two(stream(final_grad, -1))
    _, back_one = jax.vjp(lambda f, d: collide(f, d, labels), populations, design)
    adjoint, sens_one = back_one(stream(back_mid, -1))
    raw = direct + sens_two + sens_one
    cells = NX * NY * NZ
    scale = jnp.sum(jnp.abs(raw)) / cells + 1e-06
    return (adjoint, raw / scale, 20.0 * total / cells)
```

```python
import jax
import jax.numpy as jnp
from jax import lax
from jax.experimental import pallas as pl
from jax.experimental.pallas import tpu as pltpu
from jax.sharding import PartitionSpec as P

VELOCITY = [
    (0, 0, 0),
    (1, 0, 0),
    (-1, 0, 0),
    (0, 1, 0),
    (0, -1, 0),
    (0, 0, 1),
    (0, 0, -1),
    (1, 1, 0),
    (-1, -1, 0),
    (1, -1, 0),
    (-1, 1, 0),
    (1, 0, 1),
    (-1, 0, -1),
    (1, 0, -1),
    (-1, 0, 1),
    (0, 1, 1),
    (0, -1, -1),
    (0, 1, -1),
    (0, -1, 1),
]
OPPOSITE = [0, 2, 1, 4, 3, 6, 5, 8, 7, 10, 9, 12, 11, 14, 13, 16, 15, 18, 17]
PAIRS = [1, 3, 5, 7, 9, 11, 13, 15, 17]
RELAX = 1.6
INFLOW = 0.05
MESH = pl.DeviceIdType.MESH
F32 = jnp.float32

ORDER = [9, 1, 11, 13, 7, 3, 15, 17, 10, 2, 12, 14, 8, 4, 16, 18, 9, 5, 6, 0]
SLOT = {index: ORDER.index(index) for index in range(19)}
TWIN = 16
ZPLUS = [5, 11, 14, 15, 18]
ZMINUS = [6, 12, 13, 16, 17]
ROW = 8

NX, NY, NZ = 4, 16, 128
HALVES = NY // 8
ROUNDS = 4


def neighbours():
    found = []
    for dx, dy, dz in VELOCITY[1:]:
        found.append((dx, dy, dz))
    return found


NEIGHBOURS = neighbours()


def kernel(
    sizes,
    pop_hbm,
    design_hbm,
    labels_hbm,
    adj_hbm,
    sens_ref,
    obj_ref,
    pop,
    design,
    labels,
    adj,
    pads,
    zsend,
    zrecv,
    zedge,
    saved,
    raw,
    red_x,
    red_y,
    red_z,
    load_sem,
    store_sem,
    send_sem,
    recv_sem,
    red_send,
    red_recv,
):
    nx, ny, nz = sizes
    gx, gy, gz = lax.axis_index("gx"), lax.axis_index("gy"), lax.axis_index("gz")

    def device(dx, dy, dz):
        return {
            "gx": lax.rem(gx + (dx + nx), nx) if dx else gx,
            "gy": lax.rem(gy + (dy + ny), ny) if dy else gy,
            "gz": lax.rem(gz + (dz + nz), nz) if dz else gz,
        }

    loads = [
        pltpu.make_async_copy(design_hbm, design, load_sem.at[4]),
        pltpu.make_async_copy(labels_hbm, labels, load_sem.at[5]),
    ]
    slabs = {}
    for x in (0, 3, 1, 2):
        slabs[x] = pltpu.make_async_copy(pop_hbm.at[:, x], pop.at[x], load_sem.at[x])
    for copy in loads:
        copy.start()
    for x in (0, 3, 1, 2):
        slabs[x].start()

    barrier = pltpu.get_barrier_semaphore()
    partners = [n for n in NEIGHBOURS if sum(map(abs, n)) == 2]
    partners += [(k, 0, 0) for k in range(1, nx)]
    partners += [(0, k, 0) for k in range(1, ny)]
    partners += [(0, 0, k) for k in range(1, nz)]
    for partner in partners:
        pl.semaphore_signal(barrier, inc=1, device_id=device(*partner), device_id_type=MESH)

    lane = lax.broadcasted_iota(jnp.int32, (8, NZ), 1)
    first, last = lane == 0, lane == NZ - 1

    def exchange(turn):
        pad, zs, zr, ze = pads.at[turn], zsend.at[turn], zrecv.at[turn], zedge.at[turn]
        copies = {}
        for number, (dx, dy, dz) in enumerate(NEIGHBOURS):
            if dz == 0:
                if dx > 0:
                    xs, xd, group = 4, 0, slice(0, 5)
                elif dx < 0:
                    xs, xd, group = 1, 5, slice(8, 13)
                else:
                    xs, xd, group = slice(1, 5), slice(1, 5), slice(4, 9) if dy > 0 else slice(12, 17)
                if dy > 0:
                    ys, yd = slice(23, 24), slice(7, 8)
                elif dy < 0:
                    ys, yd = slice(8, 9), slice(24, 25)
                else:
                    ys, yd = slice(8, 24), slice(8, 24)
                if dx and dy:
                    group = SLOT[VELOCITY.index((dx, dy, dz))]
                src, dst = pad.at[xs, group, ys], pad.at[xd, group, yd]
            else:
                s = 0 if dz > 0 else 1
                if dx:
                    src, dst = zs.at[s], ze.at[s, 0 if dx > 0 else 1]
                elif dy > 0:
                    src, dst = zs.at[s, 15:16], zr.at[s, 7:8]
                elif dy < 0:
                    src, dst = zs.at[s, 0:1], zr.at[s, 24:25]
                else:
                    src, dst = zs.at[s], zr.at[s, 8:24]
            copies[(dx, dy, dz)] = pltpu.make_async_remote_copy(
                src_ref=src,
                dst_ref=dst,
                send_sem=send_sem.at[turn, number],
                recv_sem=recv_sem.at[turn, number],
                device_id=device(dx, dy, dz),
                device_id_type=MESH,
            )
        return copies

    exchanges = [exchange(turn) for turn in range(ROUNDS)]

    def send_x(turn):
        for (dx, dy, dz), copy in exchanges[turn].items():
            if dx and not dz:
                copy.start()

    def send_rest(turn):
        for (dx, dy, dz), copy in exchanges[turn].items():
            if not (dx and not dz):
                copy.start()

    def receive(turn):
        pad, zr, ze = pads.at[turn], zrecv.at[turn], zedge.at[turn]
        for copy in exchanges[turn].values():
            copy.wait_recv()

        @pl.when(gx == 0)
        def _():
            pad[0, 0:5, 7:25, :] = jnp.zeros((5, 18, NZ), F32)
            ze[:, 0] = jnp.zeros((2, NY, NZ), F32)

        @pl.when(gx == nx - 1)
        def _():
            pad[5, 8:13, 7:25, :] = jnp.zeros((5, 18, NZ), F32)
            ze[:, 1] = jnp.zeros((2, NY, NZ), F32)

        @pl.when(gy == 0)
        def _():
            pad[:, 4:9, 7:8, :] = jnp.zeros((6, 5, 1, NZ), F32)
            zr[:, 7:8, :] = jnp.zeros((2, 1, NZ), F32)

        @pl.when(gy == ny - 1)
        def _():
            pad[:, 12:17, 24:25, :] = jnp.zeros((6, 5, 1, NZ), F32)
            pad[0, 0:1, 24:25, :] = jnp.zeros((1, 1, NZ), F32)
            zr[:, 24:25, :] = jnp.zeros((2, 1, NZ), F32)

        @pl.when(gz == 0)
        def _():
            zr[0, 7:25, :] = jnp.zeros((18, NZ), F32)
            ze[0] = jnp.zeros((2, NY, NZ), F32)

        @pl.when(gz == nz - 1)
        def _():
            zr[1, 7:25, :] = jnp.zeros((18, NZ), F32)
            ze[1] = jnp.zeros((2, NY, NZ), F32)

        place = lane % 8
        for s in range(2):
            for h in range(HALVES):
                rows = slice(8 * h, 8 * h + 8)
                own = slice(8 * h + ROW, 8 * h + ROW + 8)
                below = pltpu.roll(ze[s, 0, rows, :], NZ - 4, 1)
                above = pltpu.roll(ze[s, 1, rows, :], 4, 1)
                zr[s, own, :] = jnp.where(
                    place == 0, below, jnp.where(place == 5, above, zr[s, own, :])
                )

    def gather(turn, x, h):
        values = []
        for index in range(19):
            cx, cy, cz = VELOCITY[index]
            slot = SLOT[index]
            if index == 9 and x > 0:
                slot = TWIN
            start = ROW + 8 * h - cy
            value = pads[turn, x + 1 - cx, slot, start : start + 8, :]
            if cz:
                s = 0 if cz > 0 else 1
                k = (ZPLUS if cz > 0 else ZMINUS).index(index)
                column = 8 * k + 1 + x - cx
                halo = zrecv[turn, s, start : start + 8, :]
                shift = (-column) % NZ if cz > 0 else NZ - 1 - column
                halo = pltpu.roll(halo, shift, 1) if shift else halo
                value = jnp.where(first if cz > 0 else last, halo, value)
            values.append(value)
        return values

    def scatter(turn, x, h, values, packed):
        rows = slice(ROW + 8 * h, ROW + 8 * h + 8)
        for index in range(19):
            cz = VELOCITY[index][2]
            value = values[index]
            if cz:
                s = 0 if cz > 0 else 1
                k = (ZPLUS if cz > 0 else ZMINUS).index(index)
                column = 8 * k + 1 + x
                shift = (column + 1) % NZ if cz > 0 else column
                packed[s][h] = jnp.where(lane == column, pltpu.roll(value, shift, 1), packed[s][h])
                value = pltpu.roll(value, 1 if cz > 0 else NZ - 1, 1)
            pads[turn, x + 1, SLOT[index], rows, :] = value
            if index == 9:
                pads[turn, x + 1, TWIN, rows, :] = value

    def stage(turn, block):
        zero = jnp.zeros((8, NZ), F32)
        packed = [[zero] * HALVES, [zero] * HALVES]
        for x in (0, 3):
            for h in range(HALVES):
                scatter(turn, x, h, block(x, h), packed)
        if turn == 0:
            pl.semaphore_wait(barrier, len(partners))
        send_x(turn)
        for x in (1, 2):
            for h in range(HALVES):
                scatter(turn, x, h, block(x, h), packed)
        for s in range(2):
            for h in range(HALVES):
                zsend[turn, s, 8 * h : 8 * h + 8, :] = packed[s][h]
        send_rest(turn)

    def moments(f):
        sums = {i: f[i] + f[i + 1] for i in PAIRS}
        diff = {i: f[i] - f[i + 1] for i in PAIRS}
        density = f[0] + (
            ((sums[1] + sums[3]) + (sums[5] + sums[7]))
            + ((sums[9] + sums[11]) + (sums[13] + (sums[15] + sums[17])))
        )
        jx = diff[1] + ((diff[7] + diff[9]) + (diff[11] + diff[13]))
        jy = diff[3] + ((diff[7] - diff[9]) + (diff[15] + diff[17]))
        jz = diff[5] + ((diff[11] - diff[13]) + (diff[15] - diff[17]))
        return density, jx, jy, jz

    def along(index, v):
        total = None
        for axis in range(3):
            c = VELOCITY[index][axis]
            if c:
                if total is None:
                    total = v[axis]
                else:
                    total = total + v[axis] if c > 0 else total - v[axis]
        return total

    def collide(which, f, x, h):
        rows = slice(8 * h, 8 * h + 8)
        mark = labels[x, rows, :]
        fluid, solid, inlet, outlet = mark == 1, mark == 2, mark == 3, mark == 4
        damping = 1.0 / (1.0 + design[x, rows, :])
        density, jx, jy, jz = moments(f)
        inverse = 1.0 / jnp.where(solid, 1.0, density)
        factor = inverse * jnp.where(fluid, damping, jnp.where(outlet, 1.0, 0.0))
        ux, uy, uz = jx * factor, jy * factor, jnp.where(inlet, INFLOW, jz * factor)
        saved[which, 0, x, rows, :] = ux
        saved[which, 1, x, rows, :] = uy
        saved[which, 2, x, rows, :] = uz
        saved[which, 3, x, rows, :] = jnp.where(
            fluid, RELAX * damping, jnp.where(outlet, inverse, 0.0)
        )
        saved[which, 4, x, rows, :] = jnp.where(fluid, -RELAX * damping * density, 0.0)
        weight = jnp.where(fluid, RELAX * density, 1.0)
        keep = jnp.where(fluid, 1.0 - RELAX, 0.0)
        rest = 1.0 - 1.5 * (ux * ux + uy * uy + uz * uz)
        wide, thin = weight * (1.0 / 18.0), weight * (1.0 / 36.0)
        post = [None] * 19
        post[0] = jnp.where(solid, f[0], keep * f[0] + (weight * (1.0 / 3.0)) * rest)
        for i in PAIRS:
            w = wide if i < 7 else thin
            cu = along(i, (ux, uy, uz))
            even = w * (rest + 4.5 * (cu * cu))
            odd = w * (3.0 * cu)
            post[i] = jnp.where(solid, f[i + 1], keep * f[i] + (even + odd))
            post[i + 1] = jnp.where(solid, f[i], keep * f[i + 1] + (even - odd))
        return post

    def transpose(which, g, x, h):
        rows = slice(8 * h, 8 * h + 8)
        mark = labels[x, rows, :]
        fluid, solid = mark == 1, mark == 2
        u = [saved[which, a, x, rows, :] for a in range(3)]
        gain, slope = saved[which, 3, x, rows, :], saved[which, 4, x, rows, :]
        ux, uy, uz = u
        s = {i: g[i] + g[i + 1] for i in PAIRS}
        d = {i: g[i] - g[i + 1] for i in PAIRS}
        wide, thin = 1.0 / 18.0, 1.0 / 36.0
        sxy, sxz, syz = s[7] + s[9], s[11] + s[13], s[15] + s[17]
        m0 = (
            (1.0 / 3.0) * g[0]
            + wide * (s[1] + s[3] + s[5])
            + thin * (sxy + sxz + syz)
        )
        m1x = wide * d[1] + thin * ((d[7] + d[9]) + (d[11] + d[13]))
        m1y = wide * d[3] + thin * ((d[7] - d[9]) + (d[15] + d[17]))
        m1z = wide * d[5] + thin * ((d[11] - d[13]) + (d[15] - d[17]))
        mxx = wide * s[1] + thin * (sxy + sxz)
        myy = wide * s[3] + thin * (sxy + syz)
        mzz = wide * s[5] + thin * (sxz + syz)
        mxy = thin * (s[7] - s[9])
        mxz = thin * (s[11] - s[13])
        myz = thin * (s[15] - s[17])
        hx = mxx * ux + mxy * uy + mxz * uz
        hy = mxy * ux + myy * uy + myz * uz
        hz = mxz * ux + myz * uy + mzz * uz
        quad = ux * hx + uy * hy + uz * hz
        square = ux * ux + uy * uy + uz * uz
        bx = 3.0 * (m1x - ux * m0) + 9.0 * hx
        by = 3.0 * (m1y - uy * m0) + 9.0 * hy
        bz = 3.0 * (m1z - uz * m0) + 9.0 * hz
        bu = bx * ux + by * uy + bz * uz
        base = jnp.where(
            fluid, RELAX * (m0 + 1.5 * square * m0 - 4.5 * quad), -(bu * gain)
        )
        e = (bx * gain, by * gain, bz * gain)
        keep = jnp.where(fluid, 1.0 - RELAX, 0.0)
        back = [None] * 19
        back[0] = jnp.where(solid, g[0], keep * g[0] + base)
        for i in PAIRS:
            ce = along(i, e)
            back[i] = jnp.where(solid, g[i + 1], keep * g[i] + (base + ce))
            back[i + 1] = jnp.where(solid, g[i], keep * g[i + 1] + (base - ce))
        return back, slope * bu

    def reverse(values):
        return [values[OPPOSITE[i]] for i in range(19)]

    for copy in loads:
        copy.wait()
    waited = set()

    def block_one(x, h):
        if x not in waited:
            slabs[x].wait()
            waited.add(x)
        f = [pop[x, i, 8 * h : 8 * h + 8, :] for i in range(19)]
        return collide(0, f, x, h)

    stage(0, block_one)

    receive(0)
    stage(1, lambda x, h: collide(1, gather(0, x, h), x, h))

    receive(1)
    lost = []

    def block_final(x, h):
        rows = slice(8 * h, 8 * h + 8)
        solidity = design[x, rows, :]
        fluid = labels[x, rows, :] == 1
        density, jx, jy, jz = moments(gather(1, x, h))
        inverse = jnp.where(fluid, 1.0 / jnp.where(fluid, density, 1.0), 0.0)
        v = (jx * inverse, jy * inverse, jz * inverse)
        square = v[0] * v[0] + v[1] * v[1] + v[2] * v[2]
        direct = 10.0 * density * square
        raw[x, rows, :] = direct
        lost.append(solidity * direct)
        base = -10.0 * solidity * square
        twice = 20.0 * solidity
        e = (twice * v[0], twice * v[1], twice * v[2])
        g = [base] * 19
        for i in PAIRS:
            ce = along(i, e)
            g[i], g[i + 1] = base + ce, base - ce
        return reverse(g)

    stage(2, block_final)

    receive(2)

    def block_two(x, h):
        rows = slice(8 * h, 8 * h + 8)
        back, sens = transpose(1, reverse(gather(2, x, h)), x, h)
        raw[x, rows, :] = raw[x, rows, :] + sens
        return reverse(back)

    stage(3, block_two)

    receive(3)
    sizes_of = jnp.zeros((8, NZ), F32)
    stores = []
    for x in range(NX):
        for h in range(HALVES):
            rows = slice(8 * h, 8 * h + 8)
            back, sens = transpose(0, reverse(gather(3, x, h)), x, h)
            total = raw[x, rows, :] + sens
            raw[x, rows, :] = total
            sizes_of = sizes_of + jnp.abs(total)
            for i in range(19):
                adj[x, i, rows, :] = back[i]
        stores.append(pltpu.make_async_copy(adj.at[x], adj_hbm.at[:, x], store_sem.at[x]))
        stores[-1].start()

    lost_of = lost[0]
    for term in lost[1:]:
        lost_of = lost_of + term
    row = lax.broadcasted_iota(jnp.int32, (8, NZ), 0)
    mine = jnp.where(
        row == 0,
        jnp.sum(lost_of, axis=0, keepdims=True),
        jnp.where(row == 1, jnp.sum(sizes_of, axis=0, keepdims=True), 0.0),
    )

    number = 0
    sent = []
    for buffer, me, count, step in (
        (red_z, gz, nz, (0, 0, 1)),
        (red_y, gy, ny, (0, 1, 0)),
        (red_x, gx, nx, (1, 0, 0)),
    ):
        buffer[me] = mine
        copies = []
        for k in range(1, count):
            copies.append(
                pltpu.make_async_remote_copy(
                    src_ref=buffer.at[me],
                    dst_ref=buffer.at[me],
                    send_sem=red_send.at[number],
                    recv_sem=red_recv.at[number],
                    device_id=device(*(k * c for c in step)),
                    device_id_type=MESH,
                )
            )
            number += 1
        for copy in copies:
            copy.start()
        for copy in copies:
            copy.wait_recv()
        sent += copies
        mine = buffer[0]
        for k in range(1, count):
            mine = mine + buffer[k]

    cells = NX * NY * NZ * nx * ny * nz
    loss = jnp.sum(jnp.where(row == 0, mine, 0.0))
    size = jnp.sum(jnp.where(row == 1, mine, 0.0))
    obj_ref[0] = 20.0 * loss / cells
    scale = size / cells + 1e-06
    inverse = 1.0 / jnp.full((8, NZ), scale, F32)
    for x in range(NX):
        for h in range(HALVES):
            rows = slice(8 * h, 8 * h + 8)
            sens_ref[x, rows, :] = raw[x, rows, :] * inverse

    for copy in stores:
        copy.wait()
    for copies in exchanges:
        for copy in copies.values():
            copy.wait_send()
    for copy in sent:
        copy.wait_send()


def solution(mesh):
    nx, ny, nz = (mesh.shape[a] for a in ("gx", "gy", "gz"))
    partners = nx + ny + nz - 3

    def body(populations, design, labels):
        cells = (NX, NY, NZ)
        adjoint, sensitivity, objective = pl.pallas_call(
            lambda *refs: kernel((nx, ny, nz), *refs),
            out_shape=(
                jax.ShapeDtypeStruct((19,) + cells, F32),
                jax.ShapeDtypeStruct(cells, F32),
                jax.ShapeDtypeStruct((1,), F32),
            ),
            in_specs=[pl.BlockSpec(memory_space=pl.ANY)] * 3,
            out_specs=(
                pl.BlockSpec(memory_space=pl.ANY),
                pl.BlockSpec(memory_space=pltpu.VMEM),
                pl.BlockSpec(memory_space=pltpu.SMEM),
            ),
            scratch_shapes=[
                pltpu.VMEM((NX, 19, NY, NZ), F32),
                pltpu.VMEM(cells, F32),
                pltpu.VMEM(cells, jnp.int32),
                pltpu.VMEM((NX, 19, NY, NZ), F32),
                pltpu.VMEM((ROUNDS, NX + 2, 20, NY + 16, NZ), F32),
                pltpu.VMEM((ROUNDS, 2, NY, NZ), F32),
                pltpu.VMEM((ROUNDS, 2, NY + 16, NZ), F32),
                pltpu.VMEM((ROUNDS, 2, 2, NY, NZ), F32),
                pltpu.VMEM((2, 5) + cells, F32),
                pltpu.VMEM(cells, F32),
                pltpu.VMEM((nx, 8, NZ), F32),
                pltpu.VMEM((ny, 8, NZ), F32),
                pltpu.VMEM((nz, 8, NZ), F32),
                pltpu.SemaphoreType.DMA((6,)),
                pltpu.SemaphoreType.DMA((NX,)),
                pltpu.SemaphoreType.DMA((ROUNDS, 18)),
                pltpu.SemaphoreType.DMA((ROUNDS, 18)),
                pltpu.SemaphoreType.DMA((partners,)),
                pltpu.SemaphoreType.DMA((partners,)),
            ],
            compiler_params=pltpu.CompilerParams(
                collective_id=0, has_side_effects=True, vmem_limit_bytes=40 * 1024 * 1024
            ),
            cost_estimate=pl.CostEstimate(
                flops=10_000_000, bytes_accessed=1_500_000, transcendentals=0
            ),
        )(populations, design, labels)
        return adjoint, sensitivity, objective.reshape(())

    in_specs = (P(None, "gx", "gy", "gz"), P("gx", "gy", "gz"), P("gx", "gy", "gz"))
    out_specs = (P(None, "gx", "gy", "gz"), P("gx", "gy", "gz"), P())
    return jax.shard_map(body, mesh=mesh, in_specs=in_specs, out_specs=out_specs, check_vma=False)
```

```python
import jax
import jax.numpy as jnp
from jax import lax
from jax.experimental import pallas as pl
from jax.experimental.pallas import tpu as pltpu
from jax.sharding import PartitionSpec as P

VELOCITY = [
    (0, 0, 0),
    (1, 0, 0),
    (-1, 0, 0),
    (0, 1, 0),
    (0, -1, 0),
    (0, 0, 1),
    (0, 0, -1),
    (1, 1, 0),
    (-1, -1, 0),
    (1, -1, 0),
    (-1, 1, 0),
    (1, 0, 1),
    (-1, 0, -1),
    (1, 0, -1),
    (-1, 0, 1),
    (0, 1, 1),
    (0, -1, -1),
    (0, 1, -1),
    (0, -1, 1),
]
OPPOSITE = [0, 2, 1, 4, 3, 6, 5, 8, 7, 10, 9, 12, 11, 14, 13, 16, 15, 18, 17]
PAIRS = [1, 3, 5, 7, 9, 11, 13, 15, 17]
RELAX = 1.6
INFLOW = 0.05
MESH = pl.DeviceIdType.MESH
F32 = jnp.float32

ORDER = [9, 1, 11, 13, 7, 3, 15, 17, 10, 2, 12, 14, 8, 4, 16, 18, 9, 5, 6, 0]
SLOT = {index: ORDER.index(index) for index in range(19)}
TWIN = 16
ZPLUS = [5, 11, 14, 15, 18]
ZMINUS = [6, 12, 13, 16, 17]
ROW = 8

NX, NY, NZ = 4, 16, 128
HALVES = NY // 8
ROUNDS = 4
PIECES = 4


def neighbours():
    found = []
    for dx, dy, dz in VELOCITY[1:]:
        found.append((dx, dy, dz))
    return found


NEIGHBOURS = neighbours()


def kernel(
    sizes,
    pop_hbm,
    design_hbm,
    labels_hbm,
    adj_hbm,
    raw_hbm,
    sums_ref,
    pop,
    design,
    labels,
    adj,
    pads,
    zsend,
    zrecv,
    zedge,
    saved,
    raw,
    red_p,
    red_y,
    load_sem,
    store_sem,
    send_sem,
    recv_sem,
    red_send,
    red_recv,
):
    nx, ny, nz = sizes
    gx, gy, gz = lax.axis_index("gx"), lax.axis_index("gy"), lax.axis_index("gz")

    def device(dx, dy, dz):
        return {
            "gx": lax.rem(gx + (dx + nx), nx) if dx else gx,
            "gy": lax.rem(gy + (dy + ny), ny) if dy else gy,
            "gz": lax.rem(gz + (dz + nz), nz) if dz else gz,
        }

    inside = {
        "gx": (gx > 0, gx < nx - 1),
        "gy": (gy > 0, gy < ny - 1),
        "gz": (gz > 0, gz < nz - 1),
    }

    def exists(dx, dy, dz):
        found = None
        for axis, d in (("gx", dx), ("gy", dy), ("gz", dz)):
            if d:
                here = inside[axis][1 if d > 0 else 0]
                found = here if found is None else found & here
        return found

    loads = [
        pltpu.make_async_copy(design_hbm, design, load_sem.at[4]),
        pltpu.make_async_copy(labels_hbm, labels, load_sem.at[5]),
    ]
    slabs = {}
    for x in (0, 3, 1, 2):
        slabs[x] = pltpu.make_async_copy(pop_hbm.at[:, x], pop.at[x], load_sem.at[x])
    for copy in loads:
        copy.start()
    for x in (0, 3, 1, 2):
        slabs[x].start()

    @pl.when(gx == 0)
    def _():
        pads[:, 0, 0:5, 7:25, :] = jnp.zeros((ROUNDS, 5, 18, NZ), F32)
        zedge[:, :, 0] = jnp.zeros((ROUNDS, 2, NY, NZ), F32)

    @pl.when(gx == nx - 1)
    def _():
        pads[:, 5, 8:13, 7:25, :] = jnp.zeros((ROUNDS, 5, 18, NZ), F32)
        zedge[:, :, 1] = jnp.zeros((ROUNDS, 2, NY, NZ), F32)

    @pl.when(gy == 0)
    def _():
        pads[:, :, 4:9, 7:8, :] = jnp.zeros((ROUNDS, NX + 2, 5, 1, NZ), F32)
        zrecv[:, :, 7:8, :] = jnp.zeros((ROUNDS, 2, 1, NZ), F32)

    @pl.when(gy == ny - 1)
    def _():
        pads[:, :, 12:17, 24:25, :] = jnp.zeros((ROUNDS, NX + 2, 5, 1, NZ), F32)
        pads[:, 0, 0:1, 24:25, :] = jnp.zeros((ROUNDS, 1, 1, NZ), F32)
        zrecv[:, :, 24:25, :] = jnp.zeros((ROUNDS, 2, 1, NZ), F32)

    @pl.when(gz == 0)
    def _():
        zrecv[:, 0, 7:25, :] = jnp.zeros((ROUNDS, 18, NZ), F32)
        zedge[:, 0] = jnp.zeros((ROUNDS, 2, NY, NZ), F32)

    @pl.when(gz == nz - 1)
    def _():
        zrecv[:, 1, 7:25, :] = jnp.zeros((ROUNDS, 18, NZ), F32)
        zedge[:, 1] = jnp.zeros((ROUNDS, 2, NY, NZ), F32)

    barrier = pltpu.get_barrier_semaphore()
    plane = [(a, 0, b) for a in range(nx) for b in range(nz) if a or b]
    column = [(0, k, 0) for k in range(1, ny)]
    partners = [n for n in NEIGHBOURS if n[1] and (n[0] or n[2])] + plane + column
    for partner in partners:
        pl.semaphore_signal(barrier, inc=1, device_id=device(*partner), device_id_type=MESH)

    lane = lax.broadcasted_iota(jnp.int32, (8, NZ), 1)
    first, last = lane == 0, lane == NZ - 1

    def exchange(turn):
        pad, zs, zr, ze = pads.at[turn], zsend.at[turn], zrecv.at[turn], zedge.at[turn]
        copies = {}
        for number, (dx, dy, dz) in enumerate(NEIGHBOURS):
            if dz == 0:
                if dx > 0:
                    xs, xd, group = 4, 0, slice(0, 5)
                elif dx < 0:
                    xs, xd, group = 1, 5, slice(8, 13)
                else:
                    xs, xd, group = slice(1, 5), slice(1, 5), slice(4, 9) if dy > 0 else slice(12, 17)
                if dy > 0:
                    ys, yd = slice(23, 24), slice(7, 8)
                elif dy < 0:
                    ys, yd = slice(8, 9), slice(24, 25)
                else:
                    ys, yd = slice(8, 24), slice(8, 24)
                if dx and dy:
                    group = SLOT[VELOCITY.index((dx, dy, dz))]
                src, dst = pad.at[xs, group, ys], pad.at[xd, group, yd]
            else:
                s = 0 if dz > 0 else 1
                if dx:
                    src, dst = zs.at[s], ze.at[s, 0 if dx > 0 else 1]
                elif dy > 0:
                    src, dst = zs.at[s, 15:16], zr.at[s, 7:8]
                elif dy < 0:
                    src, dst = zs.at[s, 0:1], zr.at[s, 24:25]
                else:
                    src, dst = zs.at[s], zr.at[s, 8:24]
            copies[(dx, dy, dz)] = pltpu.make_async_remote_copy(
                src_ref=src,
                dst_ref=dst,
                send_sem=send_sem.at[turn, number],
                recv_sem=recv_sem.at[turn, number],
                device_id=device(dx, dy, dz),
                device_id_type=MESH,
            )
        return copies

    exchanges = [exchange(turn) for turn in range(ROUNDS)]

    def send_x(turn):
        for (dx, dy, dz), copy in exchanges[turn].items():
            if dx and not dz:
                pl.when(exists(dx, dy, dz))(copy.start)

    def send_rest(turn):
        rest = [item for item in exchanges[turn].items() if item[0][2] or not item[0][0]]
        for (dx, dy, dz), copy in sorted(rest, key=lambda item: not item[0][1]):
            pl.when(exists(dx, dy, dz))(copy.start)

    def receive(turn):
        pad, zr, ze = pads.at[turn], zrecv.at[turn], zedge.at[turn]
        for (dx, dy, dz), copy in exchanges[turn].items():
            pl.when(exists(-dx, -dy, -dz))(copy.wait_recv)

        place = lane % 8
        for s in range(2):
            for h in range(HALVES):
                rows = slice(8 * h, 8 * h + 8)
                own = slice(8 * h + ROW, 8 * h + ROW + 8)
                below = pltpu.roll(ze[s, 0, rows, :], NZ - 4, 1)
                above = pltpu.roll(ze[s, 1, rows, :], 4, 1)
                zr[s, own, :] = jnp.where(
                    place == 0, below, jnp.where(place == 5, above, zr[s, own, :])
                )

    def gather(turn, x, h):
        values = []
        for index in range(19):
            cx, cy, cz = VELOCITY[index]
            slot = SLOT[index]
            if index == 9 and x > 0:
                slot = TWIN
            start = ROW + 8 * h - cy
            value = pads[turn, x + 1 - cx, slot, start : start + 8, :]
            if cz:
                s = 0 if cz > 0 else 1
                k = (ZPLUS if cz > 0 else ZMINUS).index(index)
                column = 8 * k + 1 + x - cx
                halo = zrecv[turn, s, start : start + 8, :]
                shift = (-column) % NZ if cz > 0 else NZ - 1 - column
                halo = pltpu.roll(halo, shift, 1) if shift else halo
                value = jnp.where(first if cz > 0 else last, halo, value)
            values.append(value)
        return values

    def scatter(turn, x, h, values, packed):
        rows = slice(ROW + 8 * h, ROW + 8 * h + 8)
        for index in range(19):
            cz = VELOCITY[index][2]
            value = values[index]
            if cz:
                s = 0 if cz > 0 else 1
                k = (ZPLUS if cz > 0 else ZMINUS).index(index)
                column = 8 * k + 1 + x
                shift = (column + 1) % NZ if cz > 0 else column
                packed[s][h] = jnp.where(lane == column, pltpu.roll(value, shift, 1), packed[s][h])
                value = pltpu.roll(value, 1 if cz > 0 else NZ - 1, 1)
            pads[turn, x + 1, SLOT[index], rows, :] = value
            if index == 9:
                pads[turn, x + 1, TWIN, rows, :] = value

    def stage(turn, block):
        zero = jnp.zeros((8, NZ), F32)
        packed = [[zero] * HALVES, [zero] * HALVES]
        for x in (0, 3):
            for h in range(HALVES):
                scatter(turn, x, h, block(x, h), packed)
        if turn == 0:
            pl.semaphore_wait(barrier, len(partners))
        send_x(turn)
        for x in (1, 2):
            for h in range(HALVES):
                scatter(turn, x, h, block(x, h), packed)
        for s in range(2):
            for h in range(HALVES):
                zsend[turn, s, 8 * h : 8 * h + 8, :] = packed[s][h]
        send_rest(turn)

    def moments(f):
        sums = {i: f[i] + f[i + 1] for i in PAIRS}
        diff = {i: f[i] - f[i + 1] for i in PAIRS}
        density = f[0] + (
            ((sums[1] + sums[3]) + (sums[5] + sums[7]))
            + ((sums[9] + sums[11]) + (sums[13] + (sums[15] + sums[17])))
        )
        jx = diff[1] + ((diff[7] + diff[9]) + (diff[11] + diff[13]))
        jy = diff[3] + ((diff[7] - diff[9]) + (diff[15] + diff[17]))
        jz = diff[5] + ((diff[11] - diff[13]) + (diff[15] - diff[17]))
        return density, jx, jy, jz

    def along(index, v):
        total = None
        for axis in range(3):
            c = VELOCITY[index][axis]
            if c:
                if total is None:
                    total = v[axis]
                else:
                    total = total + v[axis] if c > 0 else total - v[axis]
        return total

    def collide(which, f, x, h):
        rows = slice(8 * h, 8 * h + 8)
        mark = labels[x, rows, :]
        fluid, solid, inlet, outlet = mark == 1, mark == 2, mark == 3, mark == 4
        damping = 1.0 / (1.0 + design[x, rows, :])
        density, jx, jy, jz = moments(f)
        inverse = 1.0 / jnp.where(solid, 1.0, density)
        factor = inverse * jnp.where(fluid, damping, jnp.where(outlet, 1.0, 0.0))
        ux, uy, uz = jx * factor, jy * factor, jnp.where(inlet, INFLOW, jz * factor)
        saved[which, 0, x, rows, :] = ux
        saved[which, 1, x, rows, :] = uy
        saved[which, 2, x, rows, :] = uz
        saved[which, 3, x, rows, :] = jnp.where(
            fluid, RELAX * damping, jnp.where(outlet, inverse, 0.0)
        )
        saved[which, 4, x, rows, :] = jnp.where(fluid, -RELAX * damping * density, 0.0)
        weight = jnp.where(fluid, RELAX * density, 1.0)
        keep = jnp.where(fluid, 1.0 - RELAX, 0.0)
        rest = 1.0 - 1.5 * (ux * ux + uy * uy + uz * uz)
        wide, thin = weight * (1.0 / 18.0), weight * (1.0 / 36.0)
        post = [None] * 19
        post[0] = jnp.where(solid, f[0], keep * f[0] + (weight * (1.0 / 3.0)) * rest)
        for i in PAIRS:
            w = wide if i < 7 else thin
            cu = along(i, (ux, uy, uz))
            even = w * (rest + 4.5 * (cu * cu))
            odd = w * (3.0 * cu)
            post[i] = jnp.where(solid, f[i + 1], keep * f[i] + (even + odd))
            post[i + 1] = jnp.where(solid, f[i], keep * f[i + 1] + (even - odd))
        return post

    def transpose(which, g, x, h):
        rows = slice(8 * h, 8 * h + 8)
        mark = labels[x, rows, :]
        fluid, solid = mark == 1, mark == 2
        u = [saved[which, a, x, rows, :] for a in range(3)]
        gain, slope = saved[which, 3, x, rows, :], saved[which, 4, x, rows, :]
        ux, uy, uz = u
        s = {i: g[i] + g[i + 1] for i in PAIRS}
        d = {i: g[i] - g[i + 1] for i in PAIRS}
        wide, thin = 1.0 / 18.0, 1.0 / 36.0
        sxy, sxz, syz = s[7] + s[9], s[11] + s[13], s[15] + s[17]
        m0 = (
            (1.0 / 3.0) * g[0]
            + wide * (s[1] + s[3] + s[5])
            + thin * (sxy + sxz + syz)
        )
        m1x = wide * d[1] + thin * ((d[7] + d[9]) + (d[11] + d[13]))
        m1y = wide * d[3] + thin * ((d[7] - d[9]) + (d[15] + d[17]))
        m1z = wide * d[5] + thin * ((d[11] - d[13]) + (d[15] - d[17]))
        mxx = wide * s[1] + thin * (sxy + sxz)
        myy = wide * s[3] + thin * (sxy + syz)
        mzz = wide * s[5] + thin * (sxz + syz)
        mxy = thin * (s[7] - s[9])
        mxz = thin * (s[11] - s[13])
        myz = thin * (s[15] - s[17])
        hx = mxx * ux + mxy * uy + mxz * uz
        hy = mxy * ux + myy * uy + myz * uz
        hz = mxz * ux + myz * uy + mzz * uz
        quad = ux * hx + uy * hy + uz * hz
        square = ux * ux + uy * uy + uz * uz
        bx = 3.0 * (m1x - ux * m0) + 9.0 * hx
        by = 3.0 * (m1y - uy * m0) + 9.0 * hy
        bz = 3.0 * (m1z - uz * m0) + 9.0 * hz
        bu = bx * ux + by * uy + bz * uz
        base = jnp.where(
            fluid, RELAX * (m0 + 1.5 * square * m0 - 4.5 * quad), -(bu * gain)
        )
        e = (bx * gain, by * gain, bz * gain)
        keep = jnp.where(fluid, 1.0 - RELAX, 0.0)
        back = [None] * 19
        back[0] = jnp.where(solid, g[0], keep * g[0] + base)
        for i in PAIRS:
            ce = along(i, e)
            back[i] = jnp.where(solid, g[i + 1], keep * g[i] + (base + ce))
            back[i + 1] = jnp.where(solid, g[i], keep * g[i + 1] + (base - ce))
        return back, slope * bu

    def reverse(values):
        return [values[OPPOSITE[i]] for i in range(19)]

    for copy in loads:
        copy.wait()
    waited = set()

    def block_one(x, h):
        if x not in waited:
            slabs[x].wait()
            waited.add(x)
        f = [pop[x, i, 8 * h : 8 * h + 8, :] for i in range(19)]
        return collide(0, f, x, h)

    stage(0, block_one)

    receive(0)
    stage(1, lambda x, h: collide(1, gather(0, x, h), x, h))

    receive(1)
    lost = []

    def block_final(x, h):
        rows = slice(8 * h, 8 * h + 8)
        solidity = design[x, rows, :]
        fluid = labels[x, rows, :] == 1
        density, jx, jy, jz = moments(gather(1, x, h))
        inverse = jnp.where(fluid, 1.0 / jnp.where(fluid, density, 1.0), 0.0)
        v = (jx * inverse, jy * inverse, jz * inverse)
        square = v[0] * v[0] + v[1] * v[1] + v[2] * v[2]
        direct = 10.0 * density * square
        raw[x, rows, :] = direct
        lost.append(solidity * direct)
        base = -10.0 * solidity * square
        twice = 20.0 * solidity
        e = (twice * v[0], twice * v[1], twice * v[2])
        g = [base] * 19
        for i in PAIRS:
            ce = along(i, e)
            g[i], g[i + 1] = base + ce, base - ce
        return reverse(g)

    stage(2, block_final)

    receive(2)

    def block_two(x, h):
        rows = slice(8 * h, 8 * h + 8)
        back, sens = transpose(1, reverse(gather(2, x, h)), x, h)
        raw[x, rows, :] = raw[x, rows, :] + sens
        return reverse(back)

    stage(3, block_two)

    receive(3)
    sizes_of = jnp.zeros((8, NZ), F32)
    for x in range(NX):
        for h in range(HALVES):
            rows = slice(8 * h, 8 * h + 8)
            _, sens = transpose(0, reverse(gather(3, x, h)), x, h)
            total = raw[x, rows, :] + sens
            raw[x, rows, :] = total
            sizes_of = sizes_of + jnp.abs(total)

    lost_of = lost[0]
    for term in lost[1:]:
        lost_of = lost_of + term
    row = lax.broadcasted_iota(jnp.int32, (8, NZ), 0)
    mine = jnp.where(
        row == 0,
        jnp.sum(lost_of, axis=0, keepdims=True),
        jnp.where(row == 1, jnp.sum(sizes_of, axis=0, keepdims=True), 0.0),
    )

    def spread(buffer, me, steps, base):
        buffer[me] = mine
        copies = []
        for number, step in enumerate(steps):
            copies.append(
                pltpu.make_async_remote_copy(
                    src_ref=buffer.at[me],
                    dst_ref=buffer.at[me],
                    send_sem=red_send.at[base + number],
                    recv_sem=red_recv.at[base + number],
                    device_id=device(*step),
                    device_id_type=MESH,
                )
            )
        for copy in copies:
            copy.start()
        return copies

    def added(buffer, copies):
        for copy in copies:
            copy.wait_recv()
        terms = [buffer[k] for k in range(len(copies) + 1)]
        while len(terms) > 1:
            terms = [a + b for a, b in zip(terms[::2], terms[1::2])]
        return terms[0]

    sent = spread(red_p, gx * nz + gz, plane, 0)
    stores = [pltpu.make_async_copy(raw, raw_hbm, store_sem.at[NX])]
    stores[0].start()
    for x in range(NX):
        for h in range(HALVES):
            rows = slice(8 * h, 8 * h + 8)
            back, _ = transpose(0, reverse(gather(3, x, h)), x, h)
            for i in range(19):
                adj[x, i, rows, :] = back[i]
        stores.append(pltpu.make_async_copy(adj.at[x], adj_hbm.at[:, x], store_sem.at[x]))
        stores[-1].start()
    for turn in range(ROUNDS):
        for (dx, dy, dz), copy in exchanges[turn].items():
            pl.when(exists(dx, dy, dz))(copy.wait_send)
    mine = added(red_p, sent)
    last_sent = spread(red_y, gy, column, len(plane))
    mine = added(red_y, last_sent)
    sent = sent + last_sent

    cells = NX * NY * NZ * nx * ny * nz
    loss = jnp.sum(jnp.where(row == 0, mine, 0.0))
    size = jnp.sum(jnp.where(row == 1, mine, 0.0))
    sums_ref[0] = 20.0 * loss / cells
    sums_ref[1] = size / cells + 1e-06

    for copy in sent:
        copy.wait_send()
    for copy in stores:
        copy.wait()


def finish(sums_in, adj_in, raw_in, adj_out, sens_out, obj_out, raw, adj, sums, sem):
    cuts = [19 * k // PIECES for k in range(PIECES + 1)]
    loads = [
        pltpu.make_async_copy(sums_in, sums, sem.at[2 * PIECES]),
        pltpu.make_async_copy(raw_in, raw, sem.at[2 * PIECES + 1]),
    ]
    coming, going = [], []
    for k in range(PIECES):
        part = slice(cuts[k], cuts[k + 1])
        coming.append(pltpu.make_async_copy(adj_in.at[part], adj.at[part], sem.at[k]))
        going.append(
            pltpu.make_async_copy(adj.at[part], adj_out.at[part], sem.at[PIECES + k])
        )
        coming[k].start()
    for copy in loads:
        copy.start()
    for k in range(PIECES):
        coming[k].wait()
        going[k].start()
    for copy in loads:
        copy.wait()
    obj_out[0] = sums[0]
    inverse = 1.0 / jnp.full((8, NZ), sums[1], F32)
    for x in range(NX):
        for h in range(HALVES):
            rows = slice(8 * h, 8 * h + 8)
            raw[x, rows, :] = raw[x, rows, :] * inverse
    store = pltpu.make_async_copy(raw, sens_out, sem.at[2 * PIECES + 2])
    store.start()
    for k in range(PIECES):
        going[k].wait()
    store.wait()


def solution(mesh):
    nx, ny, nz = (mesh.shape[a] for a in ("gx", "gy", "gz"))
    partners = nx * nz + ny - 2

    def body(populations, design, labels):
        cells = (NX, NY, NZ)
        adjoint, raw, sums = pl.pallas_call(
            lambda *refs: kernel((nx, ny, nz), *refs),
            out_shape=(
                jax.ShapeDtypeStruct((19,) + cells, F32),
                jax.ShapeDtypeStruct(cells, F32),
                jax.ShapeDtypeStruct((2,), F32),
            ),
            in_specs=[pl.BlockSpec(memory_space=pltpu.HBM)] * 3,
            out_specs=(
                pl.BlockSpec(memory_space=pltpu.HBM),
                pl.BlockSpec(memory_space=pltpu.HBM),
                pl.BlockSpec(memory_space=pltpu.SMEM),
            ),
            scratch_shapes=[
                pltpu.VMEM((NX, 19, NY, NZ), F32),
                pltpu.VMEM(cells, F32),
                pltpu.VMEM(cells, jnp.int32),
                pltpu.VMEM((NX, 19, NY, NZ), F32),
                pltpu.VMEM((ROUNDS, NX + 2, 20, NY + 16, NZ), F32),
                pltpu.VMEM((ROUNDS, 2, NY, NZ), F32),
                pltpu.VMEM((ROUNDS, 2, NY + 16, NZ), F32),
                pltpu.VMEM((ROUNDS, 2, 2, NY, NZ), F32),
                pltpu.VMEM((2, 5) + cells, F32),
                pltpu.VMEM(cells, F32),
                pltpu.VMEM((nx * nz, 8, NZ), F32),
                pltpu.VMEM((ny, 8, NZ), F32),
                pltpu.SemaphoreType.DMA((6,)),
                pltpu.SemaphoreType.DMA((NX + 1,)),
                pltpu.SemaphoreType.DMA((ROUNDS, 18)),
                pltpu.SemaphoreType.DMA((ROUNDS, 18)),
                pltpu.SemaphoreType.DMA((partners,)),
                pltpu.SemaphoreType.DMA((partners,)),
            ],
            compiler_params=pltpu.CompilerParams(
                collective_id=0, has_side_effects=True, vmem_limit_bytes=60 * 1024 * 1024
            ),
            cost_estimate=pl.CostEstimate(
                flops=10_000_000, bytes_accessed=1_500_000, transcendentals=0
            ),
        )(populations, design, labels)
        adjoint, sensitivity, objective = pl.pallas_call(
            finish,
            out_shape=(
                jax.ShapeDtypeStruct((19,) + cells, F32),
                jax.ShapeDtypeStruct(cells, F32),
                jax.ShapeDtypeStruct((1,), F32),
            ),
            in_specs=[
                pl.BlockSpec(memory_space=pltpu.HBM),
                pl.BlockSpec(memory_space=pltpu.HBM),
                pl.BlockSpec(memory_space=pltpu.HBM),
            ],
            out_specs=(
                pl.BlockSpec(memory_space=pltpu.HBM),
                pl.BlockSpec(memory_space=pltpu.HBM),
                pl.BlockSpec(memory_space=pltpu.SMEM),
            ),
            scratch_shapes=[
                pltpu.VMEM(cells, F32),
                pltpu.VMEM((19,) + cells, F32),
                pltpu.SMEM((2,), F32),
                pltpu.SemaphoreType.DMA((2 * PIECES + 3,)),
            ],
            compiler_params=pltpu.CompilerParams(vmem_limit_bytes=60 * 1024 * 1024),
        )(sums, adjoint, raw)
        return adjoint, sensitivity, objective.reshape(())

    in_specs = (P(None, "gx", "gy", "gz"), P("gx", "gy", "gz"), P("gx", "gy", "gz"))
    out_specs = (P(None, "gx", "gy", "gz"), P("gx", "gy", "gz"), P())
    return jax.shard_map(body, mesh=mesh, in_specs=in_specs, out_specs=out_specs, check_vma=False)
```

```python
import jax
import jax.numpy as jnp
from jax import lax
from jax.experimental import pallas as pl
from jax.experimental.pallas import tpu as pltpu
from jax.sharding import PartitionSpec as P

VELOCITY = [
    (0, 0, 0),
    (1, 0, 0),
    (-1, 0, 0),
    (0, 1, 0),
    (0, -1, 0),
    (0, 0, 1),
    (0, 0, -1),
    (1, 1, 0),
    (-1, -1, 0),
    (1, -1, 0),
    (-1, 1, 0),
    (1, 0, 1),
    (-1, 0, -1),
    (1, 0, -1),
    (-1, 0, 1),
    (0, 1, 1),
    (0, -1, -1),
    (0, 1, -1),
    (0, -1, 1),
]
OPPOSITE = [0, 2, 1, 4, 3, 6, 5, 8, 7, 10, 9, 12, 11, 14, 13, 16, 15, 18, 17]
PAIRS = [1, 3, 5, 7, 9, 11, 13, 15, 17]
RELAX = 1.6
INFLOW = 0.05
MESH = pl.DeviceIdType.MESH
F32 = jnp.float32

ORDER = [9, 1, 11, 13, 7, 3, 15, 17, 10, 2, 12, 14, 8, 4, 16, 18, 9, 5, 6, 0]
SLOT = {index: ORDER.index(index) for index in range(19)}
TWIN = 16
ZPLUS = [5, 11, 14, 15, 18]
ZMINUS = [6, 12, 13, 16, 17]
ROW = 8

NX, NY, NZ = 4, 16, 128
HALVES = NY // 8
ROUNDS = 4
PIECES = 4


def neighbours():
    found = []
    for dx, dy, dz in VELOCITY[1:]:
        found.append((dx, dy, dz))
    return found


NEIGHBOURS = neighbours()


def kernel(
    sizes,
    pop_hbm,
    design_hbm,
    labels_hbm,
    adj_hbm,
    raw_hbm,
    sums_ref,
    pop,
    design,
    labels,
    adj,
    pads,
    zsend,
    zrecv,
    zedge,
    saved,
    raw,
    red_p,
    red_y,
    load_sem,
    store_sem,
    send_sem,
    recv_sem,
    red_send,
    red_recv,
):
    nx, ny, nz = sizes
    gx, gy, gz = lax.axis_index("gx"), lax.axis_index("gy"), lax.axis_index("gz")

    def device(dx, dy, dz):
        return {
            "gx": lax.rem(gx + (dx + nx), nx) if dx else gx,
            "gy": lax.rem(gy + (dy + ny), ny) if dy else gy,
            "gz": lax.rem(gz + (dz + nz), nz) if dz else gz,
        }

    inside = {
        "gx": (gx > 0, gx < nx - 1),
        "gy": (gy > 0, gy < ny - 1),
        "gz": (gz > 0, gz < nz - 1),
    }

    def exists(dx, dy, dz):
        found = None
        for axis, d in (("gx", dx), ("gy", dy), ("gz", dz)):
            if d:
                here = inside[axis][1 if d > 0 else 0]
                found = here if found is None else found & here
        return found

    loads = [
        pltpu.make_async_copy(design_hbm, design, load_sem.at[4]),
        pltpu.make_async_copy(labels_hbm, labels, load_sem.at[5]),
    ]
    slabs = {}
    for x in (0, 3, 1, 2):
        slabs[x] = pltpu.make_async_copy(pop_hbm.at[:, x], pop.at[x], load_sem.at[x])
    for copy in loads:
        copy.start()
    for x in (0, 3, 1, 2):
        slabs[x].start()

    @pl.when(gx == 0)
    def _():
        pads[:, 0, 0:5, 7:25, :] = jnp.zeros((ROUNDS, 5, 18, NZ), F32)
        zedge[:, :, 0] = jnp.zeros((ROUNDS, 2, NY, NZ), F32)

    @pl.when(gx == nx - 1)
    def _():
        pads[:, 5, 8:13, 7:25, :] = jnp.zeros((ROUNDS, 5, 18, NZ), F32)
        zedge[:, :, 1] = jnp.zeros((ROUNDS, 2, NY, NZ), F32)

    @pl.when(gy == 0)
    def _():
        pads[:, :, 4:9, 7:8, :] = jnp.zeros((ROUNDS, NX + 2, 5, 1, NZ), F32)
        zrecv[:, :, 7:8, :] = jnp.zeros((ROUNDS, 2, 1, NZ), F32)

    @pl.when(gy == ny - 1)
    def _():
        pads[:, :, 12:17, 24:25, :] = jnp.zeros((ROUNDS, NX + 2, 5, 1, NZ), F32)
        pads[:, 0, 0:1, 24:25, :] = jnp.zeros((ROUNDS, 1, 1, NZ), F32)
        zrecv[:, :, 24:25, :] = jnp.zeros((ROUNDS, 2, 1, NZ), F32)

    @pl.when(gz == 0)
    def _():
        zrecv[:, 0, 7:25, :] = jnp.zeros((ROUNDS, 18, NZ), F32)
        zedge[:, 0] = jnp.zeros((ROUNDS, 2, NY, NZ), F32)

    @pl.when(gz == nz - 1)
    def _():
        zrecv[:, 1, 7:25, :] = jnp.zeros((ROUNDS, 18, NZ), F32)
        zedge[:, 1] = jnp.zeros((ROUNDS, 2, NY, NZ), F32)

    barrier = pltpu.get_barrier_semaphore()
    plane = [(a, 0, b) for a in range(nx) for b in range(nz) if a or b]
    column = [(0, k, 0) for k in range(1, ny)]
    partners = [n for n in NEIGHBOURS if n[1] and (n[0] or n[2])] + plane + column
    for partner in partners:
        pl.semaphore_signal(barrier, inc=1, device_id=device(*partner), device_id_type=MESH)

    lane = lax.broadcasted_iota(jnp.int32, (8, NZ), 1)

    def exchange(turn):
        pad, zs, zr, ze = pads.at[turn], zsend.at[turn], zrecv.at[turn], zedge.at[turn]
        copies = {}
        for number, (dx, dy, dz) in enumerate(NEIGHBOURS):
            if dz == 0:
                if dx > 0:
                    xs, xd, group = 4, 0, slice(0, 5)
                elif dx < 0:
                    xs, xd, group = 1, 5, slice(8, 13)
                else:
                    xs, xd, group = slice(1, 5), slice(1, 5), slice(4, 9) if dy > 0 else slice(12, 17)
                if dy > 0:
                    ys, yd = slice(23, 24), slice(7, 8)
                elif dy < 0:
                    ys, yd = slice(8, 9), slice(24, 25)
                else:
                    ys, yd = slice(8, 24), slice(8, 24)
                if dx and dy:
                    group = SLOT[VELOCITY.index((dx, dy, dz))]
                src, dst = pad.at[xs, group, ys], pad.at[xd, group, yd]
            else:
                s = 0 if dz > 0 else 1
                if dx:
                    src, dst = zs.at[s], ze.at[s, 0 if dx > 0 else 1]
                elif dy > 0:
                    src, dst = zs.at[s, 15:16], zr.at[s, 7:8]
                elif dy < 0:
                    src, dst = zs.at[s, 0:1], zr.at[s, 24:25]
                else:
                    src, dst = zs.at[s], zr.at[s, 8:24]
            copies[(dx, dy, dz)] = pltpu.make_async_remote_copy(
                src_ref=src,
                dst_ref=dst,
                send_sem=send_sem.at[turn, number],
                recv_sem=recv_sem.at[turn, number],
                device_id=device(dx, dy, dz),
                device_id_type=MESH,
            )
        return copies

    exchanges = [exchange(turn) for turn in range(ROUNDS)]

    def send_x(turn):
        for (dx, dy, dz), copy in exchanges[turn].items():
            if dx and not dz:
                pl.when(exists(dx, dy, dz))(copy.start)

    def send_rest(turn):
        rest = [item for item in exchanges[turn].items() if item[0][2] or not item[0][0]]
        for (dx, dy, dz), copy in sorted(rest, key=lambda item: not item[0][1]):
            pl.when(exists(dx, dy, dz))(copy.start)

    def receive(turn):
        for (dx, dy, dz), copy in exchanges[turn].items():
            pl.when(exists(-dx, -dy, -dz))(copy.wait_recv)

    def column_of(index, x):
        names = ZPLUS if VELOCITY[index][2] > 0 else ZMINUS
        return 8 * names.index(index) + 1 + x

    def gather(turn, x, h):
        values = []
        for index in range(19):
            cx, cy, cz = VELOCITY[index]
            slot = SLOT[index]
            if index == 9 and x > 0:
                slot = TWIN
            start = ROW + 8 * h - cy
            value = pads[turn, x + 1 - cx, slot, start : start + 8, :]
            if cz:
                s = 0 if cz > 0 else 1
                column = column_of(index, (x - cx) % NX)
                if 0 <= x - cx < NX:
                    halo = zrecv[turn, s, start : start + 8, :]
                else:
                    halo = zedge[turn, s, 0 if cx > 0 else 1, 8 * h : 8 * h + 8, :]
                value = jnp.where(lane == column, halo, value)
                value = pltpu.roll(value, NZ - column if cz > 0 else NZ - 1 - column, 1)
            values.append(value)
        return values

    def scatter(turn, x, h, values, packed):
        rows = slice(ROW + 8 * h, ROW + 8 * h + 8)
        for index in range(19):
            cz = VELOCITY[index][2]
            value = values[index]
            if cz:
                s = 0 if cz > 0 else 1
                column = column_of(index, x)
                value = pltpu.roll(value, column + 1 if cz > 0 else column, 1)
                packed[s][h] = jnp.where(lane == column, value, packed[s][h])
            pads[turn, x + 1, SLOT[index], rows, :] = value
            if index == 9:
                pads[turn, x + 1, TWIN, rows, :] = value

    def stage(turn, block):
        zero = jnp.zeros((8, NZ), F32)
        packed = [[zero] * HALVES, [zero] * HALVES]
        for x in (0, 3):
            for h in range(HALVES):
                scatter(turn, x, h, block(x, h), packed)
        if turn == 0:
            pl.semaphore_wait(barrier, len(partners))
        send_x(turn)
        for x in (1, 2):
            for h in range(HALVES):
                scatter(turn, x, h, block(x, h), packed)
        for s in range(2):
            for h in range(HALVES):
                zsend[turn, s, 8 * h : 8 * h + 8, :] = packed[s][h]
        send_rest(turn)

    def moments(f):
        sums = {i: f[i] + f[i + 1] for i in PAIRS}
        diff = {i: f[i] - f[i + 1] for i in PAIRS}
        density = f[0] + (
            ((sums[1] + sums[3]) + (sums[5] + sums[7]))
            + ((sums[9] + sums[11]) + (sums[13] + (sums[15] + sums[17])))
        )
        jx = diff[1] + ((diff[7] + diff[9]) + (diff[11] + diff[13]))
        jy = diff[3] + ((diff[7] - diff[9]) + (diff[15] + diff[17]))
        jz = diff[5] + ((diff[11] - diff[13]) + (diff[15] - diff[17]))
        return density, jx, jy, jz

    def along(index, v):
        total = None
        for axis in range(3):
            c = VELOCITY[index][axis]
            if c:
                if total is None:
                    total = v[axis]
                else:
                    total = total + v[axis] if c > 0 else total - v[axis]
        return total

    def collide(which, f, x, h):
        rows = slice(8 * h, 8 * h + 8)
        mark = labels[x, rows, :]
        fluid, solid, inlet, outlet = mark == 1, mark == 2, mark == 3, mark == 4
        damping = 1.0 / (1.0 + design[x, rows, :])
        density, jx, jy, jz = moments(f)
        inverse = 1.0 / jnp.where(solid, 1.0, density)
        factor = inverse * jnp.where(fluid, damping, jnp.where(outlet, 1.0, 0.0))
        ux, uy, uz = jx * factor, jy * factor, jnp.where(inlet, INFLOW, jz * factor)
        saved[which, 0, x, rows, :] = ux
        saved[which, 1, x, rows, :] = uy
        saved[which, 2, x, rows, :] = uz
        saved[which, 3, x, rows, :] = jnp.where(
            fluid, RELAX * damping, jnp.where(outlet, inverse, 0.0)
        )
        saved[which, 4, x, rows, :] = jnp.where(fluid, -RELAX * damping * density, 0.0)
        weight = jnp.where(fluid, RELAX * density, 1.0)
        keep = jnp.where(fluid, 1.0 - RELAX, 0.0)
        rest = 1.0 - 1.5 * (ux * ux + uy * uy + uz * uz)
        wide, thin = weight * (1.0 / 18.0), weight * (1.0 / 36.0)
        post = [None] * 19
        post[0] = jnp.where(solid, f[0], keep * f[0] + (weight * (1.0 / 3.0)) * rest)
        for i in PAIRS:
            w = wide if i < 7 else thin
            cu = along(i, (ux, uy, uz))
            even = w * (rest + 4.5 * (cu * cu))
            odd = w * (3.0 * cu)
            post[i] = jnp.where(solid, f[i + 1], keep * f[i] + (even + odd))
            post[i + 1] = jnp.where(solid, f[i], keep * f[i + 1] + (even - odd))
        return post

    def transpose(which, g, x, h):
        rows = slice(8 * h, 8 * h + 8)
        mark = labels[x, rows, :]
        fluid, solid = mark == 1, mark == 2
        u = [saved[which, a, x, rows, :] for a in range(3)]
        gain, slope = saved[which, 3, x, rows, :], saved[which, 4, x, rows, :]
        ux, uy, uz = u
        s = {i: g[i] + g[i + 1] for i in PAIRS}
        d = {i: g[i] - g[i + 1] for i in PAIRS}
        wide, thin = 1.0 / 18.0, 1.0 / 36.0
        sxy, sxz, syz = s[7] + s[9], s[11] + s[13], s[15] + s[17]
        m0 = (
            (1.0 / 3.0) * g[0]
            + wide * (s[1] + s[3] + s[5])
            + thin * (sxy + sxz + syz)
        )
        m1x = wide * d[1] + thin * ((d[7] + d[9]) + (d[11] + d[13]))
        m1y = wide * d[3] + thin * ((d[7] - d[9]) + (d[15] + d[17]))
        m1z = wide * d[5] + thin * ((d[11] - d[13]) + (d[15] - d[17]))
        mxx = wide * s[1] + thin * (sxy + sxz)
        myy = wide * s[3] + thin * (sxy + syz)
        mzz = wide * s[5] + thin * (sxz + syz)
        mxy = thin * (s[7] - s[9])
        mxz = thin * (s[11] - s[13])
        myz = thin * (s[15] - s[17])
        hx = mxx * ux + mxy * uy + mxz * uz
        hy = mxy * ux + myy * uy + myz * uz
        hz = mxz * ux + myz * uy + mzz * uz
        quad = ux * hx + uy * hy + uz * hz
        square = ux * ux + uy * uy + uz * uz
        bx = 3.0 * (m1x - ux * m0) + 9.0 * hx
        by = 3.0 * (m1y - uy * m0) + 9.0 * hy
        bz = 3.0 * (m1z - uz * m0) + 9.0 * hz
        bu = bx * ux + by * uy + bz * uz
        base = jnp.where(
            fluid, RELAX * (m0 + 1.5 * square * m0 - 4.5 * quad), -(bu * gain)
        )
        e = (bx * gain, by * gain, bz * gain)
        keep = jnp.where(fluid, 1.0 - RELAX, 0.0)
        back = [None] * 19
        back[0] = jnp.where(solid, g[0], keep * g[0] + base)
        for i in PAIRS:
            ce = along(i, e)
            back[i] = jnp.where(solid, g[i + 1], keep * g[i] + (base + ce))
            back[i + 1] = jnp.where(solid, g[i], keep * g[i + 1] + (base - ce))
        return back, slope * bu

    def reverse(values):
        return [values[OPPOSITE[i]] for i in range(19)]

    for copy in loads:
        copy.wait()
    waited = set()

    def block_one(x, h):
        if x not in waited:
            slabs[x].wait()
            waited.add(x)
        f = [pop[x, i, 8 * h : 8 * h + 8, :] for i in range(19)]
        return collide(0, f, x, h)

    stage(0, block_one)

    receive(0)
    stage(1, lambda x, h: collide(1, gather(0, x, h), x, h))

    receive(1)
    lost = []

    def block_final(x, h):
        rows = slice(8 * h, 8 * h + 8)
        solidity = design[x, rows, :]
        fluid = labels[x, rows, :] == 1
        density, jx, jy, jz = moments(gather(1, x, h))
        inverse = jnp.where(fluid, 1.0 / jnp.where(fluid, density, 1.0), 0.0)
        v = (jx * inverse, jy * inverse, jz * inverse)
        square = v[0] * v[0] + v[1] * v[1] + v[2] * v[2]
        direct = 10.0 * density * square
        raw[x, rows, :] = direct
        lost.append(solidity * direct)
        base = -10.0 * solidity * square
        twice = 20.0 * solidity
        e = (twice * v[0], twice * v[1], twice * v[2])
        g = [base] * 19
        for i in PAIRS:
            ce = along(i, e)
            g[i], g[i + 1] = base + ce, base - ce
        return reverse(g)

    stage(2, block_final)

    receive(2)

    def block_two(x, h):
        rows = slice(8 * h, 8 * h + 8)
        back, sens = transpose(1, reverse(gather(2, x, h)), x, h)
        raw[x, rows, :] = raw[x, rows, :] + sens
        return reverse(back)

    stage(3, block_two)

    receive(3)
    sizes_of = jnp.zeros((8, NZ), F32)
    for x in range(NX):
        for h in range(HALVES):
            rows = slice(8 * h, 8 * h + 8)
            _, sens = transpose(0, reverse(gather(3, x, h)), x, h)
            total = raw[x, rows, :] + sens
            raw[x, rows, :] = total
            sizes_of = sizes_of + jnp.abs(total)

    lost_of = lost[0]
    for term in lost[1:]:
        lost_of = lost_of + term
    row = lax.broadcasted_iota(jnp.int32, (8, NZ), 0)
    mine = jnp.where(
        row == 0,
        jnp.sum(lost_of, axis=0, keepdims=True),
        jnp.where(row == 1, jnp.sum(sizes_of, axis=0, keepdims=True), 0.0),
    )

    def spread(buffer, me, steps, base):
        buffer[me] = mine
        copies = []
        for number, step in enumerate(steps):
            copies.append(
                pltpu.make_async_remote_copy(
                    src_ref=buffer.at[me],
                    dst_ref=buffer.at[me],
                    send_sem=red_send.at[base + number],
                    recv_sem=red_recv.at[base + number],
                    device_id=device(*step),
                    device_id_type=MESH,
                )
            )
        for copy in copies:
            copy.start()
        return copies

    def added(buffer, copies):
        for copy in copies:
            copy.wait_recv()
        terms = [buffer[k] for k in range(len(copies) + 1)]
        while len(terms) > 1:
            terms = [a + b for a, b in zip(terms[::2], terms[1::2])]
        return terms[0]

    sent = spread(red_p, gx * nz + gz, plane, 0)
    stores = [pltpu.make_async_copy(raw, raw_hbm, store_sem.at[NX])]
    stores[0].start()
    for x in range(NX):
        for h in range(HALVES):
            rows = slice(8 * h, 8 * h + 8)
            back, _ = transpose(0, reverse(gather(3, x, h)), x, h)
            for i in range(19):
                adj[x, i, rows, :] = back[i]
        stores.append(pltpu.make_async_copy(adj.at[x], adj_hbm.at[:, x], store_sem.at[x]))
        stores[-1].start()
    for turn in range(ROUNDS):
        for (dx, dy, dz), copy in exchanges[turn].items():
            pl.when(exists(dx, dy, dz))(copy.wait_send)
    mine = added(red_p, sent)
    last_sent = spread(red_y, gy, column, len(plane))
    mine = added(red_y, last_sent)
    sent = sent + last_sent

    cells = NX * NY * NZ * nx * ny * nz
    loss = jnp.sum(jnp.where(row == 0, mine, 0.0))
    size = jnp.sum(jnp.where(row == 1, mine, 0.0))
    sums_ref[0] = 20.0 * loss / cells
    sums_ref[1] = size / cells + 1e-06

    for copy in sent:
        copy.wait_send()
    for copy in stores:
        copy.wait()


def finish(sums_in, adj_in, raw_in, adj_out, sens_out, obj_out, raw, adj, sums, sem):
    cuts = [19 * k // PIECES for k in range(PIECES + 1)]
    loads = [
        pltpu.make_async_copy(sums_in, sums, sem.at[2 * PIECES]),
        pltpu.make_async_copy(raw_in, raw, sem.at[2 * PIECES + 1]),
    ]
    coming, going = [], []
    for k in range(PIECES):
        part = slice(cuts[k], cuts[k + 1])
        coming.append(pltpu.make_async_copy(adj_in.at[part], adj.at[part], sem.at[k]))
        going.append(
            pltpu.make_async_copy(adj.at[part], adj_out.at[part], sem.at[PIECES + k])
        )
        coming[k].start()
    for copy in loads:
        copy.start()
    for k in range(PIECES):
        coming[k].wait()
        going[k].start()
    for copy in loads:
        copy.wait()
    obj_out[0] = sums[0]
    inverse = 1.0 / jnp.full((8, NZ), sums[1], F32)
    for x in range(NX):
        for h in range(HALVES):
            rows = slice(8 * h, 8 * h + 8)
            raw[x, rows, :] = raw[x, rows, :] * inverse
    store = pltpu.make_async_copy(raw, sens_out, sem.at[2 * PIECES + 2])
    store.start()
    for k in range(PIECES):
        going[k].wait()
    store.wait()


def solution(mesh):
    nx, ny, nz = (mesh.shape[a] for a in ("gx", "gy", "gz"))
    partners = nx * nz + ny - 2

    def body(populations, design, labels):
        cells = (NX, NY, NZ)
        adjoint, raw, sums = pl.pallas_call(
            lambda *refs: kernel((nx, ny, nz), *refs),
            out_shape=(
                jax.ShapeDtypeStruct((19,) + cells, F32),
                jax.ShapeDtypeStruct(cells, F32),
                jax.ShapeDtypeStruct((2,), F32),
            ),
            in_specs=[pl.BlockSpec(memory_space=pltpu.HBM)] * 3,
            out_specs=(
                pl.BlockSpec(memory_space=pltpu.HBM),
                pl.BlockSpec(memory_space=pltpu.HBM),
                pl.BlockSpec(memory_space=pltpu.SMEM),
            ),
            scratch_shapes=[
                pltpu.VMEM((NX, 19, NY, NZ), F32),
                pltpu.VMEM(cells, F32),
                pltpu.VMEM(cells, jnp.int32),
                pltpu.VMEM((NX, 19, NY, NZ), F32),
                pltpu.VMEM((ROUNDS, NX + 2, 20, NY + 16, NZ), F32),
                pltpu.VMEM((ROUNDS, 2, NY, NZ), F32),
                pltpu.VMEM((ROUNDS, 2, NY + 16, NZ), F32),
                pltpu.VMEM((ROUNDS, 2, 2, NY, NZ), F32),
                pltpu.VMEM((2, 5) + cells, F32),
                pltpu.VMEM(cells, F32),
                pltpu.VMEM((nx * nz, 8, NZ), F32),
                pltpu.VMEM((ny, 8, NZ), F32),
                pltpu.SemaphoreType.DMA((6,)),
                pltpu.SemaphoreType.DMA((NX + 1,)),
                pltpu.SemaphoreType.DMA((ROUNDS, 18)),
                pltpu.SemaphoreType.DMA((ROUNDS, 18)),
                pltpu.SemaphoreType.DMA((partners,)),
                pltpu.SemaphoreType.DMA((partners,)),
            ],
            compiler_params=pltpu.CompilerParams(
                collective_id=0, has_side_effects=True, vmem_limit_bytes=60 * 1024 * 1024
            ),
            cost_estimate=pl.CostEstimate(
                flops=10_000_000, bytes_accessed=1_500_000, transcendentals=0
            ),
        )(populations, design, labels)
        adjoint, sensitivity, objective = pl.pallas_call(
            finish,
            out_shape=(
                jax.ShapeDtypeStruct((19,) + cells, F32),
                jax.ShapeDtypeStruct(cells, F32),
                jax.ShapeDtypeStruct((1,), F32),
            ),
            in_specs=[
                pl.BlockSpec(memory_space=pltpu.HBM),
                pl.BlockSpec(memory_space=pltpu.HBM),
                pl.BlockSpec(memory_space=pltpu.HBM),
            ],
            out_specs=(
                pl.BlockSpec(memory_space=pltpu.HBM),
                pl.BlockSpec(memory_space=pltpu.HBM),
                pl.BlockSpec(memory_space=pltpu.SMEM),
            ),
            scratch_shapes=[
                pltpu.VMEM(cells, F32),
                pltpu.VMEM((19,) + cells, F32),
                pltpu.SMEM((2,), F32),
                pltpu.SemaphoreType.DMA((2 * PIECES + 3,)),
            ],
            compiler_params=pltpu.CompilerParams(vmem_limit_bytes=60 * 1024 * 1024),
        )(sums, adjoint, raw)
        return adjoint, sensitivity, objective.reshape(())

    in_specs = (P(None, "gx", "gy", "gz"), P("gx", "gy", "gz"), P("gx", "gy", "gz"))
    out_specs = (P(None, "gx", "gy", "gz"), P("gx", "gy", "gz"), P())
    return jax.shard_map(body, mesh=mesh, in_specs=in_specs, out_specs=out_specs, check_vma=False)
```

```python
import jax
import jax.numpy as jnp
from jax import lax
from jax.experimental import pallas as pl
from jax.experimental.pallas import tpu as pltpu
from jax.sharding import PartitionSpec as P

VELOCITY = [
    (0, 0, 0),
    (1, 0, 0),
    (-1, 0, 0),
    (0, 1, 0),
    (0, -1, 0),
    (0, 0, 1),
    (0, 0, -1),
    (1, 1, 0),
    (-1, -1, 0),
    (1, -1, 0),
    (-1, 1, 0),
    (1, 0, 1),
    (-1, 0, -1),
    (1, 0, -1),
    (-1, 0, 1),
    (0, 1, 1),
    (0, -1, -1),
    (0, 1, -1),
    (0, -1, 1),
]
OPPOSITE = [0, 2, 1, 4, 3, 6, 5, 8, 7, 10, 9, 12, 11, 14, 13, 16, 15, 18, 17]
PAIRS = [1, 3, 5, 7, 9, 11, 13, 15, 17]
RELAX = 1.6
INFLOW = 0.05
MESH = pl.DeviceIdType.MESH
F32 = jnp.float32

ORDER = [9, 1, 11, 13, 7, 3, 15, 17, 10, 2, 12, 14, 8, 4, 16, 18, 9, 5, 6, 0]
SLOT = {index: ORDER.index(index) for index in range(19)}
TWIN = 16
ZPLUS = [5, 11, 14, 15, 18]
ZMINUS = [6, 13, 12, 17, 16]
ROW = 8

NX, NY, NZ = 4, 16, 128
HALVES = NY // 8
ROUNDS = 4
PIECES = 4


def neighbours():
    found = []
    for dx, dy, dz in VELOCITY[1:]:
        found.append((dx, dy, dz))
    return found


NEIGHBOURS = neighbours()


def kernel(
    sizes,
    pop_hbm,
    design_hbm,
    labels_hbm,
    adj_hbm,
    raw_hbm,
    sums_ref,
    pop,
    design,
    labels,
    adj,
    pads,
    zsend,
    zrecv,
    zedge,
    saved,
    raw,
    part,
    tile,
    zpart,
    from_x,
    from_y,
    from_xy,
    from_plane,
    from_z,
    drag,
    red_p,
    red_y,
    load_sem,
    store_sem,
    send_sem,
    recv_sem,
    part_send,
    part_recv,
    drag_send,
    drag_recv,
    red_send,
    red_recv,
):
    nx, ny, nz = sizes
    gx, gy, gz = lax.axis_index("gx"), lax.axis_index("gy"), lax.axis_index("gz")

    def device(dx, dy, dz):
        return {
            "gx": lax.rem(gx + (dx + nx), nx) if dx else gx,
            "gy": lax.rem(gy + (dy + ny), ny) if dy else gy,
            "gz": lax.rem(gz + (dz + nz), nz) if dz else gz,
        }

    inside = {
        "gx": (gx > 0, gx < nx - 1),
        "gy": (gy > 0, gy < ny - 1),
        "gz": (gz > 0, gz < nz - 1),
    }

    def exists(dx, dy, dz):
        found = None
        for axis, d in (("gx", dx), ("gy", dy), ("gz", dz)):
            if d:
                here = inside[axis][1 if d > 0 else 0]
                found = here if found is None else found & here
        return found

    loads = [
        pltpu.make_async_copy(design_hbm, design, load_sem.at[4]),
        pltpu.make_async_copy(labels_hbm, labels, load_sem.at[5]),
    ]
    slabs = {}
    for x in (0, 3, 1, 2):
        slabs[x] = pltpu.make_async_copy(pop_hbm.at[:, x], pop.at[x], load_sem.at[x])
    for copy in loads:
        copy.start()
    for x in (0, 3, 1, 2):
        slabs[x].start()

    @pl.when(gx == 0)
    def _():
        pads[:, 0, 0:5, 7:25, :] = jnp.zeros((ROUNDS, 5, 18, NZ), F32)
        zedge[:, :, 0] = jnp.zeros((ROUNDS, 2, NY, NZ), F32)

    @pl.when(gx == nx - 1)
    def _():
        pads[:, 5, 8:13, 7:25, :] = jnp.zeros((ROUNDS, 5, 18, NZ), F32)
        zedge[:, :, 1] = jnp.zeros((ROUNDS, 2, NY, NZ), F32)

    @pl.when(gy == 0)
    def _():
        pads[:, :, 4:9, 7:8, :] = jnp.zeros((ROUNDS, NX + 2, 5, 1, NZ), F32)
        zrecv[:, :, 7:8, :] = jnp.zeros((ROUNDS, 2, 1, NZ), F32)

    @pl.when(gy == ny - 1)
    def _():
        pads[:, :, 12:17, 24:25, :] = jnp.zeros((ROUNDS, NX + 2, 5, 1, NZ), F32)
        pads[:, 0, 0:1, 24:25, :] = jnp.zeros((ROUNDS, 1, 1, NZ), F32)
        zrecv[:, :, 24:25, :] = jnp.zeros((ROUNDS, 2, 1, NZ), F32)

    @pl.when(gz == 0)
    def _():
        zrecv[:, 0, 7:25, :] = jnp.zeros((ROUNDS, 18, NZ), F32)
        zedge[:, 0] = jnp.zeros((ROUNDS, 2, NY, NZ), F32)

    @pl.when(gz == nz - 1)
    def _():
        zrecv[:, 1, 7:25, :] = jnp.zeros((ROUNDS, 18, NZ), F32)
        zedge[:, 1] = jnp.zeros((ROUNDS, 2, NY, NZ), F32)

    from_y[...] = jnp.zeros(from_y.shape, F32)
    from_xy[...] = jnp.zeros(from_xy.shape, F32)
    from_plane[...] = jnp.zeros(from_plane.shape, F32)
    from_z[...] = jnp.zeros(from_z.shape, F32)
    drag[...] = jnp.zeros(drag.shape, F32)
    zpart[7:8, :] = jnp.zeros((1, NZ), F32)
    zpart[24:25, :] = jnp.zeros((1, NZ), F32)
    pads[1, 1:5, 4:9, 7:8, :] = jnp.zeros((NX, 5, 1, NZ), F32)
    pads[1, 1:5, 12:17, 24:25, :] = jnp.zeros((NX, 5, 1, NZ), F32)

    @pl.when(gx == 0)
    def _():
        from_x[0] = jnp.zeros((4, 2, NY + 16, NZ), F32)

    @pl.when(gx == nx - 1)
    def _():
        from_x[1] = jnp.zeros((4, 2, NY + 16, NZ), F32)

    barrier = pltpu.get_barrier_semaphore()
    plane = [(a, 0, b) for a in range(nx) for b in range(nz) if a or b]
    line = [(0, k, 0) for k in range(1, ny)]
    corners = [(a, b, c) for a in (1, -1) for b in (1, -1) for c in (1, -1)]
    partners = [n for n in NEIGHBOURS if n[1] and (n[0] or n[2])] + corners + plane + line
    for partner in partners:
        pl.semaphore_signal(barrier, inc=1, device_id=device(*partner), device_id_type=MESH)

    lane = lax.broadcasted_iota(jnp.int32, (8, NZ), 1)
    half = lane // 2
    place = half % 8
    even = lane % 2 == 0
    first, last = lane == 0, lane == NZ - 1
    ends = first | last

    def exchange(turn):
        pad, zs, zr, ze = pads.at[turn], zsend.at[turn], zrecv.at[turn], zedge.at[turn]
        copies = {}
        for number, (dx, dy, dz) in enumerate(NEIGHBOURS):
            if dz == 0:
                if dx > 0:
                    xs, xd, group = 4, 0, slice(0, 5)
                elif dx < 0:
                    xs, xd, group = 1, 5, slice(8, 13)
                else:
                    xs, xd, group = slice(1, 5), slice(1, 5), slice(4, 9) if dy > 0 else slice(12, 17)
                if dy > 0:
                    ys, yd = slice(23, 24), slice(7, 8)
                elif dy < 0:
                    ys, yd = slice(8, 9), slice(24, 25)
                else:
                    ys, yd = slice(8, 24), slice(8, 24)
                if dx and dy:
                    group = SLOT[VELOCITY.index((dx, dy, dz))]
                src, dst = pad.at[xs, group, ys], pad.at[xd, group, yd]
            else:
                s = 0 if dz > 0 else 1
                if dx:
                    src, dst = zs.at[s], ze.at[s, 0 if dx > 0 else 1]
                elif dy > 0:
                    src, dst = zs.at[s, 15:16], zr.at[s, 7:8]
                elif dy < 0:
                    src, dst = zs.at[s, 0:1], zr.at[s, 24:25]
                else:
                    src, dst = zs.at[s], zr.at[s, 8:24]
            copies[(dx, dy, dz)] = pltpu.make_async_remote_copy(
                src_ref=src,
                dst_ref=dst,
                send_sem=send_sem.at[turn, number],
                recv_sem=recv_sem.at[turn, number],
                device_id=device(dx, dy, dz),
                device_id_type=MESH,
            )
        return copies

    exchanges = {turn: exchange(turn) for turn in (0, 3)}

    def part_copies():
        copies = {}

        def copy(key, src, dst):
            number = len(copies)
            copies[key] = pltpu.make_async_remote_copy(
                src_ref=src,
                dst_ref=dst,
                send_sem=part_send.at[number],
                recv_sem=part_recv.at[number],
                device_id=device(*key[0]),
                device_id_type=MESH,
            )

        slabs_of = {1: slice(4, 6), -1: slice(0, 2), 0: slice(0, 6)}
        row_from = {1: slice(23, 25), -1: slice(7, 9), 0: slice(7, 25)}
        row_to = {1: slice(7, 9), -1: slice(23, 25), 0: slice(7, 25)}
        for dx in (1, -1, 0):
            for dy in (1, -1, 0):
                sx, sy = (1 - dx) // 2, (1 - dy) // 2
                if dx or dy:
                    src = part.at[:, slabs_of[dx], row_from[dy]]
                    if dx and dy:
                        dst = from_xy.at[sx, sy, :, :, 7:9]
                    elif dx:
                        dst = from_x.at[sx, :, :, 7:25]
                    else:
                        dst = from_y.at[sy, :, :, 7:9]
                    copy(((dx, dy, 0), "cells"), src, dst)
                    copy(
                        ((dx, dy, 0), "column"),
                        tile.at[row_from[dy]],
                        from_plane.at[1 - dx, 1 - dy, row_to[dy]],
                    )
                for s, dz in ((0, 1), (1, -1)):
                    copy(
                        ((dx, dy, dz), "column"),
                        tile.at[row_from[dy]],
                        from_z.at[s, 1 - dx, 1 - dy, row_to[dy]],
                    )
        return copies

    parts = part_copies()

    def drag_copies():
        copies = {}
        slab_from, slab_to = {1: 4, -1: 1, 0: slice(1, 5)}, {1: 0, -1: 5, 0: slice(1, 5)}
        row_from = {1: slice(23, 24), -1: slice(8, 9), 0: slice(8, 24)}
        row_to = {1: slice(7, 8), -1: slice(24, 25), 0: slice(8, 24)}
        for dx in (1, -1, 0):
            for dy in (1, -1, 0):
                if dx or dy:
                    number = len(copies)
                    copies[(dx, dy, 0)] = pltpu.make_async_remote_copy(
                        src_ref=drag.at[slab_from[dx], row_from[dy]],
                        dst_ref=drag.at[slab_to[dx], row_to[dy]],
                        send_sem=drag_send.at[number],
                        recv_sem=drag_recv.at[number],
                        device_id=device(dx, dy, 0),
                        device_id_type=MESH,
                    )
        return copies

    drags = drag_copies()

    def send_x(turn):
        for (dx, dy, dz), copy in exchanges[turn].items():
            if dx and not dz:
                pl.when(exists(dx, dy, dz))(copy.start)

    def send_rest(turn):
        rest = [item for item in exchanges[turn].items() if item[0][2] or not item[0][0]]
        for (dx, dy, dz), copy in sorted(rest, key=lambda item: not item[0][1]):
            pl.when(exists(dx, dy, dz))(copy.start)

    def receive(turn):
        for (dx, dy, dz), copy in exchanges[turn].items():
            pl.when(exists(-dx, -dy, -dz))(copy.wait_recv)

    def column_of(index, x, turn):
        up = VELOCITY[index][2] > 0
        k = (ZPLUS if up else ZMINUS).index(index)
        return 16 * k + 2 * (x + 1) + up if turn == 2 else 8 * k + 1 + x

    def gather(turn, x, h):
        values = []
        for index in range(19):
            cx, cy, cz = VELOCITY[index]
            slot = SLOT[index]
            if index == 9 and x > 0:
                slot = TWIN
            start = ROW + 8 * h - cy
            value = pads[turn, x + 1 - cx, slot, start : start + 8, :]
            if cz:
                s = 0 if cz > 0 else 1
                column = column_of(index, x - cx if turn == 2 else (x - cx) % NX, turn)
                if turn == 2:
                    halo = zrecv[2, 0, start : start + 8, :]
                elif 0 <= x - cx < NX:
                    halo = zrecv[turn, s, start : start + 8, :]
                else:
                    halo = zedge[turn, s, 0 if cx > 0 else 1, 8 * h : 8 * h + 8, :]
                value = jnp.where(lane == column, halo, value)
                value = pltpu.roll(value, NZ - column if cz > 0 else NZ - 1 - column, 1)
            values.append(value)
        return values

    def scatter(turn, x, h, values, packed):
        rows = slice(ROW + 8 * h, ROW + 8 * h + 8)
        for index in range(19):
            cz = VELOCITY[index][2]
            value = values[index]
            if cz:
                s = 0 if cz > 0 else 1
                column = column_of(index, x, turn)
                value = pltpu.roll(value, column + 1 if cz > 0 else column, 1)
                packed[s][h] = jnp.where(lane == column, value, packed[s][h])
            pads[turn, x + 1, SLOT[index], rows, :] = value
            if index == 9:
                pads[turn, x + 1, TWIN, rows, :] = value

    def scatter_open(x, h, values, packed):
        rows = slice(ROW + 8 * h, ROW + 8 * h + 8)
        for k in range(5):
            column = 16 * k + 2 * (x + 1)
            both = jnp.where(last, values[ZPLUS[k]], values[ZMINUS[k]])
            packed[h] = jnp.where(half == column // 2, pltpu.roll(both, column + 1, 1), packed[h])
        for index in range(19):
            cz = VELOCITY[index][2]
            value = values[index]
            if cz:
                value = pltpu.roll(value, 1 if cz > 0 else NZ - 1, 1)
                value = jnp.where(first if cz > 0 else last, 0.0, value)
            pads[1, x + 1, TWIN if index == 9 else SLOT[index], rows, :] = value

    def pack_drag(x, h, packed):
        rows = slice(8 * h, 8 * h + 8)
        value = jnp.where(labels[x, rows, :] == 1, design[x, rows, :], 0.0)
        drag[x + 1, ROW + 8 * h : ROW + 8 * h + 8, :] = value
        column = 64 + 2 * (x + 1)
        for s, shift in ((0, column + 1), (1, column)):
            packed[s][h] = jnp.where(lane == column, pltpu.roll(value, shift, 1), packed[s][h])

    def stage(turn, block):
        zero = jnp.zeros((8, NZ), F32)
        packed = [[zero] * HALVES, [zero] * HALVES]
        for x in (0, 3):
            for h in range(HALVES):
                scatter(turn, x, h, block(x, h), packed)
                if turn == 0:
                    pack_drag(x, h, packed)
        if turn == 0:
            pl.semaphore_wait(barrier, len(partners))
        send_x(turn)
        for x in (1, 2):
            for h in range(HALVES):
                scatter(turn, x, h, block(x, h), packed)
                if turn == 0:
                    pack_drag(x, h, packed)
        for s in range(2):
            for h in range(HALVES):
                zsend[turn, s, 8 * h : 8 * h + 8, :] = packed[s][h]
        send_rest(turn)

    def moments(f):
        sums = {i: f[i] + f[i + 1] for i in PAIRS}
        diff = {i: f[i] - f[i + 1] for i in PAIRS}
        density = f[0] + (
            ((sums[1] + sums[3]) + (sums[5] + sums[7]))
            + ((sums[9] + sums[11]) + (sums[13] + (sums[15] + sums[17])))
        )
        jx = diff[1] + ((diff[7] + diff[9]) + (diff[11] + diff[13]))
        jy = diff[3] + ((diff[7] - diff[9]) + (diff[15] + diff[17]))
        jz = diff[5] + ((diff[11] - diff[13]) + (diff[15] - diff[17]))
        return density, jx, jy, jz

    def along(index, v):
        total = None
        for axis in range(3):
            c = VELOCITY[index][axis]
            if c:
                if total is None:
                    total = v[axis]
                else:
                    total = total + v[axis] if c > 0 else total - v[axis]
        return total

    def collide(which, f, x, h):
        rows = slice(8 * h, 8 * h + 8)
        mark = labels[x, rows, :]
        fluid, solid, inlet, outlet = mark == 1, mark == 2, mark == 3, mark == 4
        damping = 1.0 / (1.0 + design[x, rows, :])
        density, jx, jy, jz = moments(f)
        inverse = 1.0 / jnp.where(solid, 1.0, density)
        factor = inverse * jnp.where(fluid, damping, jnp.where(outlet, 1.0, 0.0))
        ux, uy, uz = jx * factor, jy * factor, jnp.where(inlet, INFLOW, jz * factor)
        saved[which, 0, x, rows, :] = ux
        saved[which, 1, x, rows, :] = uy
        saved[which, 2, x, rows, :] = uz
        saved[which, 3, x, rows, :] = jnp.where(
            fluid, RELAX * damping, jnp.where(outlet, inverse, 0.0)
        )
        saved[which, 4, x, rows, :] = jnp.where(fluid, -RELAX * damping * density, 0.0)
        weight = jnp.where(fluid, RELAX * density, 1.0)
        keep = jnp.where(fluid, 1.0 - RELAX, 0.0)
        rest = 1.0 - 1.5 * (ux * ux + uy * uy + uz * uz)
        wide, thin = weight * (1.0 / 18.0), weight * (1.0 / 36.0)
        post = [None] * 19
        post[0] = jnp.where(solid, f[0], keep * f[0] + (weight * (1.0 / 3.0)) * rest)
        for i in PAIRS:
            w = wide if i < 7 else thin
            cu = along(i, (ux, uy, uz))
            even = w * (rest + 4.5 * (cu * cu))
            odd = w * (3.0 * cu)
            post[i] = jnp.where(solid, f[i + 1], keep * f[i] + (even + odd))
            post[i + 1] = jnp.where(solid, f[i], keep * f[i + 1] + (even - odd))
        return post

    def transpose(which, g, x, h):
        rows = slice(8 * h, 8 * h + 8)
        mark = labels[x, rows, :]
        fluid, solid = mark == 1, mark == 2
        u = [saved[which, a, x, rows, :] for a in range(3)]
        gain, slope = saved[which, 3, x, rows, :], saved[which, 4, x, rows, :]
        ux, uy, uz = u
        s = {i: g[i] + g[i + 1] for i in PAIRS}
        d = {i: g[i] - g[i + 1] for i in PAIRS}
        wide, thin = 1.0 / 18.0, 1.0 / 36.0
        sxy, sxz, syz = s[7] + s[9], s[11] + s[13], s[15] + s[17]
        m0 = (
            (1.0 / 3.0) * g[0]
            + wide * (s[1] + s[3] + s[5])
            + thin * (sxy + sxz + syz)
        )
        m1x = wide * d[1] + thin * ((d[7] + d[9]) + (d[11] + d[13]))
        m1y = wide * d[3] + thin * ((d[7] - d[9]) + (d[15] + d[17]))
        m1z = wide * d[5] + thin * ((d[11] - d[13]) + (d[15] - d[17]))
        mxx = wide * s[1] + thin * (sxy + sxz)
        myy = wide * s[3] + thin * (sxy + syz)
        mzz = wide * s[5] + thin * (sxz + syz)
        mxy = thin * (s[7] - s[9])
        mxz = thin * (s[11] - s[13])
        myz = thin * (s[15] - s[17])
        hx = mxx * ux + mxy * uy + mxz * uz
        hy = mxy * ux + myy * uy + myz * uz
        hz = mxz * ux + myz * uy + mzz * uz
        quad = ux * hx + uy * hy + uz * hz
        square = ux * ux + uy * uy + uz * uz
        bx = 3.0 * (m1x - ux * m0) + 9.0 * hx
        by = 3.0 * (m1y - uy * m0) + 9.0 * hy
        bz = 3.0 * (m1z - uz * m0) + 9.0 * hz
        bu = bx * ux + by * uy + bz * uz
        base = jnp.where(
            fluid, RELAX * (m0 + 1.5 * square * m0 - 4.5 * quad), -(bu * gain)
        )
        e = (bx * gain, by * gain, bz * gain)
        keep = jnp.where(fluid, 1.0 - RELAX, 0.0)
        back = [None] * 19
        back[0] = jnp.where(solid, g[0], keep * g[0] + base)
        for i in PAIRS:
            ce = along(i, e)
            back[i] = jnp.where(solid, g[i + 1], keep * g[i] + (base + ce))
            back[i + 1] = jnp.where(solid, g[i], keep * g[i + 1] + (base - ce))
        return back, slope * bu

    def reverse(values):
        return [values[OPPOSITE[i]] for i in range(19)]

    for copy in loads:
        copy.wait()
    waited = set()

    def block_one(x, h):
        if x not in waited:
            slabs[x].wait()
            waited.add(x)
        f = [pop[x, i, 8 * h : 8 * h + 8, :] for i in range(19)]
        return collide(0, f, x, h)

    stage(0, block_one)

    for offset, copy in drags.items():
        pl.when(exists(*offset))(copy.start)

    receive(0)
    zero = jnp.zeros((8, NZ), F32)
    packed = [zero] * HALVES
    for x in range(NX):
        for h in range(HALVES):
            values = collide(1, gather(0, x, h), x, h)
            scatter_open(x, h, values, packed)
    for h in range(HALVES):
        zpart[ROW + 8 * h : ROW + 8 * h + 8, :] = packed[h]

    def added_up(terms):
        out = [None] * 4
        for index, value in terms:
            for f, c in enumerate((1,) + VELOCITY[index]):
                if c:
                    if out[f] is None:
                        out[f] = value if c > 0 else -value
                    else:
                        out[f] = out[f] + value if c > 0 else out[f] - value
        return [zero if value is None else value for value in out]

    def reaches(h, cy):
        return 0 <= h < HALVES or (h < 0 and cy < 0) or (h >= HALVES and cy > 0)

    def own_part(x, h):
        terms = []
        for index in range(19):
            cx, cy, _ = VELOCITY[index]
            if 0 <= x - cx < NX and reaches(h, cy):
                slot = TWIN if index == 9 else SLOT[index]
                start = ROW + 8 * h - cy
                terms.append((index, pads[1, x + 1 - cx, slot, start : start + 8, :]))
        if len(terms) == 19:
            return moments([value for _, value in terms])
        return added_up(terms)

    BLOCKS = range(-1, HALVES + 1)
    tiles = [zero for _ in BLOCKS]

    def part_slab(x):
        for h in BLOCKS:
            rows = slice(ROW + 8 * h, ROW + 8 * h + 8)
            for f, value in enumerate(own_part(x, h)):
                part[f, x + 1, rows, :] = value
                column = 64 + 16 * f + 2 * (x + 1)
                tiles[h + 1] = jnp.where(
                    half == column // 2, pltpu.roll(value, column + 1, 1), tiles[h + 1]
                )

    for x in (-1, 0, 3, 4):
        part_slab(x)
    for (offset, kind), copy in parts.items():
        if kind == "cells" and offset[0]:
            pl.when(exists(*offset))(copy.start)
    for x in (1, 2):
        part_slab(x)
    for (offset, kind), copy in parts.items():
        if kind == "cells" and not offset[0]:
            pl.when(exists(*offset))(copy.start)

    for h in BLOCKS:
        terms = []
        for k, index in enumerate(ZPLUS):
            cx, cy, _ = VELOCITY[index]
            value = zero
            if reaches(h, cy):
                start = ROW + 8 * h - cy
                value = zpart[start : start + 8, :]
                shift = (2 * cx - 16 * k) % NZ
                value = pltpu.roll(value, shift, 1) if shift else value
            terms.append(value)
        weight = (terms[0] + (terms[1] + terms[2])) + (terms[3] + terms[4])
        sums = (weight, terms[1] - terms[2], terms[3] - terms[4], jnp.where(even, weight, -weight))
        for f, value in enumerate(sums):
            value = jnp.where(lane < 16, value, 0.0)
            tiles[h + 1] = tiles[h + 1] + (pltpu.roll(value, 16 * f, 1) if f else value)
        tile[ROW + 8 * h : ROW + 8 * h + 8, :] = tiles[h + 1]
    columns = [item for item in parts.items() if item[0][1] == "column"]
    for (offset, _), copy in sorted(columns, key=lambda item: -sum(map(abs, item[0][0]))):
        pl.when(exists(*offset))(copy.start)

    for (dx, dy, dz), copy in drags.items():
        pl.when(exists(-dx, -dy, -dz))(copy.wait_recv)
    for ((dx, dy, dz), _), copy in parts.items():
        pl.when(exists(-dx, -dy, -dz))(copy.wait_recv)

    def all_around(read, h, middle=None):
        rows = slice(ROW + 8 * h, ROW + 8 * h + 8)
        sums = []
        for a in range(3):
            terms = [middle if middle is not None and a == b == 1 else read(a, b, rows) for b in range(3)]
            sums.append((terms[0] + terms[1]) + terms[2])
        below, above = pltpu.roll(sums[0], NZ - 8, 1), pltpu.roll(sums[2], 8, 1)
        return sums[1] + jnp.where(
            place < 2, below, jnp.where((place == 4) | (place == 5), above, 0.0)
        )

    through = [[all_around(lambda a, b, r, s=s: from_z[s, a, b, r, :], h) for h in BLOCKS] for s in range(2)]
    inward = [jnp.where(even, low, pltpu.roll(high, NZ - 2, 1)) for low, high in zip(*through)]
    lost = []

    def gradient(solidity, seen, density, momentum):
        inverse = jnp.where(seen, 1.0 / jnp.where(seen, density, 1.0), 0.0)
        v = [m * inverse for m in momentum]
        square = v[0] * v[0] + v[1] * v[1] + v[2] * v[2]
        twice = 20.0 * solidity
        return square, -10.0 * solidity * square, [twice * a for a in v]

    for x in (0, 1, 2, 3, -1, 4):
        for h in BLOCKS:
            rows = slice(ROW + 8 * h, ROW + 8 * h + 8)
            total = []
            for f in range(4):
                value = part[f, x + 1, rows, :]
                if x < 1:
                    value = value + from_x[0, f, x + 1, rows, :]
                if x > 2:
                    value = value + from_x[1, f, x - 3, rows, :]
                side = 0 if h < 1 else 1
                near = slice(8 * (h + 1 - 2 * side), 8 * (h + 1 - 2 * side) + 8)
                value = value + from_y[side, f, x + 1, near, :]
                if x < 1:
                    value = value + from_xy[0, side, f, x + 1, near, :]
                if x > 2:
                    value = value + from_xy[1, side, f, x - 3, near, :]
                column = 16 * f + 2 * (x + 1)
                turned = pltpu.roll(inward[h + 1], NZ - column, 1) if column else inward[h + 1]
                value = value + jnp.where(ends, turned, 0.0)
                total.append(value)
            if 0 <= x < NX and 0 <= h < HALVES:
                own = slice(8 * h, 8 * h + 8)
                solidity, seen = design[x, own, :], labels[x, own, :] == 1
            else:
                solidity = drag[x + 1, rows, :]
                seen = solidity > 0.0
            square, base, e = gradient(solidity, seen, total[0], total[1:])
            if 0 <= x < NX and 0 <= h < HALVES:
                direct = 10.0 * total[0] * square
                raw[x, own, :] = direct
                lost.append(solidity * direct)
            for index in range(19):
                cx, cy, cz = VELOCITY[index]
                if not (0 <= x + cx < NX and (0 <= h < HALVES or (cy > 0 if h < 0 else cy < 0))):
                    continue
                value = base
                for c, a in zip((cx, cy, cz), e):
                    if c:
                        value = value - a if c > 0 else value + a
                if cz:
                    value = pltpu.roll(value, column_of(index, x, 2) + (cz > 0), 1)
                pads[2, x + 1, SLOT[index], rows, :] = value
                if index == 9:
                    pads[2, x + 1, TWIN, rows, :] = value

    for h in BLOCKS:
        rows = slice(ROW + 8 * h, ROW + 8 * h + 8)
        about = all_around(lambda a, b, r: from_plane[a, b, r, :], h, tile[rows, :])
        about = about + jnp.where(
            even,
            pltpu.roll(through[1][h + 1], NZ - 65, 1),
            pltpu.roll(through[0][h + 1], NZ - 63, 1),
        )
        total = [about] + [pltpu.roll(about, NZ - 16 * f, 1) for f in range(1, 4)]

        def drags_at(low, high, column):
            return jnp.where(
                even, pltpu.roll(high, NZ - column, 1), pltpu.roll(low, NZ + 1 - column, 1)
            )

        solidity = drags_at(zrecv[0, 0, rows, :], zrecv[0, 1, rows, :], 64)
        if 0 <= h < HALVES:
            own = slice(8 * h, 8 * h + 8)
            below = drags_at(zedge[0, 0, 0, own, :], zedge[0, 1, 0, own, :], 72)
            above = drags_at(zedge[0, 0, 1, own, :], zedge[0, 1, 1, own, :], 56)
            solidity = jnp.where(place == 0, below, jnp.where(place == 5, above, solidity))
        _, base, e = gradient(solidity, solidity > 0.0, total[0], total[1:])
        base = base + jnp.where(even, e[2], -e[2])
        out = None
        for k, index in enumerate(ZPLUS):
            value = base
            for c, a in zip(VELOCITY[index][:2], e):
                if c:
                    value = value - a if c > 0 else value + a
            out = value if k == 0 else jnp.where(lane >= 16 * k, pltpu.roll(value, 16 * k, 1), out)
        zrecv[2, 0, rows, :] = out

    def block_two(x, h):
        rows = slice(8 * h, 8 * h + 8)
        back, sens = transpose(1, reverse(gather(2, x, h)), x, h)
        raw[x, rows, :] = raw[x, rows, :] + sens
        return reverse(back)

    stage(3, block_two)

    receive(3)
    sizes_of = jnp.zeros((8, NZ), F32)
    for x in range(NX):
        for h in range(HALVES):
            rows = slice(8 * h, 8 * h + 8)
            _, sens = transpose(0, reverse(gather(3, x, h)), x, h)
            total = raw[x, rows, :] + sens
            raw[x, rows, :] = total
            sizes_of = sizes_of + jnp.abs(total)

    lost_of = lost[0]
    for term in lost[1:]:
        lost_of = lost_of + term
    row = lax.broadcasted_iota(jnp.int32, (8, NZ), 0)
    mine = jnp.where(
        row == 0,
        jnp.sum(lost_of, axis=0, keepdims=True),
        jnp.where(row == 1, jnp.sum(sizes_of, axis=0, keepdims=True), 0.0),
    )

    def spread(buffer, me, steps, base):
        buffer[me] = mine
        copies = []
        for number, step in enumerate(steps):
            copies.append(
                pltpu.make_async_remote_copy(
                    src_ref=buffer.at[me],
                    dst_ref=buffer.at[me],
                    send_sem=red_send.at[base + number],
                    recv_sem=red_recv.at[base + number],
                    device_id=device(*step),
                    device_id_type=MESH,
                )
            )
        for copy in copies:
            copy.start()
        return copies

    def added(buffer, copies):
        for copy in copies:
            copy.wait_recv()
        terms = [buffer[k] for k in range(len(copies) + 1)]
        while len(terms) > 1:
            terms = [a + b for a, b in zip(terms[::2], terms[1::2])]
        return terms[0]

    sent = spread(red_p, gx * nz + gz, plane, 0)
    stores = [pltpu.make_async_copy(raw, raw_hbm, store_sem.at[NX])]
    stores[0].start()
    for x in range(NX):
        for h in range(HALVES):
            rows = slice(8 * h, 8 * h + 8)
            back, _ = transpose(0, reverse(gather(3, x, h)), x, h)
            for i in range(19):
                adj[x, i, rows, :] = back[i]
        stores.append(pltpu.make_async_copy(adj.at[x], adj_hbm.at[:, x], store_sem.at[x]))
        stores[-1].start()
    for turn in exchanges:
        for (dx, dy, dz), copy in exchanges[turn].items():
            pl.when(exists(dx, dy, dz))(copy.wait_send)
    for offset, copy in drags.items():
        pl.when(exists(*offset))(copy.wait_send)
    for (offset, _), copy in parts.items():
        pl.when(exists(*offset))(copy.wait_send)
    mine = added(red_p, sent)
    last_sent = spread(red_y, gy, line, len(plane))
    mine = added(red_y, last_sent)
    sent = sent + last_sent

    cells = NX * NY * NZ * nx * ny * nz
    loss = jnp.sum(jnp.where(row == 0, mine, 0.0))
    size = jnp.sum(jnp.where(row == 1, mine, 0.0))
    sums_ref[0] = 20.0 * loss / cells
    sums_ref[1] = size / cells + 1e-06

    for copy in sent:
        copy.wait_send()
    for copy in stores:
        copy.wait()


def finish(sums_in, adj_in, raw_in, adj_out, sens_out, obj_out, raw, adj, sums, sem):
    cuts = [19 * k // PIECES for k in range(PIECES + 1)]
    loads = [
        pltpu.make_async_copy(sums_in, sums, sem.at[2 * PIECES]),
        pltpu.make_async_copy(raw_in, raw, sem.at[2 * PIECES + 1]),
    ]
    coming, going = [], []
    for k in range(PIECES):
        part = slice(cuts[k], cuts[k + 1])
        coming.append(pltpu.make_async_copy(adj_in.at[part], adj.at[part], sem.at[k]))
        going.append(
            pltpu.make_async_copy(adj.at[part], adj_out.at[part], sem.at[PIECES + k])
        )
        coming[k].start()
    for copy in loads:
        copy.start()
    for k in range(PIECES):
        coming[k].wait()
        going[k].start()
    for copy in loads:
        copy.wait()
    obj_out[0] = sums[0]
    inverse = 1.0 / jnp.full((8, NZ), sums[1], F32)
    for x in range(NX):
        for h in range(HALVES):
            rows = slice(8 * h, 8 * h + 8)
            raw[x, rows, :] = raw[x, rows, :] * inverse
    store = pltpu.make_async_copy(raw, sens_out, sem.at[2 * PIECES + 2])
    store.start()
    for k in range(PIECES):
        going[k].wait()
    store.wait()


def solution(mesh):
    nx, ny, nz = (mesh.shape[a] for a in ("gx", "gy", "gz"))
    partners = nx * nz + ny - 2

    def body(populations, design, labels):
        cells = (NX, NY, NZ)
        adjoint, raw, sums = pl.pallas_call(
            lambda *refs: kernel((nx, ny, nz), *refs),
            out_shape=(
                jax.ShapeDtypeStruct((19,) + cells, F32),
                jax.ShapeDtypeStruct(cells, F32),
                jax.ShapeDtypeStruct((2,), F32),
            ),
            in_specs=[pl.BlockSpec(memory_space=pltpu.HBM)] * 3,
            out_specs=(
                pl.BlockSpec(memory_space=pltpu.HBM),
                pl.BlockSpec(memory_space=pltpu.HBM),
                pl.BlockSpec(memory_space=pltpu.SMEM),
            ),
            scratch_shapes=[
                pltpu.VMEM((NX, 19, NY, NZ), F32),
                pltpu.VMEM(cells, F32),
                pltpu.VMEM(cells, jnp.int32),
                pltpu.VMEM((NX, 19, NY, NZ), F32),
                pltpu.VMEM((ROUNDS, NX + 2, 20, NY + 16, NZ), F32),
                pltpu.VMEM((ROUNDS, 2, NY, NZ), F32),
                pltpu.VMEM((ROUNDS, 2, NY + 16, NZ), F32),
                pltpu.VMEM((ROUNDS, 2, 2, NY, NZ), F32),
                pltpu.VMEM((2, 5) + cells, F32),
                pltpu.VMEM(cells, F32),
                pltpu.VMEM((4, NX + 2, NY + 16, NZ), F32),
                pltpu.VMEM((NY + 16, NZ), F32),
                pltpu.VMEM((NY + 16, NZ), F32),
                pltpu.VMEM((2, 4, 2, NY + 16, NZ), F32),
                pltpu.VMEM((2, 4, NX + 2, 16, NZ), F32),
                pltpu.VMEM((2, 2, 4, 2, 16, NZ), F32),
                pltpu.VMEM((3, 3, NY + 16, NZ), F32),
                pltpu.VMEM((2, 3, 3, NY + 16, NZ), F32),
                pltpu.VMEM((NX + 2, NY + 16, NZ), F32),
                pltpu.VMEM((nx * nz, 8, NZ), F32),
                pltpu.VMEM((ny, 8, NZ), F32),
                pltpu.SemaphoreType.DMA((6,)),
                pltpu.SemaphoreType.DMA((NX + 1,)),
                pltpu.SemaphoreType.DMA((ROUNDS, 18)),
                pltpu.SemaphoreType.DMA((ROUNDS, 18)),
                pltpu.SemaphoreType.DMA((34,)),
                pltpu.SemaphoreType.DMA((34,)),
                pltpu.SemaphoreType.DMA((8,)),
                pltpu.SemaphoreType.DMA((8,)),
                pltpu.SemaphoreType.DMA((partners,)),
                pltpu.SemaphoreType.DMA((partners,)),
            ],
            compiler_params=pltpu.CompilerParams(
                collective_id=0, has_side_effects=True, vmem_limit_bytes=60 * 1024 * 1024
            ),
            cost_estimate=pl.CostEstimate(
                flops=10_000_000, bytes_accessed=1_500_000, transcendentals=0
            ),
        )(populations, design, labels)
        adjoint, sensitivity, objective = pl.pallas_call(
            finish,
            out_shape=(
                jax.ShapeDtypeStruct((19,) + cells, F32),
                jax.ShapeDtypeStruct(cells, F32),
                jax.ShapeDtypeStruct((1,), F32),
            ),
            in_specs=[
                pl.BlockSpec(memory_space=pltpu.HBM),
                pl.BlockSpec(memory_space=pltpu.HBM),
                pl.BlockSpec(memory_space=pltpu.HBM),
            ],
            out_specs=(
                pl.BlockSpec(memory_space=pltpu.HBM),
                pl.BlockSpec(memory_space=pltpu.HBM),
                pl.BlockSpec(memory_space=pltpu.SMEM),
            ),
            scratch_shapes=[
                pltpu.VMEM(cells, F32),
                pltpu.VMEM((19,) + cells, F32),
                pltpu.SMEM((2,), F32),
                pltpu.SemaphoreType.DMA((2 * PIECES + 3,)),
            ],
            compiler_params=pltpu.CompilerParams(vmem_limit_bytes=60 * 1024 * 1024),
        )(sums, adjoint, raw)
        return adjoint, sensitivity, objective.reshape(())

    in_specs = (P(None, "gx", "gy", "gz"), P("gx", "gy", "gz"), P("gx", "gy", "gz"))
    out_specs = (P(None, "gx", "gy", "gz"), P("gx", "gy", "gz"), P())
    return jax.shard_map(body, mesh=mesh, in_specs=in_specs, out_specs=out_specs, check_vma=False)
```

```python
import jax
import jax.numpy as jnp
from jax import lax
from jax.experimental import pallas as pl
from jax.experimental.pallas import tpu as pltpu
from jax.sharding import PartitionSpec as P

VELOCITY = [
    (0, 0, 0),
    (1, 0, 0),
    (-1, 0, 0),
    (0, 1, 0),
    (0, -1, 0),
    (0, 0, 1),
    (0, 0, -1),
    (1, 1, 0),
    (-1, -1, 0),
    (1, -1, 0),
    (-1, 1, 0),
    (1, 0, 1),
    (-1, 0, -1),
    (1, 0, -1),
    (-1, 0, 1),
    (0, 1, 1),
    (0, -1, -1),
    (0, 1, -1),
    (0, -1, 1),
]
OPPOSITE = [0, 2, 1, 4, 3, 6, 5, 8, 7, 10, 9, 12, 11, 14, 13, 16, 15, 18, 17]
PAIRS = [1, 3, 5, 7, 9, 11, 13, 15, 17]
RELAX = 1.6
INFLOW = 0.05
MESH = pl.DeviceIdType.MESH
F32 = jnp.float32

ORDER = [9, 1, 11, 13, 7, 3, 15, 17, 10, 2, 12, 14, 8, 4, 16, 18, 9, 5, 6, 0]
SLOT = {index: ORDER.index(index) for index in range(19)}
TWIN = 16
ZPLUS = [5, 11, 14, 15, 18]
ZMINUS = [6, 13, 12, 17, 16]
ROW = 8

NX, NY, NZ = 4, 16, 128
HALVES = NY // 8
ROUNDS = 4
PIECES = 4


def neighbours():
    found = []
    for dx, dy, dz in VELOCITY[1:]:
        found.append((dx, dy, dz))
    return found


NEIGHBOURS = neighbours()


def kernel(
    sizes,
    pop_hbm,
    design_hbm,
    labels_hbm,
    adj_hbm,
    raw_hbm,
    sums_ref,
    pop,
    design,
    labels,
    adj,
    pads,
    zsend,
    zrecv,
    zedge,
    saved,
    raw,
    part,
    tile,
    zpart,
    from_x,
    from_y,
    from_xy,
    from_plane,
    from_z,
    drag,
    red_p,
    red_y,
    load_sem,
    store_sem,
    send_sem,
    recv_sem,
    part_send,
    part_recv,
    drag_send,
    drag_recv,
    red_send,
    red_recv,
):
    nx, ny, nz = sizes
    gx, gy, gz = lax.axis_index("gx"), lax.axis_index("gy"), lax.axis_index("gz")

    def device(dx, dy, dz):
        return {
            "gx": lax.rem(gx + (dx + nx), nx) if dx else gx,
            "gy": lax.rem(gy + (dy + ny), ny) if dy else gy,
            "gz": lax.rem(gz + (dz + nz), nz) if dz else gz,
        }

    inside = {
        "gx": (gx > 0, gx < nx - 1),
        "gy": (gy > 0, gy < ny - 1),
        "gz": (gz > 0, gz < nz - 1),
    }

    def exists(dx, dy, dz):
        found = None
        for axis, d in (("gx", dx), ("gy", dy), ("gz", dz)):
            if d:
                here = inside[axis][1 if d > 0 else 0]
                found = here if found is None else found & here
        return found

    loads = [
        pltpu.make_async_copy(design_hbm, design, load_sem.at[4]),
        pltpu.make_async_copy(labels_hbm, labels, load_sem.at[5]),
    ]
    slabs = {}
    for x in (0, 3, 1, 2):
        slabs[x] = pltpu.make_async_copy(pop_hbm.at[:, x], pop.at[x], load_sem.at[x])
    for copy in loads:
        copy.start()
    for x in (0, 3, 1, 2):
        slabs[x].start()

    @pl.when(gx == 0)
    def _():
        pads[:, 0, 0:5, 7:25, :] = jnp.zeros((ROUNDS, 5, 18, NZ), F32)
        zedge[:, :, 0] = jnp.zeros((ROUNDS, 2, NY, NZ), F32)

    @pl.when(gx == nx - 1)
    def _():
        pads[:, 5, 8:13, 7:25, :] = jnp.zeros((ROUNDS, 5, 18, NZ), F32)
        zedge[:, :, 1] = jnp.zeros((ROUNDS, 2, NY, NZ), F32)

    @pl.when(gy == 0)
    def _():
        pads[:, :, 4:9, 7:8, :] = jnp.zeros((ROUNDS, NX + 2, 5, 1, NZ), F32)
        zrecv[:, :, 7:8, :] = jnp.zeros((ROUNDS, 2, 1, NZ), F32)

    @pl.when(gy == ny - 1)
    def _():
        pads[:, :, 12:17, 24:25, :] = jnp.zeros((ROUNDS, NX + 2, 5, 1, NZ), F32)
        pads[:, 0, 0:1, 24:25, :] = jnp.zeros((ROUNDS, 1, 1, NZ), F32)
        zrecv[:, :, 24:25, :] = jnp.zeros((ROUNDS, 2, 1, NZ), F32)

    @pl.when(gz == 0)
    def _():
        zrecv[:, 0, 7:25, :] = jnp.zeros((ROUNDS, 18, NZ), F32)
        zedge[:, 0] = jnp.zeros((ROUNDS, 2, NY, NZ), F32)

    @pl.when(gz == nz - 1)
    def _():
        zrecv[:, 1, 7:25, :] = jnp.zeros((ROUNDS, 18, NZ), F32)
        zedge[:, 1] = jnp.zeros((ROUNDS, 2, NY, NZ), F32)

    from_y[...] = jnp.zeros(from_y.shape, F32)
    from_xy[...] = jnp.zeros(from_xy.shape, F32)
    from_plane[...] = jnp.zeros(from_plane.shape, F32)
    from_z[...] = jnp.zeros(from_z.shape, F32)
    drag[...] = jnp.zeros(drag.shape, F32)
    zpart[7:8, :] = jnp.zeros((1, NZ), F32)
    zpart[24:25, :] = jnp.zeros((1, NZ), F32)
    pads[1, 1:5, 4:9, 7:8, :] = jnp.zeros((NX, 5, 1, NZ), F32)
    pads[1, 1:5, 12:17, 24:25, :] = jnp.zeros((NX, 5, 1, NZ), F32)

    @pl.when(gx == 0)
    def _():
        from_x[0] = jnp.zeros((4, 2, NY + 16, NZ), F32)

    @pl.when(gx == nx - 1)
    def _():
        from_x[1] = jnp.zeros((4, 2, NY + 16, NZ), F32)

    barrier = pltpu.get_barrier_semaphore()
    plane = [(a, 0, b) for a in range(nx) for b in range(nz) if a or b]
    line = [(0, k, 0) for k in range(1, ny)]
    corners = [(a, b, c) for a in (1, -1) for b in (1, -1) for c in (1, -1)]
    partners = [n for n in NEIGHBOURS if n[1] and (n[0] or n[2])] + corners + plane + line
    for partner in partners:
        pl.semaphore_signal(barrier, inc=1, device_id=device(*partner), device_id_type=MESH)

    lane = lax.broadcasted_iota(jnp.int32, (8, NZ), 1)
    half = lane // 2
    place = half % 8
    even = lane % 2 == 0
    first, last = lane == 0, lane == NZ - 1
    ends = first | last

    def exchange(turn):
        pad, zs, zr, ze = pads.at[turn], zsend.at[turn], zrecv.at[turn], zedge.at[turn]
        copies = {}
        for number, (dx, dy, dz) in enumerate(NEIGHBOURS):
            if dz == 0:
                if dx > 0:
                    xs, xd, group = 4, 0, slice(0, 5)
                elif dx < 0:
                    xs, xd, group = 1, 5, slice(8, 13)
                else:
                    xs, xd, group = slice(1, 5), slice(1, 5), slice(4, 9) if dy > 0 else slice(12, 17)
                if dy > 0:
                    ys, yd = slice(23, 24), slice(7, 8)
                elif dy < 0:
                    ys, yd = slice(8, 9), slice(24, 25)
                else:
                    ys, yd = slice(8, 24), slice(8, 24)
                if dx and dy:
                    group = SLOT[VELOCITY.index((dx, dy, dz))]
                src, dst = pad.at[xs, group, ys], pad.at[xd, group, yd]
            else:
                s = 0 if dz > 0 else 1
                if dx:
                    src, dst = zs.at[s], ze.at[s, 0 if dx > 0 else 1]
                elif dy > 0:
                    src, dst = zs.at[s, 15:16], zr.at[s, 7:8]
                elif dy < 0:
                    src, dst = zs.at[s, 0:1], zr.at[s, 24:25]
                else:
                    src, dst = zs.at[s], zr.at[s, 8:24]
            copies[(dx, dy, dz)] = pltpu.make_async_remote_copy(
                src_ref=src,
                dst_ref=dst,
                send_sem=send_sem.at[turn, number],
                recv_sem=recv_sem.at[turn, number],
                device_id=device(dx, dy, dz),
                device_id_type=MESH,
            )
        return copies

    exchanges = {turn: exchange(turn) for turn in (0, 3)}

    def part_copies():
        copies = {}

        def copy(key, src, dst):
            number = len(copies)
            copies[key] = pltpu.make_async_remote_copy(
                src_ref=src,
                dst_ref=dst,
                send_sem=part_send.at[number],
                recv_sem=part_recv.at[number],
                device_id=device(*key[0]),
                device_id_type=MESH,
            )

        slabs_of = {1: slice(4, 6), -1: slice(0, 2), 0: slice(0, 6)}
        row_from = {1: slice(23, 25), -1: slice(7, 9), 0: slice(7, 25)}
        row_to = {1: slice(7, 9), -1: slice(23, 25), 0: slice(7, 25)}
        for dx in (1, -1, 0):
            for dy in (1, -1, 0):
                sx, sy = (1 - dx) // 2, (1 - dy) // 2
                if dx or dy:
                    src = part.at[:, slabs_of[dx], row_from[dy]]
                    if dx and dy:
                        dst = from_xy.at[sx, sy, :, :, 7:9]
                    elif dx:
                        dst = from_x.at[sx, :, :, 7:25]
                    else:
                        dst = from_y.at[sy, :, :, 7:9]
                    copy(((dx, dy, 0), "cells"), src, dst)
                    copy(
                        ((dx, dy, 0), "column"),
                        tile.at[row_from[dy]],
                        from_plane.at[1 - dx, 1 - dy, row_to[dy]],
                    )
                for s, dz in ((0, 1), (1, -1)):
                    copy(
                        ((dx, dy, dz), "column"),
                        tile.at[row_from[dy]],
                        from_z.at[s, 1 - dx, 1 - dy, row_to[dy]],
                    )
        return copies

    parts = part_copies()

    def drag_copies():
        copies = {}
        slab_from, slab_to = {1: 4, -1: 1, 0: slice(1, 5)}, {1: 0, -1: 5, 0: slice(1, 5)}
        row_from = {1: slice(23, 24), -1: slice(8, 9), 0: slice(8, 24)}
        row_to = {1: slice(7, 8), -1: slice(24, 25), 0: slice(8, 24)}
        for dx in (1, -1, 0):
            for dy in (1, -1, 0):
                if dx or dy:
                    number = len(copies)
                    copies[(dx, dy, 0)] = pltpu.make_async_remote_copy(
                        src_ref=drag.at[slab_from[dx], row_from[dy]],
                        dst_ref=drag.at[slab_to[dx], row_to[dy]],
                        send_sem=drag_send.at[number],
                        recv_sem=drag_recv.at[number],
                        device_id=device(dx, dy, 0),
                        device_id_type=MESH,
                    )
        return copies

    drags = drag_copies()

    def send_x(turn):
        for (dx, dy, dz), copy in exchanges[turn].items():
            if dx and not dz:
                pl.when(exists(dx, dy, dz))(copy.start)

    def send_rest(turn):
        rest = [item for item in exchanges[turn].items() if item[0][2] or not item[0][0]]
        for (dx, dy, dz), copy in sorted(rest, key=lambda item: not item[0][1]):
            pl.when(exists(dx, dy, dz))(copy.start)

    def receive(turn):
        for (dx, dy, dz), copy in exchanges[turn].items():
            pl.when(exists(-dx, -dy, -dz))(copy.wait_recv)

    def column_of(index, x, turn):
        up = VELOCITY[index][2] > 0
        k = (ZPLUS if up else ZMINUS).index(index)
        return 16 * k + 2 * (x + 1) + up if turn == 2 else 8 * k + 1 + x

    def gather(turn, x, h):
        values = []
        for index in range(19):
            cx, cy, cz = VELOCITY[index]
            slot = SLOT[index]
            if index == 9 and x > 0:
                slot = TWIN
            start = ROW + 8 * h - cy
            value = pads[turn, x + 1 - cx, slot, start : start + 8, :]
            if cz:
                s = 0 if cz > 0 else 1
                column = column_of(index, x - cx if turn == 2 else (x - cx) % NX, turn)
                if turn == 2:
                    halo = zrecv[2, 0, start : start + 8, :]
                elif 0 <= x - cx < NX:
                    halo = zrecv[turn, s, start : start + 8, :]
                else:
                    halo = zedge[turn, s, 0 if cx > 0 else 1, 8 * h : 8 * h + 8, :]
                value = jnp.where(lane == column, halo, value)
                value = pltpu.roll(value, NZ - column if cz > 0 else NZ - 1 - column, 1)
            values.append(value)
        return values

    def scatter(turn, x, h, values, packed):
        rows = slice(ROW + 8 * h, ROW + 8 * h + 8)
        for index in range(19):
            cz = VELOCITY[index][2]
            value = values[index]
            if cz:
                s = 0 if cz > 0 else 1
                column = column_of(index, x, turn)
                value = pltpu.roll(value, column + 1 if cz > 0 else column, 1)
                packed[s][h] = jnp.where(lane == column, value, packed[s][h])
            pads[turn, x + 1, SLOT[index], rows, :] = value
            if index == 9:
                pads[turn, x + 1, TWIN, rows, :] = value

    def scatter_open(x, h, values, packed):
        rows = slice(ROW + 8 * h, ROW + 8 * h + 8)
        for k in range(5):
            column = 16 * k + 2 * (x + 1)
            both = jnp.where(last, values[ZPLUS[k]], values[ZMINUS[k]])
            packed[h] = jnp.where(half == column // 2, pltpu.roll(both, column + 1, 1), packed[h])
        for index in range(19):
            cz = VELOCITY[index][2]
            value = values[index]
            if cz:
                value = pltpu.roll(value, 1 if cz > 0 else NZ - 1, 1)
                value = jnp.where(first if cz > 0 else last, 0.0, value)
            pads[1, x + 1, TWIN if index == 9 else SLOT[index], rows, :] = value

    def pack_drag(x, h, packed):
        rows = slice(8 * h, 8 * h + 8)
        value = jnp.where(labels[x, rows, :] == 1, design[x, rows, :], 0.0)
        drag[x + 1, ROW + 8 * h : ROW + 8 * h + 8, :] = value
        column = 64 + 2 * (x + 1)
        for s, shift in ((0, column + 1), (1, column)):
            packed[s][h] = jnp.where(lane == column, pltpu.roll(value, shift, 1), packed[s][h])

    def stage(turn, block):
        zero = jnp.zeros((8, NZ), F32)
        packed = [[zero] * HALVES, [zero] * HALVES]
        for x in (0, 3):
            for h in range(HALVES):
                scatter(turn, x, h, block(x, h), packed)
                if turn == 0:
                    pack_drag(x, h, packed)
        if turn == 0:
            pl.semaphore_wait(barrier, len(partners))
        send_x(turn)
        for x in (1, 2):
            for h in range(HALVES):
                scatter(turn, x, h, block(x, h), packed)
                if turn == 0:
                    pack_drag(x, h, packed)
        for s in range(2):
            for h in range(HALVES):
                zsend[turn, s, 8 * h : 8 * h + 8, :] = packed[s][h]
        send_rest(turn)

    def moments(f):
        sums = {i: f[i] + f[i + 1] for i in PAIRS}
        diff = {i: f[i] - f[i + 1] for i in PAIRS}
        density = f[0] + (
            ((sums[1] + sums[3]) + (sums[5] + sums[7]))
            + ((sums[9] + sums[11]) + (sums[13] + (sums[15] + sums[17])))
        )
        jx = diff[1] + ((diff[7] + diff[9]) + (diff[11] + diff[13]))
        jy = diff[3] + ((diff[7] - diff[9]) + (diff[15] + diff[17]))
        jz = diff[5] + ((diff[11] - diff[13]) + (diff[15] - diff[17]))
        return density, jx, jy, jz

    def along(index, v):
        total = None
        for axis in range(3):
            c = VELOCITY[index][axis]
            if c:
                if total is None:
                    total = v[axis]
                else:
                    total = total + v[axis] if c > 0 else total - v[axis]
        return total

    def collide(which, f, x, h):
        rows = slice(8 * h, 8 * h + 8)
        mark = labels[x, rows, :]
        fluid, solid, inlet, outlet = mark == 1, mark == 2, mark == 3, mark == 4
        damping = 1.0 / (1.0 + design[x, rows, :])
        density, jx, jy, jz = moments(f)
        inverse = 1.0 / jnp.where(solid, 1.0, density)
        factor = inverse * jnp.where(fluid, damping, jnp.where(outlet, 1.0, 0.0))
        ux, uy, uz = jx * factor, jy * factor, jnp.where(inlet, INFLOW, jz * factor)
        saved[which, 0, x, rows, :] = ux
        saved[which, 1, x, rows, :] = uy
        saved[which, 2, x, rows, :] = uz
        saved[which, 3, x, rows, :] = jnp.where(
            fluid, RELAX * damping, jnp.where(outlet, inverse, 0.0)
        )
        saved[which, 4, x, rows, :] = jnp.where(fluid, -RELAX * damping * density, 0.0)
        weight = jnp.where(fluid, RELAX * density, 1.0)
        keep = jnp.where(fluid, 1.0 - RELAX, 0.0)
        rest = 1.0 - 1.5 * (ux * ux + uy * uy + uz * uz)
        wide, thin = weight * (1.0 / 18.0), weight * (1.0 / 36.0)
        post = [None] * 19
        post[0] = jnp.where(solid, f[0], keep * f[0] + (weight * (1.0 / 3.0)) * rest)
        for i in PAIRS:
            w = wide if i < 7 else thin
            cu = along(i, (ux, uy, uz))
            even = w * (rest + 4.5 * (cu * cu))
            odd = w * (3.0 * cu)
            post[i] = jnp.where(solid, f[i + 1], keep * f[i] + (even + odd))
            post[i + 1] = jnp.where(solid, f[i], keep * f[i + 1] + (even - odd))
        return post

    def transpose(which, g, x, h):
        rows = slice(8 * h, 8 * h + 8)
        mark = labels[x, rows, :]
        fluid, solid = mark == 1, mark == 2
        u = [saved[which, a, x, rows, :] for a in range(3)]
        gain, slope = saved[which, 3, x, rows, :], saved[which, 4, x, rows, :]
        ux, uy, uz = u
        s = {i: g[i] + g[i + 1] for i in PAIRS}
        d = {i: g[i] - g[i + 1] for i in PAIRS}
        wide, thin = 1.0 / 18.0, 1.0 / 36.0
        sxy, sxz, syz = s[7] + s[9], s[11] + s[13], s[15] + s[17]
        m0 = (
            (1.0 / 3.0) * g[0]
            + wide * (s[1] + s[3] + s[5])
            + thin * (sxy + sxz + syz)
        )
        m1x = wide * d[1] + thin * ((d[7] + d[9]) + (d[11] + d[13]))
        m1y = wide * d[3] + thin * ((d[7] - d[9]) + (d[15] + d[17]))
        m1z = wide * d[5] + thin * ((d[11] - d[13]) + (d[15] - d[17]))
        mxx = wide * s[1] + thin * (sxy + sxz)
        myy = wide * s[3] + thin * (sxy + syz)
        mzz = wide * s[5] + thin * (sxz + syz)
        mxy = thin * (s[7] - s[9])
        mxz = thin * (s[11] - s[13])
        myz = thin * (s[15] - s[17])
        hx = mxx * ux + mxy * uy + mxz * uz
        hy = mxy * ux + myy * uy + myz * uz
        hz = mxz * ux + myz * uy + mzz * uz
        quad = ux * hx + uy * hy + uz * hz
        square = ux * ux + uy * uy + uz * uz
        bx = 3.0 * (m1x - ux * m0) + 9.0 * hx
        by = 3.0 * (m1y - uy * m0) + 9.0 * hy
        bz = 3.0 * (m1z - uz * m0) + 9.0 * hz
        bu = bx * ux + by * uy + bz * uz
        base = jnp.where(
            fluid, RELAX * (m0 + 1.5 * square * m0 - 4.5 * quad), -(bu * gain)
        )
        e = (bx * gain, by * gain, bz * gain)
        keep = jnp.where(fluid, 1.0 - RELAX, 0.0)
        back = [None] * 19
        back[0] = jnp.where(solid, g[0], keep * g[0] + base)
        for i in PAIRS:
            ce = along(i, e)
            back[i] = jnp.where(solid, g[i + 1], keep * g[i] + (base + ce))
            back[i + 1] = jnp.where(solid, g[i], keep * g[i + 1] + (base - ce))
        return back, slope * bu

    def reverse(values):
        return [values[OPPOSITE[i]] for i in range(19)]

    for copy in loads:
        copy.wait()
    waited = set()

    def block_one(x, h):
        if x not in waited:
            slabs[x].wait()
            waited.add(x)
        f = [pop[x, i, 8 * h : 8 * h + 8, :] for i in range(19)]
        return collide(0, f, x, h)

    stage(0, block_one)

    for offset, copy in drags.items():
        pl.when(exists(*offset))(copy.start)

    receive(0)
    zero = jnp.zeros((8, NZ), F32)
    packed = [zero] * HALVES
    for x in range(NX):
        for h in range(HALVES):
            values = collide(1, gather(0, x, h), x, h)
            scatter_open(x, h, values, packed)
    for h in range(HALVES):
        zpart[ROW + 8 * h : ROW + 8 * h + 8, :] = packed[h]

    def added_up(terms):
        out = [None] * 4
        for index, value in terms:
            for f, c in enumerate((1,) + VELOCITY[index]):
                if c:
                    if out[f] is None:
                        out[f] = value if c > 0 else -value
                    else:
                        out[f] = out[f] + value if c > 0 else out[f] - value
        return [zero if value is None else value for value in out]

    def reaches(h, cy):
        return 0 <= h < HALVES or (h < 0 and cy < 0) or (h >= HALVES and cy > 0)

    def own_part(x, h):
        terms = []
        for index in range(19):
            cx, cy, _ = VELOCITY[index]
            if 0 <= x - cx < NX and reaches(h, cy):
                slot = TWIN if index == 9 else SLOT[index]
                start = ROW + 8 * h - cy
                terms.append((index, pads[1, x + 1 - cx, slot, start : start + 8, :]))
        if len(terms) == 19:
            return moments([value for _, value in terms])
        return added_up(terms)

    BLOCKS = range(-1, HALVES + 1)
    tiles = [zero for _ in BLOCKS]

    def part_slab(x):
        for h in BLOCKS:
            rows = slice(ROW + 8 * h, ROW + 8 * h + 8)
            for f, value in enumerate(own_part(x, h)):
                part[f, x + 1, rows, :] = value
                column = 64 + 16 * f + 2 * (x + 1)
                tiles[h + 1] = jnp.where(
                    half == column // 2, pltpu.roll(value, column + 1, 1), tiles[h + 1]
                )

    for x in (-1, 0, 3, 4):
        part_slab(x)
    for (offset, kind), copy in parts.items():
        if kind == "cells" and offset[0]:
            pl.when(exists(*offset))(copy.start)
    for x in (1, 2):
        part_slab(x)
    for (offset, kind), copy in parts.items():
        if kind == "cells" and not offset[0]:
            pl.when(exists(*offset))(copy.start)

    for h in BLOCKS:
        terms = []
        for k, index in enumerate(ZPLUS):
            cx, cy, _ = VELOCITY[index]
            value = zero
            if reaches(h, cy):
                start = ROW + 8 * h - cy
                value = zpart[start : start + 8, :]
                shift = (2 * cx - 16 * k) % NZ
                value = pltpu.roll(value, shift, 1) if shift else value
            terms.append(value)
        weight = (terms[0] + (terms[1] + terms[2])) + (terms[3] + terms[4])
        sums = (weight, terms[1] - terms[2], terms[3] - terms[4], jnp.where(even, weight, -weight))
        for f, value in enumerate(sums):
            value = jnp.where(lane < 16, value, 0.0)
            tiles[h + 1] = tiles[h + 1] + (pltpu.roll(value, 16 * f, 1) if f else value)
        tile[ROW + 8 * h : ROW + 8 * h + 8, :] = tiles[h + 1]
    columns = [item for item in parts.items() if item[0][1] == "column"]
    for (offset, _), copy in sorted(columns, key=lambda item: -sum(map(abs, item[0][0]))):
        pl.when(exists(*offset))(copy.start)

    for (dx, dy, dz), copy in drags.items():
        pl.when(exists(-dx, -dy, -dz))(copy.wait_recv)
    for ((dx, dy, dz), _), copy in parts.items():
        pl.when(exists(-dx, -dy, -dz))(copy.wait_recv)

    def all_around(read, h, middle=None):
        rows = slice(ROW + 8 * h, ROW + 8 * h + 8)
        sums = []
        for a in range(3):
            terms = [middle if middle is not None and a == b == 1 else read(a, b, rows) for b in range(3)]
            sums.append((terms[0] + terms[1]) + terms[2])
        below, above = pltpu.roll(sums[0], NZ - 8, 1), pltpu.roll(sums[2], 8, 1)
        return sums[1] + jnp.where(
            place < 2, below, jnp.where((place == 4) | (place == 5), above, 0.0)
        )

    through = [[all_around(lambda a, b, r, s=s: from_z[s, a, b, r, :], h) for h in BLOCKS] for s in range(2)]
    inward = [jnp.where(even, low, pltpu.roll(high, NZ - 2, 1)) for low, high in zip(*through)]
    lost = []

    def gradient(solidity, seen, density, momentum):
        inverse = jnp.where(seen, 1.0 / jnp.where(seen, density, 1.0), 0.0)
        v = [m * inverse for m in momentum]
        square = v[0] * v[0] + v[1] * v[1] + v[2] * v[2]
        twice = 20.0 * solidity
        return square, -10.0 * solidity * square, [twice * a for a in v]

    for x in (0, 1, 2, 3, -1, 4):
        for h in BLOCKS:
            rows = slice(ROW + 8 * h, ROW + 8 * h + 8)
            total = []
            for f in range(4):
                value = part[f, x + 1, rows, :]
                if x < 1:
                    value = value + from_x[0, f, x + 1, rows, :]
                if x > 2:
                    value = value + from_x[1, f, x - 3, rows, :]
                side = 0 if h < 1 else 1
                near = slice(8 * (h + 1 - 2 * side), 8 * (h + 1 - 2 * side) + 8)
                value = value + from_y[side, f, x + 1, near, :]
                if x < 1:
                    value = value + from_xy[0, side, f, x + 1, near, :]
                if x > 2:
                    value = value + from_xy[1, side, f, x - 3, near, :]
                column = 16 * f + 2 * (x + 1)
                turned = pltpu.roll(inward[h + 1], NZ - column, 1) if column else inward[h + 1]
                value = value + jnp.where(ends, turned, 0.0)
                total.append(value)
            if 0 <= x < NX and 0 <= h < HALVES:
                own = slice(8 * h, 8 * h + 8)
                solidity, seen = design[x, own, :], labels[x, own, :] == 1
            else:
                solidity = drag[x + 1, rows, :]
                seen = solidity > 0.0
            square, base, e = gradient(solidity, seen, total[0], total[1:])
            if 0 <= x < NX and 0 <= h < HALVES:
                direct = 10.0 * total[0] * square
                raw[x, own, :] = direct
                lost.append(solidity * direct)
            for index in range(19):
                cx, cy, cz = VELOCITY[index]
                if not (0 <= x + cx < NX and (0 <= h < HALVES or (cy > 0 if h < 0 else cy < 0))):
                    continue
                value = base
                for c, a in zip((cx, cy, cz), e):
                    if c:
                        value = value - a if c > 0 else value + a
                if cz:
                    value = pltpu.roll(value, column_of(index, x, 2) + (cz > 0), 1)
                pads[2, x + 1, SLOT[index], rows, :] = value
                if index == 9:
                    pads[2, x + 1, TWIN, rows, :] = value

    for h in BLOCKS:
        rows = slice(ROW + 8 * h, ROW + 8 * h + 8)
        about = all_around(lambda a, b, r: from_plane[a, b, r, :], h, tile[rows, :])
        about = about + jnp.where(
            even,
            pltpu.roll(through[1][h + 1], NZ - 65, 1),
            pltpu.roll(through[0][h + 1], NZ - 63, 1),
        )
        total = [about] + [pltpu.roll(about, NZ - 16 * f, 1) for f in range(1, 4)]

        def drags_at(low, high, column):
            return jnp.where(
                even, pltpu.roll(high, NZ - column, 1), pltpu.roll(low, NZ + 1 - column, 1)
            )

        solidity = drags_at(zrecv[0, 0, rows, :], zrecv[0, 1, rows, :], 64)
        if 0 <= h < HALVES:
            own = slice(8 * h, 8 * h + 8)
            below = drags_at(zedge[0, 0, 0, own, :], zedge[0, 1, 0, own, :], 72)
            above = drags_at(zedge[0, 0, 1, own, :], zedge[0, 1, 1, own, :], 56)
            solidity = jnp.where(place == 0, below, jnp.where(place == 5, above, solidity))
        _, base, e = gradient(solidity, solidity > 0.0, total[0], total[1:])
        base = base + jnp.where(even, e[2], -e[2])
        out = None
        for k, index in enumerate(ZPLUS):
            value = base
            for c, a in zip(VELOCITY[index][:2], e):
                if c:
                    value = value - a if c > 0 else value + a
            out = value if k == 0 else jnp.where(lane >= 16 * k, pltpu.roll(value, 16 * k, 1), out)
        zrecv[2, 0, rows, :] = out

    def block_two(x, h):
        rows = slice(8 * h, 8 * h + 8)
        back, sens = transpose(1, reverse(gather(2, x, h)), x, h)
        raw[x, rows, :] = raw[x, rows, :] + sens
        return reverse(back)

    stage(3, block_two)

    receive(3)
    sizes_of = jnp.zeros((8, NZ), F32)
    for x in range(NX):
        for h in range(HALVES):
            rows = slice(8 * h, 8 * h + 8)
            _, sens = transpose(0, reverse(gather(3, x, h)), x, h)
            total = raw[x, rows, :] + sens
            raw[x, rows, :] = total
            sizes_of = sizes_of + jnp.abs(total)

    lost_of = lost[0]
    for term in lost[1:]:
        lost_of = lost_of + term
    left = lax.broadcasted_iota(jnp.int32, (1, NZ), 1) < NZ // 2

    def folded(value):
        value = value + pltpu.roll(value, NZ // 2, 1)
        return jnp.sum(value, axis=0, keepdims=True)

    mine = jnp.where(left, folded(lost_of), folded(sizes_of))

    def spread(buffer, me, steps, base):
        buffer[pl.ds(me, 1), :] = mine
        copies = []
        for number, step in enumerate(steps):
            copies.append(
                pltpu.make_async_remote_copy(
                    src_ref=buffer.at[pl.ds(me, 1)],
                    dst_ref=buffer.at[pl.ds(me, 1)],
                    send_sem=red_send.at[base + number],
                    recv_sem=red_recv.at[base + number],
                    device_id=device(*step),
                    device_id_type=MESH,
                )
            )
        for copy in copies:
            copy.start()
        return copies

    def added(buffer, copies):
        for copy in copies:
            copy.wait_recv()
        return jnp.sum(buffer[...], axis=0, keepdims=True)

    sent = spread(red_p, gx * nz + gz, plane, 0)
    stores = [pltpu.make_async_copy(raw, raw_hbm, store_sem.at[NX])]
    stores[0].start()
    for x in range(NX):
        for h in range(HALVES):
            rows = slice(8 * h, 8 * h + 8)
            back, _ = transpose(0, reverse(gather(3, x, h)), x, h)
            for i in range(19):
                adj[x, i, rows, :] = back[i]
        stores.append(pltpu.make_async_copy(adj.at[x], adj_hbm.at[:, x], store_sem.at[x]))
        stores[-1].start()
    for turn in exchanges:
        for (dx, dy, dz), copy in exchanges[turn].items():
            pl.when(exists(dx, dy, dz))(copy.wait_send)
    for offset, copy in drags.items():
        pl.when(exists(*offset))(copy.wait_send)
    for (offset, _), copy in parts.items():
        pl.when(exists(*offset))(copy.wait_send)
    mine = added(red_p, sent)
    last_sent = spread(red_y, gy, line, len(plane))
    mine = added(red_y, last_sent)
    sent = sent + last_sent

    cells = NX * NY * NZ * nx * ny * nz
    loss = jnp.sum(jnp.where(left, mine, 0.0))
    size = jnp.sum(jnp.where(left, 0.0, mine))
    sums_ref[0] = 20.0 * loss / cells
    sums_ref[1] = size / cells + 1e-06

    for copy in sent:
        copy.wait_send()
    for copy in stores:
        copy.wait()


def finish(sums_in, adj_in, raw_in, adj_out, sens_out, obj_out, raw, adj, sums, sem):
    cuts = [19 * k // PIECES for k in range(PIECES + 1)]
    loads = [
        pltpu.make_async_copy(sums_in, sums, sem.at[2 * PIECES]),
        pltpu.make_async_copy(raw_in, raw, sem.at[2 * PIECES + 1]),
    ]
    coming, going = [], []
    for k in range(PIECES):
        part = slice(cuts[k], cuts[k + 1])
        coming.append(pltpu.make_async_copy(adj_in.at[part], adj.at[part], sem.at[k]))
        going.append(
            pltpu.make_async_copy(adj.at[part], adj_out.at[part], sem.at[PIECES + k])
        )
        coming[k].start()
    for copy in loads:
        copy.start()
    for k in range(PIECES):
        coming[k].wait()
        going[k].start()
    for copy in loads:
        copy.wait()
    obj_out[0] = sums[0]
    inverse = 1.0 / jnp.full((8, NZ), sums[1], F32)
    for x in range(NX):
        for h in range(HALVES):
            rows = slice(8 * h, 8 * h + 8)
            raw[x, rows, :] = raw[x, rows, :] * inverse
    store = pltpu.make_async_copy(raw, sens_out, sem.at[2 * PIECES + 2])
    store.start()
    for k in range(PIECES):
        going[k].wait()
    store.wait()


def solution(mesh):
    nx, ny, nz = (mesh.shape[a] for a in ("gx", "gy", "gz"))
    partners = nx * nz + ny - 2

    def body(populations, design, labels):
        cells = (NX, NY, NZ)
        adjoint, raw, sums = pl.pallas_call(
            lambda *refs: kernel((nx, ny, nz), *refs),
            out_shape=(
                jax.ShapeDtypeStruct((19,) + cells, F32),
                jax.ShapeDtypeStruct(cells, F32),
                jax.ShapeDtypeStruct((2,), F32),
            ),
            in_specs=[pl.BlockSpec(memory_space=pltpu.HBM)] * 3,
            out_specs=(
                pl.BlockSpec(memory_space=pltpu.HBM),
                pl.BlockSpec(memory_space=pltpu.HBM),
                pl.BlockSpec(memory_space=pltpu.SMEM),
            ),
            scratch_shapes=[
                pltpu.VMEM((NX, 19, NY, NZ), F32),
                pltpu.VMEM(cells, F32),
                pltpu.VMEM(cells, jnp.int32),
                pltpu.VMEM((NX, 19, NY, NZ), F32),
                pltpu.VMEM((ROUNDS, NX + 2, 20, NY + 16, NZ), F32),
                pltpu.VMEM((ROUNDS, 2, NY, NZ), F32),
                pltpu.VMEM((ROUNDS, 2, NY + 16, NZ), F32),
                pltpu.VMEM((ROUNDS, 2, 2, NY, NZ), F32),
                pltpu.VMEM((2, 5) + cells, F32),
                pltpu.VMEM(cells, F32),
                pltpu.VMEM((4, NX + 2, NY + 16, NZ), F32),
                pltpu.VMEM((NY + 16, NZ), F32),
                pltpu.VMEM((NY + 16, NZ), F32),
                pltpu.VMEM((2, 4, 2, NY + 16, NZ), F32),
                pltpu.VMEM((2, 4, NX + 2, 16, NZ), F32),
                pltpu.VMEM((2, 2, 4, 2, 16, NZ), F32),
                pltpu.VMEM((3, 3, NY + 16, NZ), F32),
                pltpu.VMEM((2, 3, 3, NY + 16, NZ), F32),
                pltpu.VMEM((NX + 2, NY + 16, NZ), F32),
                pltpu.VMEM((nx * nz, NZ), F32),
                pltpu.VMEM((ny, NZ), F32),
                pltpu.SemaphoreType.DMA((6,)),
                pltpu.SemaphoreType.DMA((NX + 1,)),
                pltpu.SemaphoreType.DMA((ROUNDS, 18)),
                pltpu.SemaphoreType.DMA((ROUNDS, 18)),
                pltpu.SemaphoreType.DMA((34,)),
                pltpu.SemaphoreType.DMA((34,)),
                pltpu.SemaphoreType.DMA((8,)),
                pltpu.SemaphoreType.DMA((8,)),
                pltpu.SemaphoreType.DMA((partners,)),
                pltpu.SemaphoreType.DMA((partners,)),
            ],
            compiler_params=pltpu.CompilerParams(
                collective_id=0, has_side_effects=True, vmem_limit_bytes=60 * 1024 * 1024
            ),
            cost_estimate=pl.CostEstimate(
                flops=10_000_000, bytes_accessed=1_500_000, transcendentals=0
            ),
        )(populations, design, labels)
        adjoint, sensitivity, objective = pl.pallas_call(
            finish,
            out_shape=(
                jax.ShapeDtypeStruct((19,) + cells, F32),
                jax.ShapeDtypeStruct(cells, F32),
                jax.ShapeDtypeStruct((1,), F32),
            ),
            in_specs=[
                pl.BlockSpec(memory_space=pltpu.HBM),
                pl.BlockSpec(memory_space=pltpu.HBM),
                pl.BlockSpec(memory_space=pltpu.HBM),
            ],
            out_specs=(
                pl.BlockSpec(memory_space=pltpu.HBM),
                pl.BlockSpec(memory_space=pltpu.HBM),
                pl.BlockSpec(memory_space=pltpu.SMEM),
            ),
            scratch_shapes=[
                pltpu.VMEM(cells, F32),
                pltpu.VMEM((19,) + cells, F32),
                pltpu.SMEM((2,), F32),
                pltpu.SemaphoreType.DMA((2 * PIECES + 3,)),
            ],
            compiler_params=pltpu.CompilerParams(vmem_limit_bytes=60 * 1024 * 1024),
        )(sums, adjoint, raw)
        return adjoint, sensitivity, objective.reshape(())

    in_specs = (P(None, "gx", "gy", "gz"), P("gx", "gy", "gz"), P("gx", "gy", "gz"))
    out_specs = (P(None, "gx", "gy", "gz"), P("gx", "gy", "gz"), P())
    return jax.shard_map(body, mesh=mesh, in_specs=in_specs, out_specs=out_specs, check_vma=False)
```

```python
import jax
import jax.numpy as jnp
from jax import lax
from jax.experimental import pallas as pl
from jax.experimental.pallas import tpu as pltpu
from jax.sharding import PartitionSpec as P

VELOCITY = [
    (0, 0, 0),
    (1, 0, 0),
    (-1, 0, 0),
    (0, 1, 0),
    (0, -1, 0),
    (0, 0, 1),
    (0, 0, -1),
    (1, 1, 0),
    (-1, -1, 0),
    (1, -1, 0),
    (-1, 1, 0),
    (1, 0, 1),
    (-1, 0, -1),
    (1, 0, -1),
    (-1, 0, 1),
    (0, 1, 1),
    (0, -1, -1),
    (0, 1, -1),
    (0, -1, 1),
]
OPPOSITE = [0, 2, 1, 4, 3, 6, 5, 8, 7, 10, 9, 12, 11, 14, 13, 16, 15, 18, 17]
PAIRS = [1, 3, 5, 7, 9, 11, 13, 15, 17]
RELAX = 1.6
INFLOW = 0.05
MESH = pl.DeviceIdType.MESH
F32 = jnp.float32

ORDER = [9, 1, 11, 13, 7, 3, 15, 17, 10, 2, 12, 14, 8, 4, 16, 18, 9, 5, 6, 0]
SLOT = {index: ORDER.index(index) for index in range(19)}
TWIN = 16
ZPLUS = [5, 11, 14, 15, 18]
ZMINUS = [6, 13, 12, 17, 16]
ROW = 8

NX, NY, NZ = 4, 16, 128
HALVES = NY // 8
ROUNDS = 4
PIECES = 4


def neighbours():
    found = []
    for dx, dy, dz in VELOCITY[1:]:
        found.append((dx, dy, dz))
    return found


NEIGHBOURS = neighbours()


def kernel(
    sizes,
    pop_hbm,
    design_hbm,
    labels_hbm,
    adj_hbm,
    raw_hbm,
    sums_ref,
    pop,
    design,
    labels,
    adj,
    pads,
    zsend,
    zrecv,
    zedge,
    saved,
    raw,
    part,
    tile,
    zpart,
    from_x,
    from_y,
    from_xy,
    from_plane,
    from_z,
    drag,
    red_p,
    red_y,
    load_sem,
    store_sem,
    send_sem,
    recv_sem,
    part_send,
    part_recv,
    drag_send,
    drag_recv,
    red_send,
    red_recv,
):
    nx, ny, nz = sizes
    gx, gy, gz = lax.axis_index("gx"), lax.axis_index("gy"), lax.axis_index("gz")

    def device(dx, dy, dz):
        return {
            "gx": lax.rem(gx + (dx + nx), nx) if dx else gx,
            "gy": lax.rem(gy + (dy + ny), ny) if dy else gy,
            "gz": lax.rem(gz + (dz + nz), nz) if dz else gz,
        }

    inside = {
        "gx": (gx > 0, gx < nx - 1),
        "gy": (gy > 0, gy < ny - 1),
        "gz": (gz > 0, gz < nz - 1),
    }

    def exists(dx, dy, dz):
        found = None
        for axis, d in (("gx", dx), ("gy", dy), ("gz", dz)):
            if d:
                here = inside[axis][1 if d > 0 else 0]
                found = here if found is None else found & here
        return found

    loads = [
        pltpu.make_async_copy(design_hbm, design, load_sem.at[4]),
        pltpu.make_async_copy(labels_hbm, labels, load_sem.at[5]),
    ]
    slabs = {}
    for x in (0, 3, 1, 2):
        slabs[x] = pltpu.make_async_copy(pop_hbm.at[:, x], pop.at[x], load_sem.at[x])
    for copy in loads:
        copy.start()
    for x in (0, 3, 1, 2):
        slabs[x].start()

    @pl.when(gx == 0)
    def _():
        pads[:, 0, 0:5, 7:25, :] = jnp.zeros((ROUNDS, 5, 18, NZ), F32)
        zedge[:, :, 0] = jnp.zeros((ROUNDS, 2, NY, NZ), F32)

    @pl.when(gx == nx - 1)
    def _():
        pads[:, 5, 8:13, 7:25, :] = jnp.zeros((ROUNDS, 5, 18, NZ), F32)
        zedge[:, :, 1] = jnp.zeros((ROUNDS, 2, NY, NZ), F32)

    @pl.when(gy == 0)
    def _():
        pads[:, :, 4:9, 7:8, :] = jnp.zeros((ROUNDS, NX + 2, 5, 1, NZ), F32)
        zrecv[:, :, 7:8, :] = jnp.zeros((ROUNDS, 2, 1, NZ), F32)

    @pl.when(gy == ny - 1)
    def _():
        pads[:, :, 12:17, 24:25, :] = jnp.zeros((ROUNDS, NX + 2, 5, 1, NZ), F32)
        pads[:, 0, 0:1, 24:25, :] = jnp.zeros((ROUNDS, 1, 1, NZ), F32)
        zrecv[:, :, 24:25, :] = jnp.zeros((ROUNDS, 2, 1, NZ), F32)

    @pl.when(gz == 0)
    def _():
        zrecv[:, 0, 7:25, :] = jnp.zeros((ROUNDS, 18, NZ), F32)
        zedge[:, 0] = jnp.zeros((ROUNDS, 2, NY, NZ), F32)

    @pl.when(gz == nz - 1)
    def _():
        zrecv[:, 1, 7:25, :] = jnp.zeros((ROUNDS, 18, NZ), F32)
        zedge[:, 1] = jnp.zeros((ROUNDS, 2, NY, NZ), F32)

    from_y[...] = jnp.zeros(from_y.shape, F32)
    from_xy[...] = jnp.zeros(from_xy.shape, F32)
    from_plane[...] = jnp.zeros(from_plane.shape, F32)
    from_z[...] = jnp.zeros(from_z.shape, F32)
    drag[...] = jnp.zeros(drag.shape, F32)
    zpart[7:8, :] = jnp.zeros((1, NZ), F32)
    zpart[24:25, :] = jnp.zeros((1, NZ), F32)
    pads[1, 1:5, 4:9, 7:8, :] = jnp.zeros((NX, 5, 1, NZ), F32)
    pads[1, 1:5, 12:17, 24:25, :] = jnp.zeros((NX, 5, 1, NZ), F32)

    @pl.when(gx == 0)
    def _():
        from_x[0] = jnp.zeros((4, 2, NY + 16, NZ), F32)

    @pl.when(gx == nx - 1)
    def _():
        from_x[1] = jnp.zeros((4, 2, NY + 16, NZ), F32)

    barrier = pltpu.get_barrier_semaphore()
    core = lax.rem(gz, 2)
    twin = gz + 1 - 2 * core

    def far(step):
        return -sum(min(a, n - a) for a, n in zip(step, sizes))

    line = sorted([(0, k, 0) for k in range(1, ny)], key=far)
    plane = [(a, 0, b) for a in range(nx) for b in range(0, nz, 2) if a or b]
    plane = sorted(plane, key=far)
    pairs = [device(*step) for step in line]
    pairs = [there for step in pairs for there in (step, {**step, "gz": twin})]
    pairs.append({"gx": gx, "gy": gy, "gz": twin})
    corners = [(a, b, c) for a in (1, -1) for b in (1, -1) for c in (1, -1)]
    faces = [(1, 0, 0), (-1, 0, 0), (0, 1, 0), (0, -1, 0)]
    around = [n for n in NEIGHBOURS if n not in faces] + corners + plane
    partners = [device(*n) for n in around] + pairs
    for partner in partners:
        pl.semaphore_signal(barrier, inc=1, device_id=partner, device_id_type=MESH)

    lane = lax.broadcasted_iota(jnp.int32, (8, NZ), 1)
    half = lane // 2
    place = half % 8
    even = lane % 2 == 0
    first, last = lane == 0, lane == NZ - 1
    ends = first | last

    def exchange(turn):
        pad, zs, zr, ze = pads.at[turn], zsend.at[turn], zrecv.at[turn], zedge.at[turn]
        copies = {}
        for number, (dx, dy, dz) in enumerate(NEIGHBOURS):
            if dz == 0:
                if dx > 0:
                    xs, xd, group = 4, 0, slice(0, 5)
                elif dx < 0:
                    xs, xd, group = 1, 5, slice(8, 13)
                else:
                    xs, xd, group = slice(1, 5), slice(1, 5), slice(4, 9) if dy > 0 else slice(12, 17)
                if dy > 0:
                    ys, yd = slice(23, 24), slice(7, 8)
                elif dy < 0:
                    ys, yd = slice(8, 9), slice(24, 25)
                else:
                    ys, yd = slice(8, 24), slice(8, 24)
                if dx and dy:
                    group = SLOT[VELOCITY.index((dx, dy, dz))]
                src, dst = pad.at[xs, group, ys], pad.at[xd, group, yd]
            else:
                s = 0 if dz > 0 else 1
                if dx:
                    src, dst = zs.at[s], ze.at[s, 0 if dx > 0 else 1]
                elif dy > 0:
                    src, dst = zs.at[s, 15:16], zr.at[s, 7:8]
                elif dy < 0:
                    src, dst = zs.at[s, 0:1], zr.at[s, 24:25]
                else:
                    src, dst = zs.at[s], zr.at[s, 8:24]
            copies[(dx, dy, dz)] = pltpu.make_async_remote_copy(
                src_ref=src,
                dst_ref=dst,
                send_sem=send_sem.at[turn, number],
                recv_sem=recv_sem.at[turn, number],
                device_id=device(dx, dy, dz),
                device_id_type=MESH,
            )
        return copies

    exchanges = {turn: exchange(turn) for turn in (0, 3)}

    def part_copies():
        copies = {}

        def copy(key, src, dst):
            number = len(copies)
            copies[key] = pltpu.make_async_remote_copy(
                src_ref=src,
                dst_ref=dst,
                send_sem=part_send.at[number],
                recv_sem=part_recv.at[number],
                device_id=device(*key[0]),
                device_id_type=MESH,
            )

        slabs_of = {1: slice(4, 6), -1: slice(0, 2), 0: slice(0, 6)}
        row_from = {1: slice(23, 25), -1: slice(7, 9), 0: slice(7, 25)}
        row_to = {1: slice(7, 9), -1: slice(23, 25), 0: slice(7, 25)}
        for dx in (1, -1, 0):
            for dy in (1, -1, 0):
                sx, sy = (1 - dx) // 2, (1 - dy) // 2
                if dx or dy:
                    src = part.at[:, slabs_of[dx], row_from[dy]]
                    if dx and dy:
                        dst = from_xy.at[sx, sy, :, :, 7:9]
                    elif dx:
                        dst = from_x.at[sx, :, :, 7:25]
                    else:
                        dst = from_y.at[sy, :, :, 7:9]
                    copy(((dx, dy, 0), "cells"), src, dst)
                    copy(
                        ((dx, dy, 0), "column"),
                        tile.at[row_from[dy]],
                        from_plane.at[1 - dx, 1 - dy, row_to[dy]],
                    )
                for s, dz in ((0, 1), (1, -1)):
                    copy(
                        ((dx, dy, dz), "column"),
                        tile.at[row_from[dy]],
                        from_z.at[s, 1 - dx, 1 - dy, row_to[dy]],
                    )
        return copies

    parts = part_copies()

    def drag_copies():
        copies = {}
        slab_from, slab_to = {1: 4, -1: 1, 0: slice(1, 5)}, {1: 0, -1: 5, 0: slice(1, 5)}
        row_from = {1: slice(23, 24), -1: slice(8, 9), 0: slice(8, 24)}
        row_to = {1: slice(7, 8), -1: slice(24, 25), 0: slice(8, 24)}
        for dx in (1, -1, 0):
            for dy in (1, -1, 0):
                if dx or dy:
                    number = len(copies)
                    copies[(dx, dy, 0)] = pltpu.make_async_remote_copy(
                        src_ref=drag.at[slab_from[dx], row_from[dy]],
                        dst_ref=drag.at[slab_to[dx], row_to[dy]],
                        send_sem=drag_send.at[number],
                        recv_sem=drag_recv.at[number],
                        device_id=device(dx, dy, 0),
                        device_id_type=MESH,
                    )
        return copies

    drags = drag_copies()

    def send_x(turn):
        for (dx, dy, dz), copy in sorted(exchanges[turn].items(), key=lambda item: not item[0][1]):
            if dx and not dz:
                pl.when(exists(dx, dy, dz))(copy.start)

    def send_rest(turn):
        rest = [item for item in exchanges[turn].items() if item[0][2] or not item[0][0]]
        for (dx, dy, dz), copy in sorted(
            rest, key=lambda item: (not item[0][1], -sum(map(abs, item[0])))
        ):
            pl.when(exists(dx, dy, dz))(copy.start)

    def receive(turn):
        for (dx, dy, dz), copy in exchanges[turn].items():
            pl.when(exists(-dx, -dy, -dz))(copy.wait_recv)

    def column_of(index, x, turn):
        up = VELOCITY[index][2] > 0
        k = (ZPLUS if up else ZMINUS).index(index)
        return 16 * k + 2 * (x + 1) + up if turn == 2 else 8 * k + 1 + x

    def gather(turn, x, h):
        values = []
        for index in range(19):
            cx, cy, cz = VELOCITY[index]
            slot = SLOT[index]
            if index == 9 and x > 0:
                slot = TWIN
            start = ROW + 8 * h - cy
            value = pads[turn, x + 1 - cx, slot, start : start + 8, :]
            if cz:
                s = 0 if cz > 0 else 1
                column = column_of(index, x - cx if turn == 2 else (x - cx) % NX, turn)
                if turn == 2:
                    halo = zrecv[2, 0, start : start + 8, :]
                elif 0 <= x - cx < NX:
                    halo = zrecv[turn, s, start : start + 8, :]
                else:
                    halo = zedge[turn, s, 0 if cx > 0 else 1, 8 * h : 8 * h + 8, :]
                value = jnp.where(lane == column, halo, value)
                value = pltpu.roll(value, NZ - column if cz > 0 else NZ - 1 - column, 1)
            values.append(value)
        return values

    def scatter(turn, x, h, values, packed):
        rows = slice(ROW + 8 * h, ROW + 8 * h + 8)
        for index in range(19):
            cz = VELOCITY[index][2]
            value = values[index]
            if cz:
                s = 0 if cz > 0 else 1
                column = column_of(index, x, turn)
                value = pltpu.roll(value, column + 1 if cz > 0 else column, 1)
                packed[s][h] = jnp.where(lane == column, value, packed[s][h])
            pads[turn, x + 1, SLOT[index], rows, :] = value
            if index == 9:
                pads[turn, x + 1, TWIN, rows, :] = value

    def scatter_open(x, h, values, packed):
        rows = slice(ROW + 8 * h, ROW + 8 * h + 8)
        for k in range(5):
            column = 16 * k + 2 * (x + 1)
            both = jnp.where(last, values[ZPLUS[k]], values[ZMINUS[k]])
            packed[h] = jnp.where(half == column // 2, pltpu.roll(both, column + 1, 1), packed[h])
        for index in range(19):
            cz = VELOCITY[index][2]
            value = values[index]
            if cz:
                value = pltpu.roll(value, 1 if cz > 0 else NZ - 1, 1)
                value = jnp.where(first if cz > 0 else last, 0.0, value)
            pads[1, x + 1, TWIN if index == 9 else SLOT[index], rows, :] = value

    def pack_drag(x, h, packed):
        rows = slice(8 * h, 8 * h + 8)
        value = jnp.where(labels[x, rows, :] == 1, design[x, rows, :], 0.0)
        drag[x + 1, ROW + 8 * h : ROW + 8 * h + 8, :] = value
        column = 64 + 2 * (x + 1)
        for s, shift in ((0, column + 1), (1, column)):
            packed[s][h] = jnp.where(lane == column, pltpu.roll(value, shift, 1), packed[s][h])

    def stage(turn, block):
        zero = jnp.zeros((8, NZ), F32)
        packed = [[zero] * HALVES, [zero] * HALVES]
        for x in (0, 3):
            for h in range(HALVES):
                scatter(turn, x, h, block(x, h), packed)
                if turn == 0:
                    pack_drag(x, h, packed)
        if turn == 0:
            pl.semaphore_wait(barrier, len(partners))
        send_x(turn)
        for x in (1, 2):
            for h in range(HALVES):
                scatter(turn, x, h, block(x, h), packed)
                if turn == 0:
                    pack_drag(x, h, packed)
        for s in range(2):
            for h in range(HALVES):
                zsend[turn, s, 8 * h : 8 * h + 8, :] = packed[s][h]
        send_rest(turn)

    def moments(f):
        sums = {i: f[i] + f[i + 1] for i in PAIRS}
        diff = {i: f[i] - f[i + 1] for i in PAIRS}
        density = f[0] + (
            ((sums[1] + sums[3]) + (sums[5] + sums[7]))
            + ((sums[9] + sums[11]) + (sums[13] + (sums[15] + sums[17])))
        )
        jx = diff[1] + ((diff[7] + diff[9]) + (diff[11] + diff[13]))
        jy = diff[3] + ((diff[7] - diff[9]) + (diff[15] + diff[17]))
        jz = diff[5] + ((diff[11] - diff[13]) + (diff[15] - diff[17]))
        return density, jx, jy, jz

    def along(index, v):
        total = None
        for axis in range(3):
            c = VELOCITY[index][axis]
            if c:
                if total is None:
                    total = v[axis]
                else:
                    total = total + v[axis] if c > 0 else total - v[axis]
        return total

    def collide(which, f, x, h):
        rows = slice(8 * h, 8 * h + 8)
        mark = labels[x, rows, :]
        fluid, solid, inlet, outlet = mark == 1, mark == 2, mark == 3, mark == 4
        damping = 1.0 / (1.0 + design[x, rows, :])
        density, jx, jy, jz = moments(f)
        inverse = 1.0 / jnp.where(solid, 1.0, density)
        factor = inverse * jnp.where(fluid, damping, jnp.where(outlet, 1.0, 0.0))
        ux, uy, uz = jx * factor, jy * factor, jnp.where(inlet, INFLOW, jz * factor)
        saved[which, 0, x, rows, :] = ux
        saved[which, 1, x, rows, :] = uy
        saved[which, 2, x, rows, :] = uz
        saved[which, 3, x, rows, :] = jnp.where(
            fluid, RELAX * damping, jnp.where(outlet, inverse, 0.0)
        )
        saved[which, 4, x, rows, :] = jnp.where(fluid, -RELAX * damping * density, 0.0)
        weight = jnp.where(fluid, RELAX * density, 1.0)
        keep = jnp.where(fluid, 1.0 - RELAX, 0.0)
        rest = 1.0 - 1.5 * (ux * ux + uy * uy + uz * uz)
        wide, thin = weight * (1.0 / 18.0), weight * (1.0 / 36.0)
        post = [None] * 19
        post[0] = jnp.where(solid, f[0], keep * f[0] + (weight * (1.0 / 3.0)) * rest)
        for i in PAIRS:
            w = wide if i < 7 else thin
            cu = along(i, (ux, uy, uz))
            even = w * (rest + 4.5 * (cu * cu))
            odd = w * (3.0 * cu)
            post[i] = jnp.where(solid, f[i + 1], keep * f[i] + (even + odd))
            post[i + 1] = jnp.where(solid, f[i], keep * f[i + 1] + (even - odd))
        return post

    def transpose(which, g, x, h):
        rows = slice(8 * h, 8 * h + 8)
        mark = labels[x, rows, :]
        fluid, solid = mark == 1, mark == 2
        u = [saved[which, a, x, rows, :] for a in range(3)]
        gain, slope = saved[which, 3, x, rows, :], saved[which, 4, x, rows, :]
        ux, uy, uz = u
        s = {i: g[i] + g[i + 1] for i in PAIRS}
        d = {i: g[i] - g[i + 1] for i in PAIRS}
        wide, thin = 1.0 / 18.0, 1.0 / 36.0
        sxy, sxz, syz = s[7] + s[9], s[11] + s[13], s[15] + s[17]
        m0 = (
            (1.0 / 3.0) * g[0]
            + wide * (s[1] + s[3] + s[5])
            + thin * (sxy + sxz + syz)
        )
        m1x = wide * d[1] + thin * ((d[7] + d[9]) + (d[11] + d[13]))
        m1y = wide * d[3] + thin * ((d[7] - d[9]) + (d[15] + d[17]))
        m1z = wide * d[5] + thin * ((d[11] - d[13]) + (d[15] - d[17]))
        mxx = wide * s[1] + thin * (sxy + sxz)
        myy = wide * s[3] + thin * (sxy + syz)
        mzz = wide * s[5] + thin * (sxz + syz)
        mxy = thin * (s[7] - s[9])
        mxz = thin * (s[11] - s[13])
        myz = thin * (s[15] - s[17])
        hx = mxx * ux + mxy * uy + mxz * uz
        hy = mxy * ux + myy * uy + myz * uz
        hz = mxz * ux + myz * uy + mzz * uz
        quad = ux * hx + uy * hy + uz * hz
        square = ux * ux + uy * uy + uz * uz
        bx = 3.0 * (m1x - ux * m0) + 9.0 * hx
        by = 3.0 * (m1y - uy * m0) + 9.0 * hy
        bz = 3.0 * (m1z - uz * m0) + 9.0 * hz
        bu = bx * ux + by * uy + bz * uz
        base = jnp.where(
            fluid, RELAX * (m0 + 1.5 * square * m0 - 4.5 * quad), -(bu * gain)
        )
        e = (bx * gain, by * gain, bz * gain)
        keep = jnp.where(fluid, 1.0 - RELAX, 0.0)
        back = [None] * 19
        back[0] = jnp.where(solid, g[0], keep * g[0] + base)
        for i in PAIRS:
            ce = along(i, e)
            back[i] = jnp.where(solid, g[i + 1], keep * g[i] + (base + ce))
            back[i + 1] = jnp.where(solid, g[i], keep * g[i + 1] + (base - ce))
        return back, slope * bu

    def reverse(values):
        return [values[OPPOSITE[i]] for i in range(19)]

    for copy in loads:
        copy.wait()
    waited = set()

    def block_one(x, h):
        if x not in waited:
            slabs[x].wait()
            waited.add(x)
        f = [pop[x, i, 8 * h : 8 * h + 8, :] for i in range(19)]
        return collide(0, f, x, h)

    stage(0, block_one)

    for offset, copy in drags.items():
        pl.when(exists(*offset))(copy.start)

    receive(0)
    zero = jnp.zeros((8, NZ), F32)
    packed = [zero] * HALVES
    for x in range(NX):
        for h in range(HALVES):
            values = collide(1, gather(0, x, h), x, h)
            scatter_open(x, h, values, packed)
    for h in range(HALVES):
        zpart[ROW + 8 * h : ROW + 8 * h + 8, :] = packed[h]

    def added_up(terms):
        out = [None] * 4
        for index, value in terms:
            for f, c in enumerate((1,) + VELOCITY[index]):
                if c:
                    if out[f] is None:
                        out[f] = value if c > 0 else -value
                    else:
                        out[f] = out[f] + value if c > 0 else out[f] - value
        return [zero if value is None else value for value in out]

    def reaches(h, cy):
        return 0 <= h < HALVES or (h < 0 and cy < 0) or (h >= HALVES and cy > 0)

    def own_part(x, h):
        terms = []
        for index in range(19):
            cx, cy, _ = VELOCITY[index]
            if 0 <= x - cx < NX and reaches(h, cy):
                slot = TWIN if index == 9 else SLOT[index]
                start = ROW + 8 * h - cy
                terms.append((index, pads[1, x + 1 - cx, slot, start : start + 8, :]))
        if len(terms) == 19:
            return moments([value for _, value in terms])
        return added_up(terms)

    BLOCKS = range(-1, HALVES + 1)
    tiles = [zero for _ in BLOCKS]

    def part_slab(x):
        for h in BLOCKS:
            rows = slice(ROW + 8 * h, ROW + 8 * h + 8)
            for f, value in enumerate(own_part(x, h)):
                part[f, x + 1, rows, :] = value
                column = 64 + 16 * f + 2 * (x + 1)
                tiles[h + 1] = jnp.where(
                    half == column // 2, pltpu.roll(value, column + 1, 1), tiles[h + 1]
                )

    for x in (-1, 0, 3, 4):
        part_slab(x)
    for (offset, kind), copy in parts.items():
        if kind == "cells" and offset[0]:
            pl.when(exists(*offset))(copy.start)
    for x in (1, 2):
        part_slab(x)
    for (offset, kind), copy in parts.items():
        if kind == "cells" and not offset[0]:
            pl.when(exists(*offset))(copy.start)

    for h in BLOCKS:
        terms = []
        for k, index in enumerate(ZPLUS):
            cx, cy, _ = VELOCITY[index]
            value = zero
            if reaches(h, cy):
                start = ROW + 8 * h - cy
                value = zpart[start : start + 8, :]
                shift = (2 * cx - 16 * k) % NZ
                value = pltpu.roll(value, shift, 1) if shift else value
            terms.append(value)
        weight = (terms[0] + (terms[1] + terms[2])) + (terms[3] + terms[4])
        sums = (weight, terms[1] - terms[2], terms[3] - terms[4], jnp.where(even, weight, -weight))
        for f, value in enumerate(sums):
            value = jnp.where(lane < 16, value, 0.0)
            tiles[h + 1] = tiles[h + 1] + (pltpu.roll(value, 16 * f, 1) if f else value)
        tile[ROW + 8 * h : ROW + 8 * h + 8, :] = tiles[h + 1]
    columns = [item for item in parts.items() if item[0][1] == "column"]
    for (offset, _), copy in sorted(columns, key=lambda item: -sum(map(abs, item[0][0]))):
        pl.when(exists(*offset))(copy.start)

    for (dx, dy, dz), copy in drags.items():
        pl.when(exists(-dx, -dy, -dz))(copy.wait_recv)
    for ((dx, dy, dz), _), copy in parts.items():
        pl.when(exists(-dx, -dy, -dz))(copy.wait_recv)

    def all_around(read, h, middle=None):
        rows = slice(ROW + 8 * h, ROW + 8 * h + 8)
        sums = []
        for a in range(3):
            terms = [middle if middle is not None and a == b == 1 else read(a, b, rows) for b in range(3)]
            sums.append((terms[0] + terms[1]) + terms[2])
        below, above = pltpu.roll(sums[0], NZ - 8, 1), pltpu.roll(sums[2], 8, 1)
        return sums[1] + jnp.where(
            place < 2, below, jnp.where((place == 4) | (place == 5), above, 0.0)
        )

    through = [[all_around(lambda a, b, r, s=s: from_z[s, a, b, r, :], h) for h in BLOCKS] for s in range(2)]
    inward = [jnp.where(even, low, pltpu.roll(high, NZ - 2, 1)) for low, high in zip(*through)]
    lost = []

    def gradient(solidity, seen, density, momentum):
        inverse = jnp.where(seen, 1.0 / jnp.where(seen, density, 1.0), 0.0)
        v = [m * inverse for m in momentum]
        square = v[0] * v[0] + v[1] * v[1] + v[2] * v[2]
        twice = 20.0 * solidity
        return square, -10.0 * solidity * square, [twice * a for a in v]

    for x in (0, 1, 2, 3, -1, 4):
        for h in BLOCKS:
            rows = slice(ROW + 8 * h, ROW + 8 * h + 8)
            total = []
            for f in range(4):
                value = part[f, x + 1, rows, :]
                if x < 1:
                    value = value + from_x[0, f, x + 1, rows, :]
                if x > 2:
                    value = value + from_x[1, f, x - 3, rows, :]
                side = 0 if h < 1 else 1
                near = slice(8 * (h + 1 - 2 * side), 8 * (h + 1 - 2 * side) + 8)
                value = value + from_y[side, f, x + 1, near, :]
                if x < 1:
                    value = value + from_xy[0, side, f, x + 1, near, :]
                if x > 2:
                    value = value + from_xy[1, side, f, x - 3, near, :]
                column = 16 * f + 2 * (x + 1)
                turned = pltpu.roll(inward[h + 1], NZ - column, 1) if column else inward[h + 1]
                value = value + jnp.where(ends, turned, 0.0)
                total.append(value)
            if 0 <= x < NX and 0 <= h < HALVES:
                own = slice(8 * h, 8 * h + 8)
                solidity, seen = design[x, own, :], labels[x, own, :] == 1
            else:
                solidity = drag[x + 1, rows, :]
                seen = solidity > 0.0
            square, base, e = gradient(solidity, seen, total[0], total[1:])
            if 0 <= x < NX and 0 <= h < HALVES:
                direct = 10.0 * total[0] * square
                raw[x, own, :] = direct
                lost.append(solidity * direct)
            for index in range(19):
                cx, cy, cz = VELOCITY[index]
                if not (0 <= x + cx < NX and (0 <= h < HALVES or (cy > 0 if h < 0 else cy < 0))):
                    continue
                value = base
                for c, a in zip((cx, cy, cz), e):
                    if c:
                        value = value - a if c > 0 else value + a
                if cz:
                    value = pltpu.roll(value, column_of(index, x, 2) + (cz > 0), 1)
                pads[2, x + 1, SLOT[index], rows, :] = value
                if index == 9:
                    pads[2, x + 1, TWIN, rows, :] = value

    for h in BLOCKS:
        rows = slice(ROW + 8 * h, ROW + 8 * h + 8)
        about = all_around(lambda a, b, r: from_plane[a, b, r, :], h, tile[rows, :])
        about = about + jnp.where(
            even,
            pltpu.roll(through[1][h + 1], NZ - 65, 1),
            pltpu.roll(through[0][h + 1], NZ - 63, 1),
        )
        total = [about] + [pltpu.roll(about, NZ - 16 * f, 1) for f in range(1, 4)]

        def drags_at(low, high, column):
            return jnp.where(
                even, pltpu.roll(high, NZ - column, 1), pltpu.roll(low, NZ + 1 - column, 1)
            )

        solidity = drags_at(zrecv[0, 0, rows, :], zrecv[0, 1, rows, :], 64)
        if 0 <= h < HALVES:
            own = slice(8 * h, 8 * h + 8)
            below = drags_at(zedge[0, 0, 0, own, :], zedge[0, 1, 0, own, :], 72)
            above = drags_at(zedge[0, 0, 1, own, :], zedge[0, 1, 1, own, :], 56)
            solidity = jnp.where(place == 0, below, jnp.where(place == 5, above, solidity))
        _, base, e = gradient(solidity, solidity > 0.0, total[0], total[1:])
        base = base + jnp.where(even, e[2], -e[2])
        out = None
        for k, index in enumerate(ZPLUS):
            value = base
            for c, a in zip(VELOCITY[index][:2], e):
                if c:
                    value = value - a if c > 0 else value + a
            out = value if k == 0 else jnp.where(lane >= 16 * k, pltpu.roll(value, 16 * k, 1), out)
        zrecv[2, 0, rows, :] = out

    def block_two(x, h):
        rows = slice(8 * h, 8 * h + 8)
        back, sens = transpose(1, reverse(gather(2, x, h)), x, h)
        raw[x, rows, :] = raw[x, rows, :] + sens
        return reverse(back)

    stage(3, block_two)

    receive(3)
    sizes_of = jnp.zeros((8, NZ), F32)
    for x in range(NX):
        for h in range(HALVES):
            rows = slice(8 * h, 8 * h + 8)
            _, sens = transpose(0, reverse(gather(3, x, h)), x, h)
            total = raw[x, rows, :] + sens
            raw[x, rows, :] = total
            sizes_of = sizes_of + jnp.abs(total)

    lost_of = lost[0]
    for term in lost[1:]:
        lost_of = lost_of + term
    left = lax.broadcasted_iota(jnp.int32, (1, NZ), 1) < NZ // 2

    def folded(value):
        value = value + pltpu.roll(value, NZ // 2, 1)
        return jnp.sum(value, axis=0, keepdims=True)

    mine = jnp.where(left, folded(lost_of), folded(sizes_of))

    def spread(buffer, me, targets, base):
        buffer[pl.ds(me, 1), :] = mine
        copies = []
        for number, target in enumerate(targets):
            copies.append(
                pltpu.make_async_remote_copy(
                    src_ref=buffer.at[pl.ds(me, 1)],
                    dst_ref=buffer.at[pl.ds(me, 1)],
                    send_sem=red_send.at[base + number],
                    recv_sem=red_recv.at[base + number],
                    device_id=target,
                    device_id_type=MESH,
                )
            )
        for copy in copies:
            copy.start()
        return copies

    def added(buffer, copies):
        for copy in copies:
            copy.wait_recv()
        return jnp.sum(buffer[...], axis=0, keepdims=True)

    sent = spread(red_y, gy * 2 + core, pairs, 0)
    stores = [pltpu.make_async_copy(raw, raw_hbm, store_sem.at[NX])]
    stores[0].start()
    for x in range(NX):
        for h in range(HALVES):
            rows = slice(8 * h, 8 * h + 8)
            back, _ = transpose(0, reverse(gather(3, x, h)), x, h)
            for i in range(19):
                adj[x, i, rows, :] = back[i]
        stores.append(pltpu.make_async_copy(adj.at[x], adj_hbm.at[:, x], store_sem.at[x]))
        stores[-1].start()
    for turn in exchanges:
        for (dx, dy, dz), copy in exchanges[turn].items():
            pl.when(exists(dx, dy, dz))(copy.wait_send)
    for offset, copy in drags.items():
        pl.when(exists(*offset))(copy.wait_send)
    for (offset, _), copy in parts.items():
        pl.when(exists(*offset))(copy.wait_send)
    mine = added(red_y, sent)
    last_sent = spread(red_p, gx * (nz // 2) + gz // 2, [device(*step) for step in plane], len(pairs))
    mine = added(red_p, last_sent)
    sent = sent + last_sent

    cells = NX * NY * NZ * nx * ny * nz
    loss = jnp.sum(jnp.where(left, mine, 0.0))
    size = jnp.sum(jnp.where(left, 0.0, mine))
    sums_ref[0] = 20.0 * loss / cells
    sums_ref[1] = size / cells + 1e-06

    for copy in sent:
        copy.wait_send()
    for copy in stores:
        copy.wait()


def finish(sums_in, adj_in, raw_in, adj_out, sens_out, obj_out, raw, adj, sums, sem):
    cuts = [19 * k // PIECES for k in range(PIECES + 1)]
    loads = [
        pltpu.make_async_copy(sums_in, sums, sem.at[2 * PIECES]),
        pltpu.make_async_copy(raw_in, raw, sem.at[2 * PIECES + 1]),
    ]
    coming, going = [], []
    for k in range(PIECES):
        part = slice(cuts[k], cuts[k + 1])
        coming.append(pltpu.make_async_copy(adj_in.at[part], adj.at[part], sem.at[k]))
        going.append(
            pltpu.make_async_copy(adj.at[part], adj_out.at[part], sem.at[PIECES + k])
        )
        coming[k].start()
    for copy in loads:
        copy.start()
    for k in range(PIECES):
        coming[k].wait()
        going[k].start()
    for copy in loads:
        copy.wait()
    obj_out[0] = sums[0]
    inverse = 1.0 / jnp.full((8, NZ), sums[1], F32)
    for x in range(NX):
        for h in range(HALVES):
            rows = slice(8 * h, 8 * h + 8)
            raw[x, rows, :] = raw[x, rows, :] * inverse
    store = pltpu.make_async_copy(raw, sens_out, sem.at[2 * PIECES + 2])
    store.start()
    for k in range(PIECES):
        going[k].wait()
    store.wait()


def solution(mesh):
    nx, ny, nz = (mesh.shape[a] for a in ("gx", "gy", "gz"))
    partners = nx * nz // 2 + 2 * ny - 2

    def body(populations, design, labels):
        cells = (NX, NY, NZ)
        adjoint, raw, sums = pl.pallas_call(
            lambda *refs: kernel((nx, ny, nz), *refs),
            out_shape=(
                jax.ShapeDtypeStruct((19,) + cells, F32),
                jax.ShapeDtypeStruct(cells, F32),
                jax.ShapeDtypeStruct((2,), F32),
            ),
            in_specs=[pl.BlockSpec(memory_space=pltpu.HBM)] * 3,
            out_specs=(
                pl.BlockSpec(memory_space=pltpu.HBM),
                pl.BlockSpec(memory_space=pltpu.HBM),
                pl.BlockSpec(memory_space=pltpu.SMEM),
            ),
            scratch_shapes=[
                pltpu.VMEM((NX, 19, NY, NZ), F32),
                pltpu.VMEM(cells, F32),
                pltpu.VMEM(cells, jnp.int32),
                pltpu.VMEM((NX, 19, NY, NZ), F32),
                pltpu.VMEM((ROUNDS, NX + 2, 20, NY + 16, NZ), F32),
                pltpu.VMEM((ROUNDS, 2, NY, NZ), F32),
                pltpu.VMEM((ROUNDS, 2, NY + 16, NZ), F32),
                pltpu.VMEM((ROUNDS, 2, 2, NY, NZ), F32),
                pltpu.VMEM((2, 5) + cells, F32),
                pltpu.VMEM(cells, F32),
                pltpu.VMEM((4, NX + 2, NY + 16, NZ), F32),
                pltpu.VMEM((NY + 16, NZ), F32),
                pltpu.VMEM((NY + 16, NZ), F32),
                pltpu.VMEM((2, 4, 2, NY + 16, NZ), F32),
                pltpu.VMEM((2, 4, NX + 2, 16, NZ), F32),
                pltpu.VMEM((2, 2, 4, 2, 16, NZ), F32),
                pltpu.VMEM((3, 3, NY + 16, NZ), F32),
                pltpu.VMEM((2, 3, 3, NY + 16, NZ), F32),
                pltpu.VMEM((NX + 2, NY + 16, NZ), F32),
                pltpu.VMEM((nx * nz // 2, NZ), F32),
                pltpu.VMEM((2 * ny, NZ), F32),
                pltpu.SemaphoreType.DMA((6,)),
                pltpu.SemaphoreType.DMA((NX + 1,)),
                pltpu.SemaphoreType.DMA((ROUNDS, 18)),
                pltpu.SemaphoreType.DMA((ROUNDS, 18)),
                pltpu.SemaphoreType.DMA((34,)),
                pltpu.SemaphoreType.DMA((34,)),
                pltpu.SemaphoreType.DMA((8,)),
                pltpu.SemaphoreType.DMA((8,)),
                pltpu.SemaphoreType.DMA((partners,)),
                pltpu.SemaphoreType.DMA((partners,)),
            ],
            compiler_params=pltpu.CompilerParams(
                collective_id=0, has_side_effects=True, vmem_limit_bytes=60 * 1024 * 1024
            ),
            cost_estimate=pl.CostEstimate(
                flops=10_000_000, bytes_accessed=1_500_000, transcendentals=0
            ),
        )(populations, design, labels)
        adjoint, sensitivity, objective = pl.pallas_call(
            finish,
            out_shape=(
                jax.ShapeDtypeStruct((19,) + cells, F32),
                jax.ShapeDtypeStruct(cells, F32),
                jax.ShapeDtypeStruct((1,), F32),
            ),
            in_specs=[
                pl.BlockSpec(memory_space=pltpu.HBM),
                pl.BlockSpec(memory_space=pltpu.HBM),
                pl.BlockSpec(memory_space=pltpu.HBM),
            ],
            out_specs=(
                pl.BlockSpec(memory_space=pltpu.HBM),
                pl.BlockSpec(memory_space=pltpu.HBM),
                pl.BlockSpec(memory_space=pltpu.SMEM),
            ),
            scratch_shapes=[
                pltpu.VMEM(cells, F32),
                pltpu.VMEM((19,) + cells, F32),
                pltpu.SMEM((2,), F32),
                pltpu.SemaphoreType.DMA((2 * PIECES + 3,)),
            ],
            compiler_params=pltpu.CompilerParams(vmem_limit_bytes=60 * 1024 * 1024),
        )(sums, adjoint, raw)
        return adjoint, sensitivity, objective.reshape(())

    in_specs = (P(None, "gx", "gy", "gz"), P("gx", "gy", "gz"), P("gx", "gy", "gz"))
    out_specs = (P(None, "gx", "gy", "gz"), P("gx", "gy", "gz"), P())
    return jax.shard_map(body, mesh=mesh, in_specs=in_specs, out_specs=out_specs, check_vma=False)
```

```python
import jax
import jax.numpy as jnp
from jax import lax
from jax.experimental import pallas as pl
from jax.experimental.pallas import tpu as pltpu
from jax.sharding import PartitionSpec as P

VELOCITY = [
    (0, 0, 0),
    (1, 0, 0),
    (-1, 0, 0),
    (0, 1, 0),
    (0, -1, 0),
    (0, 0, 1),
    (0, 0, -1),
    (1, 1, 0),
    (-1, -1, 0),
    (1, -1, 0),
    (-1, 1, 0),
    (1, 0, 1),
    (-1, 0, -1),
    (1, 0, -1),
    (-1, 0, 1),
    (0, 1, 1),
    (0, -1, -1),
    (0, 1, -1),
    (0, -1, 1),
]
OPPOSITE = [0, 2, 1, 4, 3, 6, 5, 8, 7, 10, 9, 12, 11, 14, 13, 16, 15, 18, 17]
PAIRS = [1, 3, 5, 7, 9, 11, 13, 15, 17]
RELAX = 1.6
INFLOW = 0.05
MESH = pl.DeviceIdType.MESH
F32 = jnp.float32

ORDER = [9, 1, 11, 13, 7, 3, 15, 17, 10, 2, 12, 14, 8, 4, 16, 18, 9, 5, 6, 0]
SLOT = {index: ORDER.index(index) for index in range(19)}
TWIN = 16
ZPLUS = [5, 11, 14, 15, 18]
ZMINUS = [6, 13, 12, 17, 16]
ROW = 8

NX, NY, NZ = 4, 16, 128
HALVES = NY // 8
ROUNDS = 4
PIECES = 4


def neighbours():
    found = []
    for dx, dy, dz in VELOCITY[1:]:
        found.append((dx, dy, dz))
    return found


NEIGHBOURS = neighbours()


def kernel(
    sizes,
    pop_hbm,
    design_hbm,
    labels_hbm,
    adj_hbm,
    raw_hbm,
    sums_ref,
    pop,
    design,
    labels,
    adj,
    pads,
    zsend,
    zrecv,
    zedge,
    saved,
    raw,
    part,
    tile,
    zpart,
    from_x,
    from_y,
    from_xy,
    from_plane,
    from_z,
    drag,
    red_p,
    red_y,
    load_sem,
    store_sem,
    send_sem,
    recv_sem,
    part_send,
    part_recv,
    drag_send,
    drag_recv,
    red_send,
    red_recv,
):
    nx, ny, nz = sizes
    gx, gy, gz = lax.axis_index("gx"), lax.axis_index("gy"), lax.axis_index("gz")

    def device(dx, dy, dz):
        return {
            "gx": lax.rem(gx + (dx + nx), nx) if dx else gx,
            "gy": lax.rem(gy + (dy + ny), ny) if dy else gy,
            "gz": lax.rem(gz + (dz + nz), nz) if dz else gz,
        }

    inside = {
        "gx": (gx > 0, gx < nx - 1),
        "gy": (gy > 0, gy < ny - 1),
        "gz": (gz > 0, gz < nz - 1),
    }

    def exists(dx, dy, dz):
        found = None
        for axis, d in (("gx", dx), ("gy", dy), ("gz", dz)):
            if d:
                here = inside[axis][1 if d > 0 else 0]
                found = here if found is None else found & here
        return found

    loads = [
        pltpu.make_async_copy(design_hbm, design, load_sem.at[4]),
        pltpu.make_async_copy(labels_hbm, labels, load_sem.at[5]),
    ]
    slabs = {}
    for x in (0, 3, 1, 2):
        slabs[x] = pltpu.make_async_copy(pop_hbm.at[:, x], pop.at[x], load_sem.at[x])
    for copy in loads:
        copy.start()
    for x in (0, 3, 1, 2):
        slabs[x].start()

    @pl.when(gx == 0)
    def _():
        pads[:, 0, 0:5, 7:25, :] = jnp.zeros((ROUNDS, 5, 18, NZ), F32)
        zedge[:, :, 0] = jnp.zeros((ROUNDS, 2, NY, NZ), F32)

    @pl.when(gx == nx - 1)
    def _():
        pads[:, 5, 8:13, 7:25, :] = jnp.zeros((ROUNDS, 5, 18, NZ), F32)
        zedge[:, :, 1] = jnp.zeros((ROUNDS, 2, NY, NZ), F32)

    @pl.when(gy == 0)
    def _():
        pads[:, :, 4:9, 7:8, :] = jnp.zeros((ROUNDS, NX + 2, 5, 1, NZ), F32)
        zrecv[:, :, 7:8, :] = jnp.zeros((ROUNDS, 2, 1, NZ), F32)

    @pl.when(gy == ny - 1)
    def _():
        pads[:, :, 12:17, 24:25, :] = jnp.zeros((ROUNDS, NX + 2, 5, 1, NZ), F32)
        pads[:, 0, 0:1, 24:25, :] = jnp.zeros((ROUNDS, 1, 1, NZ), F32)
        zrecv[:, :, 24:25, :] = jnp.zeros((ROUNDS, 2, 1, NZ), F32)

    @pl.when(gz == 0)
    def _():
        zrecv[:, 0, 7:25, :] = jnp.zeros((ROUNDS, 18, NZ), F32)
        zedge[:, 0] = jnp.zeros((ROUNDS, 2, NY, NZ), F32)

    @pl.when(gz == nz - 1)
    def _():
        zrecv[:, 1, 7:25, :] = jnp.zeros((ROUNDS, 18, NZ), F32)
        zedge[:, 1] = jnp.zeros((ROUNDS, 2, NY, NZ), F32)

    from_y[...] = jnp.zeros(from_y.shape, F32)
    from_xy[...] = jnp.zeros(from_xy.shape, F32)
    from_plane[...] = jnp.zeros(from_plane.shape, F32)
    from_z[...] = jnp.zeros(from_z.shape, F32)
    drag[...] = jnp.zeros(drag.shape, F32)
    zpart[7:8, :] = jnp.zeros((1, NZ), F32)
    zpart[24:25, :] = jnp.zeros((1, NZ), F32)
    pads[1, 1:5, 4:9, 7:8, :] = jnp.zeros((NX, 5, 1, NZ), F32)
    pads[1, 1:5, 12:17, 24:25, :] = jnp.zeros((NX, 5, 1, NZ), F32)

    @pl.when(gx == 0)
    def _():
        from_x[0] = jnp.zeros((4, 2, NY + 16, NZ), F32)

    @pl.when(gx == nx - 1)
    def _():
        from_x[1] = jnp.zeros((4, 2, NY + 16, NZ), F32)

    barrier = pltpu.get_barrier_semaphore()
    core = lax.rem(gz, 2)
    twin = gz + 1 - 2 * core

    def far(step):
        return -sum(min(a, n - a) for a, n in zip(step, sizes))

    line = sorted([(0, k, 0) for k in range(1, ny)], key=far)
    plane = [(a, 0, b) for a in range(nx) for b in range(0, nz, 2) if a or b]
    plane = sorted(plane, key=far)
    pairs = [device(*step) for step in line]
    pairs = [there for step in pairs for there in (step, {**step, "gz": twin})]
    pairs.append({"gx": gx, "gy": gy, "gz": twin})
    corners = [(a, b, c) for a in (1, -1) for b in (1, -1) for c in (1, -1)]
    faces = [(1, 0, 0), (-1, 0, 0), (0, 1, 0), (0, -1, 0)]
    around = [n for n in NEIGHBOURS if n not in faces] + corners + plane
    partners = [device(*n) for n in around] + pairs
    for partner in partners:
        pl.semaphore_signal(barrier, inc=1, device_id=partner, device_id_type=MESH)

    lane = lax.broadcasted_iota(jnp.int32, (8, NZ), 1)
    half = lane // 2
    place = half % 8
    even = lane % 2 == 0
    first, last = lane == 0, lane == NZ - 1
    ends = first | last

    def exchange(turn):
        pad, zs, zr, ze = pads.at[turn], zsend.at[turn], zrecv.at[turn], zedge.at[turn]
        copies = {}
        for number, (dx, dy, dz) in enumerate(NEIGHBOURS):
            if dz == 0:
                if dx > 0:
                    xs, xd, group = 4, 0, slice(0, 5)
                elif dx < 0:
                    xs, xd, group = 1, 5, slice(8, 13)
                else:
                    xs, xd, group = slice(1, 5), slice(1, 5), slice(4, 9) if dy > 0 else slice(12, 17)
                if dy > 0:
                    ys, yd = slice(23, 24), slice(7, 8)
                elif dy < 0:
                    ys, yd = slice(8, 9), slice(24, 25)
                else:
                    ys, yd = slice(8, 24), slice(8, 24)
                if dx and dy:
                    group = SLOT[VELOCITY.index((dx, dy, dz))]
                src, dst = pad.at[xs, group, ys], pad.at[xd, group, yd]
            else:
                s = 0 if dz > 0 else 1
                if dx:
                    src, dst = zs.at[s], ze.at[s, 0 if dx > 0 else 1]
                elif dy > 0:
                    src, dst = zs.at[s, 15:16], zr.at[s, 7:8]
                elif dy < 0:
                    src, dst = zs.at[s, 0:1], zr.at[s, 24:25]
                else:
                    src, dst = zs.at[s], zr.at[s, 8:24]
            copies[(dx, dy, dz)] = pltpu.make_async_remote_copy(
                src_ref=src,
                dst_ref=dst,
                send_sem=send_sem.at[turn, number],
                recv_sem=recv_sem.at[turn, number],
                device_id=device(dx, dy, dz),
                device_id_type=MESH,
            )
        return copies

    exchanges = {turn: exchange(turn) for turn in (0, 3)}

    def part_copies():
        copies = {}

        def copy(key, src, dst):
            number = len(copies)
            copies[key] = pltpu.make_async_remote_copy(
                src_ref=src,
                dst_ref=dst,
                send_sem=part_send.at[number],
                recv_sem=part_recv.at[number],
                device_id=device(*key[0]),
                device_id_type=MESH,
            )

        slabs_of = {1: slice(4, 6), -1: slice(0, 2), 0: slice(0, 6)}
        row_from = {1: slice(23, 25), -1: slice(7, 9), 0: slice(7, 25)}
        row_to = {1: slice(7, 9), -1: slice(23, 25), 0: slice(7, 25)}
        for dx in (1, -1, 0):
            for dy in (1, -1, 0):
                sx, sy = (1 - dx) // 2, (1 - dy) // 2
                if dx or dy:
                    src = part.at[:, slabs_of[dx], row_from[dy]]
                    if dx and dy:
                        dst = from_xy.at[sx, sy, :, :, 7:9]
                    elif dx:
                        dst = from_x.at[sx, :, :, 7:25]
                    else:
                        dst = from_y.at[sy, :, :, 7:9]
                    copy(((dx, dy, 0), "cells"), src, dst)
                    copy(
                        ((dx, dy, 0), "column"),
                        tile.at[row_from[dy]],
                        from_plane.at[1 - dx, 1 - dy, row_to[dy]],
                    )
                for s, dz in ((0, 1), (1, -1)):
                    copy(
                        ((dx, dy, dz), "column"),
                        tile.at[row_from[dy]],
                        from_z.at[s, 1 - dx, 1 - dy, row_to[dy]],
                    )
        return copies

    parts = part_copies()

    def drag_copies():
        copies = {}
        slab_from, slab_to = {1: 4, -1: 1, 0: slice(1, 5)}, {1: 0, -1: 5, 0: slice(1, 5)}
        row_from = {1: slice(23, 24), -1: slice(8, 9), 0: slice(8, 24)}
        row_to = {1: slice(7, 8), -1: slice(24, 25), 0: slice(8, 24)}
        for dx in (1, -1, 0):
            for dy in (1, -1, 0):
                if dx or dy:
                    number = len(copies)
                    copies[(dx, dy, 0)] = pltpu.make_async_remote_copy(
                        src_ref=drag.at[slab_from[dx], row_from[dy]],
                        dst_ref=drag.at[slab_to[dx], row_to[dy]],
                        send_sem=drag_send.at[number],
                        recv_sem=drag_recv.at[number],
                        device_id=device(dx, dy, 0),
                        device_id_type=MESH,
                    )
        return copies

    drags = drag_copies()

    def send_x(turn):
        for (dx, dy, dz), copy in sorted(exchanges[turn].items(), key=lambda item: not item[0][1]):
            if dx and not dz:
                pl.when(exists(dx, dy, dz))(copy.start)

    def send_rest(turn):
        rest = [item for item in exchanges[turn].items() if item[0][2] or not item[0][0]]
        for (dx, dy, dz), copy in sorted(
            rest, key=lambda item: (not item[0][1], -sum(map(abs, item[0])))
        ):
            pl.when(exists(dx, dy, dz))(copy.start)

    def receive(turn):
        for (dx, dy, dz), copy in exchanges[turn].items():
            pl.when(exists(-dx, -dy, -dz))(copy.wait_recv)

    def column_of(index, x, turn):
        up = VELOCITY[index][2] > 0
        k = (ZPLUS if up else ZMINUS).index(index)
        return 16 * k + 2 * (x + 1) + up if turn == 2 else 8 * k + 1 + x

    def gather(turn, x, h):
        values = []
        for index in range(19):
            cx, cy, cz = VELOCITY[index]
            slot = SLOT[index]
            if index == 9 and x > 0:
                slot = TWIN
            start = ROW + 8 * h - cy
            value = pads[turn, x + 1 - cx, slot, start : start + 8, :]
            if cz:
                s = 0 if cz > 0 else 1
                column = column_of(index, x - cx if turn == 2 else (x - cx) % NX, turn)
                if turn == 2:
                    halo = zrecv[2, 0, start : start + 8, :]
                elif 0 <= x - cx < NX:
                    halo = zrecv[turn, s, start : start + 8, :]
                else:
                    halo = zedge[turn, s, 0 if cx > 0 else 1, 8 * h : 8 * h + 8, :]
                value = jnp.where(lane == column, halo, value)
                value = pltpu.roll(value, NZ - column if cz > 0 else NZ - 1 - column, 1)
            values.append(value)
        return values

    def scatter(turn, x, h, values, packed):
        rows = slice(ROW + 8 * h, ROW + 8 * h + 8)
        for index in range(19):
            cz = VELOCITY[index][2]
            value = values[index]
            if cz:
                s = 0 if cz > 0 else 1
                column = column_of(index, x, turn)
                value = pltpu.roll(value, column + 1 if cz > 0 else column, 1)
                packed[s][h] = jnp.where(lane == column, value, packed[s][h])
            pads[turn, x + 1, SLOT[index], rows, :] = value
            if index == 9:
                pads[turn, x + 1, TWIN, rows, :] = value

    def scatter_open(x, h, values, packed):
        rows = slice(ROW + 8 * h, ROW + 8 * h + 8)
        for k in range(5):
            column = 16 * k + 2 * (x + 1)
            both = jnp.where(last, values[ZPLUS[k]], values[ZMINUS[k]])
            packed[h] = jnp.where(half == column // 2, pltpu.roll(both, column + 1, 1), packed[h])
        for index in range(19):
            cz = VELOCITY[index][2]
            value = values[index]
            if cz:
                value = pltpu.roll(value, 1 if cz > 0 else NZ - 1, 1)
                value = jnp.where(first if cz > 0 else last, 0.0, value)
            pads[1, x + 1, TWIN if index == 9 else SLOT[index], rows, :] = value

    def pack_drag(x, h, packed):
        rows = slice(8 * h, 8 * h + 8)
        value = jnp.where(labels[x, rows, :] == 1, design[x, rows, :], 0.0)
        drag[x + 1, ROW + 8 * h : ROW + 8 * h + 8, :] = value
        column = 64 + 2 * (x + 1)
        for s, shift in ((0, column + 1), (1, column)):
            packed[s][h] = jnp.where(lane == column, pltpu.roll(value, shift, 1), packed[s][h])

    def stage(turn, block):
        zero = jnp.zeros((8, NZ), F32)
        packed = [[zero] * HALVES, [zero] * HALVES]
        for x in (0, 3):
            for h in range(HALVES):
                scatter(turn, x, h, block(x, h), packed)
                if turn == 0:
                    pack_drag(x, h, packed)
        if turn == 0:
            pl.semaphore_wait(barrier, len(partners))
        send_x(turn)
        for x in (1, 2):
            for h in range(HALVES):
                scatter(turn, x, h, block(x, h), packed)
                if turn == 0:
                    pack_drag(x, h, packed)
        for s in range(2):
            for h in range(HALVES):
                zsend[turn, s, 8 * h : 8 * h + 8, :] = packed[s][h]
        send_rest(turn)

    def moments(f):
        sums = {i: f[i] + f[i + 1] for i in PAIRS}
        diff = {i: f[i] - f[i + 1] for i in PAIRS}
        density = f[0] + (
            ((sums[1] + sums[3]) + (sums[5] + sums[7]))
            + ((sums[9] + sums[11]) + (sums[13] + (sums[15] + sums[17])))
        )
        jx = diff[1] + ((diff[7] + diff[9]) + (diff[11] + diff[13]))
        jy = diff[3] + ((diff[7] - diff[9]) + (diff[15] + diff[17]))
        jz = diff[5] + ((diff[11] - diff[13]) + (diff[15] - diff[17]))
        return density, jx, jy, jz

    def along(index, v):
        total = None
        for axis in range(3):
            c = VELOCITY[index][axis]
            if c:
                if total is None:
                    total = v[axis]
                else:
                    total = total + v[axis] if c > 0 else total - v[axis]
        return total

    def collide(which, f, x, h):
        rows = slice(8 * h, 8 * h + 8)
        mark = labels[x, rows, :]
        fluid, solid, inlet, outlet = mark == 1, mark == 2, mark == 3, mark == 4
        damping = 1.0 / (1.0 + design[x, rows, :])
        density, jx, jy, jz = moments(f)
        inverse = 1.0 / jnp.where(solid, 1.0, density)
        factor = inverse * jnp.where(fluid, damping, jnp.where(outlet, 1.0, 0.0))
        ux, uy, uz = jx * factor, jy * factor, jnp.where(inlet, INFLOW, jz * factor)
        saved[which, 0, x, rows, :] = ux
        saved[which, 1, x, rows, :] = uy
        saved[which, 2, x, rows, :] = uz
        saved[which, 3, x, rows, :] = jnp.where(
            fluid, RELAX * damping, jnp.where(outlet, inverse, 0.0)
        )
        saved[which, 4, x, rows, :] = jnp.where(fluid, -RELAX * damping * density, 0.0)
        weight = jnp.where(fluid, RELAX * density, 1.0)
        keep = jnp.where(fluid, 1.0 - RELAX, 0.0)
        rest = 1.0 - 1.5 * (ux * ux + uy * uy + uz * uz)
        wide, thin = weight * (1.0 / 18.0), weight * (1.0 / 36.0)
        post = [None] * 19
        post[0] = jnp.where(solid, f[0], keep * f[0] + (weight * (1.0 / 3.0)) * rest)
        for i in PAIRS:
            w = wide if i < 7 else thin
            cu = along(i, (ux, uy, uz))
            even = w * (rest + 4.5 * (cu * cu))
            odd = w * (3.0 * cu)
            post[i] = jnp.where(solid, f[i + 1], keep * f[i] + (even + odd))
            post[i + 1] = jnp.where(solid, f[i], keep * f[i + 1] + (even - odd))
        return post

    def transpose(which, g, x, h):
        rows = slice(8 * h, 8 * h + 8)
        mark = labels[x, rows, :]
        fluid, solid = mark == 1, mark == 2
        u = [saved[which, a, x, rows, :] for a in range(3)]
        gain, slope = saved[which, 3, x, rows, :], saved[which, 4, x, rows, :]
        ux, uy, uz = u
        s = {i: g[i] + g[i + 1] for i in PAIRS}
        d = {i: g[i] - g[i + 1] for i in PAIRS}
        wide, thin = 1.0 / 18.0, 1.0 / 36.0
        sxy, sxz, syz = s[7] + s[9], s[11] + s[13], s[15] + s[17]
        m0 = (
            (1.0 / 3.0) * g[0]
            + wide * (s[1] + s[3] + s[5])
            + thin * (sxy + sxz + syz)
        )
        m1x = wide * d[1] + thin * ((d[7] + d[9]) + (d[11] + d[13]))
        m1y = wide * d[3] + thin * ((d[7] - d[9]) + (d[15] + d[17]))
        m1z = wide * d[5] + thin * ((d[11] - d[13]) + (d[15] - d[17]))
        mxx = wide * s[1] + thin * (sxy + sxz)
        myy = wide * s[3] + thin * (sxy + syz)
        mzz = wide * s[5] + thin * (sxz + syz)
        mxy = thin * (s[7] - s[9])
        mxz = thin * (s[11] - s[13])
        myz = thin * (s[15] - s[17])
        hx = mxx * ux + mxy * uy + mxz * uz
        hy = mxy * ux + myy * uy + myz * uz
        hz = mxz * ux + myz * uy + mzz * uz
        quad = ux * hx + uy * hy + uz * hz
        square = ux * ux + uy * uy + uz * uz
        bx = 3.0 * (m1x - ux * m0) + 9.0 * hx
        by = 3.0 * (m1y - uy * m0) + 9.0 * hy
        bz = 3.0 * (m1z - uz * m0) + 9.0 * hz
        bu = bx * ux + by * uy + bz * uz
        base = jnp.where(
            fluid, RELAX * (m0 + 1.5 * square * m0 - 4.5 * quad), -(bu * gain)
        )
        e = (bx * gain, by * gain, bz * gain)
        keep = jnp.where(fluid, 1.0 - RELAX, 0.0)
        back = [None] * 19
        back[0] = jnp.where(solid, g[0], keep * g[0] + base)
        for i in PAIRS:
            ce = along(i, e)
            back[i] = jnp.where(solid, g[i + 1], keep * g[i] + (base + ce))
            back[i + 1] = jnp.where(solid, g[i], keep * g[i + 1] + (base - ce))
        return back, slope * bu

    def reverse(values):
        return [values[OPPOSITE[i]] for i in range(19)]

    for copy in loads:
        copy.wait()
    waited = set()

    def block_one(x, h):
        if x not in waited:
            slabs[x].wait()
            waited.add(x)
        f = [pop[x, i, 8 * h : 8 * h + 8, :] for i in range(19)]
        return collide(0, f, x, h)

    stage(0, block_one)

    for offset, copy in drags.items():
        pl.when(exists(*offset))(copy.start)

    receive(0)
    zero = jnp.zeros((8, NZ), F32)
    packed = [zero] * HALVES
    for x in range(NX):
        for h in range(HALVES):
            values = collide(1, gather(0, x, h), x, h)
            scatter_open(x, h, values, packed)
    for h in range(HALVES):
        zpart[ROW + 8 * h : ROW + 8 * h + 8, :] = packed[h]

    def added_up(terms):
        out = [None] * 4
        for index, value in terms:
            for f, c in enumerate((1,) + VELOCITY[index]):
                if c:
                    if out[f] is None:
                        out[f] = value if c > 0 else -value
                    else:
                        out[f] = out[f] + value if c > 0 else out[f] - value
        return [zero if value is None else value for value in out]

    def reaches(h, cy):
        return 0 <= h < HALVES or (h < 0 and cy < 0) or (h >= HALVES and cy > 0)

    def own_part(x, h):
        terms = []
        for index in range(19):
            cx, cy, _ = VELOCITY[index]
            if 0 <= x - cx < NX and reaches(h, cy):
                slot = TWIN if index == 9 else SLOT[index]
                start = ROW + 8 * h - cy
                terms.append((index, pads[1, x + 1 - cx, slot, start : start + 8, :]))
        if len(terms) == 19:
            return moments([value for _, value in terms])
        return added_up(terms)

    BLOCKS = range(-1, HALVES + 1)
    tiles = [zero for _ in BLOCKS]

    def part_slab(x):
        for h in BLOCKS:
            rows = slice(ROW + 8 * h, ROW + 8 * h + 8)
            for f, value in enumerate(own_part(x, h)):
                part[f, x + 1, rows, :] = value
                column = 64 + 16 * f + 2 * (x + 1)
                tiles[h + 1] = jnp.where(
                    half == column // 2, pltpu.roll(value, column + 1, 1), tiles[h + 1]
                )

    for x in (-1, 0, 3, 4):
        part_slab(x)
    for (offset, kind), copy in parts.items():
        if kind == "cells" and offset[0]:
            pl.when(exists(*offset))(copy.start)
    for x in (1, 2):
        part_slab(x)
    for (offset, kind), copy in parts.items():
        if kind == "cells" and not offset[0]:
            pl.when(exists(*offset))(copy.start)

    for h in BLOCKS:
        terms = []
        for k, index in enumerate(ZPLUS):
            cx, cy, _ = VELOCITY[index]
            value = zero
            if reaches(h, cy):
                start = ROW + 8 * h - cy
                value = zpart[start : start + 8, :]
                shift = (2 * cx - 16 * k) % NZ
                value = pltpu.roll(value, shift, 1) if shift else value
            terms.append(value)
        weight = (terms[0] + (terms[1] + terms[2])) + (terms[3] + terms[4])
        sums = (weight, terms[1] - terms[2], terms[3] - terms[4], jnp.where(even, weight, -weight))
        for f, value in enumerate(sums):
            value = jnp.where(lane < 16, value, 0.0)
            tiles[h + 1] = tiles[h + 1] + (pltpu.roll(value, 16 * f, 1) if f else value)
        tile[ROW + 8 * h : ROW + 8 * h + 8, :] = tiles[h + 1]
    columns = [item for item in parts.items() if item[0][1] == "column"]
    for (offset, _), copy in sorted(columns, key=lambda item: -sum(map(abs, item[0][0]))):
        pl.when(exists(*offset))(copy.start)

    for (dx, dy, dz), copy in drags.items():
        pl.when(exists(-dx, -dy, -dz))(copy.wait_recv)
    for ((dx, dy, dz), _), copy in parts.items():
        pl.when(exists(-dx, -dy, -dz))(copy.wait_recv)

    def all_around(read, h, middle=None):
        rows = slice(ROW + 8 * h, ROW + 8 * h + 8)
        sums = []
        for a in range(3):
            terms = [middle if middle is not None and a == b == 1 else read(a, b, rows) for b in range(3)]
            sums.append((terms[0] + terms[1]) + terms[2])
        below, above = pltpu.roll(sums[0], NZ - 8, 1), pltpu.roll(sums[2], 8, 1)
        return sums[1] + jnp.where(
            place < 2, below, jnp.where((place == 4) | (place == 5), above, 0.0)
        )

    through = [[all_around(lambda a, b, r, s=s: from_z[s, a, b, r, :], h) for h in BLOCKS] for s in range(2)]
    inward = [jnp.where(even, low, pltpu.roll(high, NZ - 2, 1)) for low, high in zip(*through)]
    lost = []

    def gradient(solidity, seen, density, momentum):
        inverse = jnp.where(seen, 1.0 / jnp.where(seen, density, 1.0), 0.0)
        v = [m * inverse for m in momentum]
        square = v[0] * v[0] + v[1] * v[1] + v[2] * v[2]
        twice = 20.0 * solidity
        return square, -10.0 * solidity * square, [twice * a for a in v]

    for x in (0, 1, 2, 3, -1, 4):
        for h in BLOCKS:
            rows = slice(ROW + 8 * h, ROW + 8 * h + 8)
            total = []
            for f in range(4):
                value = part[f, x + 1, rows, :]
                if x < 1:
                    value = value + from_x[0, f, x + 1, rows, :]
                if x > 2:
                    value = value + from_x[1, f, x - 3, rows, :]
                side = 0 if h < 1 else 1
                near = slice(8 * (h + 1 - 2 * side), 8 * (h + 1 - 2 * side) + 8)
                value = value + from_y[side, f, x + 1, near, :]
                if x < 1:
                    value = value + from_xy[0, side, f, x + 1, near, :]
                if x > 2:
                    value = value + from_xy[1, side, f, x - 3, near, :]
                column = 16 * f + 2 * (x + 1)
                turned = pltpu.roll(inward[h + 1], NZ - column, 1) if column else inward[h + 1]
                value = value + jnp.where(ends, turned, 0.0)
                total.append(value)
            if 0 <= x < NX and 0 <= h < HALVES:
                own = slice(8 * h, 8 * h + 8)
                solidity, seen = design[x, own, :], labels[x, own, :] == 1
            else:
                solidity = drag[x + 1, rows, :]
                seen = solidity > 0.0
            square, base, e = gradient(solidity, seen, total[0], total[1:])
            if 0 <= x < NX and 0 <= h < HALVES:
                direct = 10.0 * total[0] * square
                raw[x, own, :] = direct
                lost.append(solidity * direct)
            for index in range(19):
                cx, cy, cz = VELOCITY[index]
                if not (0 <= x + cx < NX and (0 <= h < HALVES or (cy > 0 if h < 0 else cy < 0))):
                    continue
                value = base
                for c, a in zip((cx, cy, cz), e):
                    if c:
                        value = value - a if c > 0 else value + a
                if cz:
                    value = pltpu.roll(value, column_of(index, x, 2) + (cz > 0), 1)
                pads[2, x + 1, SLOT[index], rows, :] = value
                if index == 9:
                    pads[2, x + 1, TWIN, rows, :] = value

    for h in BLOCKS:
        rows = slice(ROW + 8 * h, ROW + 8 * h + 8)
        about = all_around(lambda a, b, r: from_plane[a, b, r, :], h, tile[rows, :])
        about = about + jnp.where(
            even,
            pltpu.roll(through[1][h + 1], NZ - 65, 1),
            pltpu.roll(through[0][h + 1], NZ - 63, 1),
        )
        total = [about] + [pltpu.roll(about, NZ - 16 * f, 1) for f in range(1, 4)]

        def drags_at(low, high, column):
            return jnp.where(
                even, pltpu.roll(high, NZ - column, 1), pltpu.roll(low, NZ + 1 - column, 1)
            )

        solidity = drags_at(zrecv[0, 0, rows, :], zrecv[0, 1, rows, :], 64)
        if 0 <= h < HALVES:
            own = slice(8 * h, 8 * h + 8)
            below = drags_at(zedge[0, 0, 0, own, :], zedge[0, 1, 0, own, :], 72)
            above = drags_at(zedge[0, 0, 1, own, :], zedge[0, 1, 1, own, :], 56)
            solidity = jnp.where(place == 0, below, jnp.where(place == 5, above, solidity))
        _, base, e = gradient(solidity, solidity > 0.0, total[0], total[1:])
        base = base + jnp.where(even, e[2], -e[2])
        out = None
        for k, index in enumerate(ZPLUS):
            value = base
            for c, a in zip(VELOCITY[index][:2], e):
                if c:
                    value = value - a if c > 0 else value + a
            out = value if k == 0 else jnp.where(lane >= 16 * k, pltpu.roll(value, 16 * k, 1), out)
        zrecv[2, 0, rows, :] = out

    def block_two(x, h):
        rows = slice(8 * h, 8 * h + 8)
        back, sens = transpose(1, reverse(gather(2, x, h)), x, h)
        raw[x, rows, :] = raw[x, rows, :] + sens
        return reverse(back)

    stage(3, block_two)

    receive(3)
    sizes_of = jnp.zeros((8, NZ), F32)
    for x in range(NX):
        for h in range(HALVES):
            rows = slice(8 * h, 8 * h + 8)
            _, sens = transpose(0, reverse(gather(3, x, h)), x, h)
            total = raw[x, rows, :] + sens
            raw[x, rows, :] = total
            sizes_of = sizes_of + jnp.abs(total)

    lost_of = lost[0]
    for term in lost[1:]:
        lost_of = lost_of + term
    left = lax.broadcasted_iota(jnp.int32, (1, NZ), 1) < NZ // 2

    def folded(value):
        value = value + pltpu.roll(value, NZ // 2, 1)
        return jnp.sum(value, axis=0, keepdims=True)

    mine = jnp.where(left, folded(lost_of), folded(sizes_of))

    def spread(buffer, me, targets, base):
        buffer[pl.ds(me, 1), :] = mine
        copies = []
        for number, target in enumerate(targets):
            copies.append(
                pltpu.make_async_remote_copy(
                    src_ref=buffer.at[pl.ds(me, 1)],
                    dst_ref=buffer.at[pl.ds(me, 1)],
                    send_sem=red_send.at[base + number],
                    recv_sem=red_recv.at[base + number],
                    device_id=target,
                    device_id_type=MESH,
                )
            )
        for copy in copies:
            copy.start()
        return copies

    def added(buffer, copies):
        for copy in copies:
            copy.wait_recv()
        return jnp.sum(buffer[...], axis=0, keepdims=True)

    sent = spread(red_y, gy * 2 + core, pairs, 0)
    stores = [pltpu.make_async_copy(raw, raw_hbm, store_sem.at[NX])]
    stores[0].start()
    for x in range(NX):
        for h in range(HALVES):
            rows = slice(8 * h, 8 * h + 8)
            back, _ = transpose(0, reverse(gather(3, x, h)), x, h)
            for i in range(19):
                adj[x, i, rows, :] = back[i]
        stores.append(pltpu.make_async_copy(adj.at[x], adj_hbm.at[:, x], store_sem.at[x]))
        stores[-1].start()
    for turn in exchanges:
        for (dx, dy, dz), copy in exchanges[turn].items():
            pl.when(exists(dx, dy, dz))(copy.wait_send)
    for offset, copy in drags.items():
        pl.when(exists(*offset))(copy.wait_send)
    for (offset, _), copy in parts.items():
        pl.when(exists(*offset))(copy.wait_send)
    mine = added(red_y, sent)
    last_sent = spread(red_p, gx * (nz // 2) + gz // 2, [device(*step) for step in plane], len(pairs))
    for copy in stores:
        copy.wait()
    for copy in sent:
        copy.wait_send()
    mine = added(red_p, last_sent)

    cells = NX * NY * NZ * nx * ny * nz
    loss = jnp.sum(jnp.where(left, mine, 0.0))
    size = jnp.sum(jnp.where(left, 0.0, mine))
    sums_ref[0] = 20.0 * loss / cells
    sums_ref[1] = size / cells + 1e-06

    for copy in last_sent:
        copy.wait_send()


def finish(sums_in, adj_in, raw_in, adj_out, sens_out, obj_out, raw, adj, sums, sem):
    cuts = [19 * k // PIECES for k in range(PIECES + 1)]
    loads = [
        pltpu.make_async_copy(sums_in, sums, sem.at[2 * PIECES]),
        pltpu.make_async_copy(raw_in, raw, sem.at[2 * PIECES + 1]),
    ]
    coming, going = [], []
    for k in range(PIECES):
        part = slice(cuts[k], cuts[k + 1])
        coming.append(pltpu.make_async_copy(adj_in.at[part], adj.at[part], sem.at[k]))
        going.append(
            pltpu.make_async_copy(adj.at[part], adj_out.at[part], sem.at[PIECES + k])
        )
        coming[k].start()
    for copy in loads:
        copy.start()
    for k in range(PIECES):
        coming[k].wait()
        going[k].start()
    for copy in loads:
        copy.wait()
    obj_out[0] = sums[0]
    inverse = 1.0 / jnp.full((8, NZ), sums[1], F32)
    for x in range(NX):
        for h in range(HALVES):
            rows = slice(8 * h, 8 * h + 8)
            raw[x, rows, :] = raw[x, rows, :] * inverse
    store = pltpu.make_async_copy(raw, sens_out, sem.at[2 * PIECES + 2])
    store.start()
    for k in range(PIECES):
        going[k].wait()
    store.wait()


def solution(mesh):
    nx, ny, nz = (mesh.shape[a] for a in ("gx", "gy", "gz"))
    partners = nx * nz // 2 + 2 * ny - 2

    def body(populations, design, labels):
        cells = (NX, NY, NZ)
        adjoint, raw, sums = pl.pallas_call(
            lambda *refs: kernel((nx, ny, nz), *refs),
            out_shape=(
                jax.ShapeDtypeStruct((19,) + cells, F32),
                jax.ShapeDtypeStruct(cells, F32),
                jax.ShapeDtypeStruct((2,), F32),
            ),
            in_specs=[pl.BlockSpec(memory_space=pltpu.HBM)] * 3,
            out_specs=(
                pl.BlockSpec(memory_space=pltpu.HBM),
                pl.BlockSpec(memory_space=pltpu.HBM),
                pl.BlockSpec(memory_space=pltpu.SMEM),
            ),
            scratch_shapes=[
                pltpu.VMEM((NX, 19, NY, NZ), F32),
                pltpu.VMEM(cells, F32),
                pltpu.VMEM(cells, jnp.int32),
                pltpu.VMEM((NX, 19, NY, NZ), F32),
                pltpu.VMEM((ROUNDS, NX + 2, 20, NY + 16, NZ), F32),
                pltpu.VMEM((ROUNDS, 2, NY, NZ), F32),
                pltpu.VMEM((ROUNDS, 2, NY + 16, NZ), F32),
                pltpu.VMEM((ROUNDS, 2, 2, NY, NZ), F32),
                pltpu.VMEM((2, 5) + cells, F32),
                pltpu.VMEM(cells, F32),
                pltpu.VMEM((4, NX + 2, NY + 16, NZ), F32),
                pltpu.VMEM((NY + 16, NZ), F32),
                pltpu.VMEM((NY + 16, NZ), F32),
                pltpu.VMEM((2, 4, 2, NY + 16, NZ), F32),
                pltpu.VMEM((2, 4, NX + 2, 16, NZ), F32),
                pltpu.VMEM((2, 2, 4, 2, 16, NZ), F32),
                pltpu.VMEM((3, 3, NY + 16, NZ), F32),
                pltpu.VMEM((2, 3, 3, NY + 16, NZ), F32),
                pltpu.VMEM((NX + 2, NY + 16, NZ), F32),
                pltpu.VMEM((nx * nz // 2, NZ), F32),
                pltpu.VMEM((2 * ny, NZ), F32),
                pltpu.SemaphoreType.DMA((6,)),
                pltpu.SemaphoreType.DMA((NX + 1,)),
                pltpu.SemaphoreType.DMA((ROUNDS, 18)),
                pltpu.SemaphoreType.DMA((ROUNDS, 18)),
                pltpu.SemaphoreType.DMA((34,)),
                pltpu.SemaphoreType.DMA((34,)),
                pltpu.SemaphoreType.DMA((8,)),
                pltpu.SemaphoreType.DMA((8,)),
                pltpu.SemaphoreType.DMA((partners,)),
                pltpu.SemaphoreType.DMA((partners,)),
            ],
            compiler_params=pltpu.CompilerParams(
                collective_id=0, has_side_effects=True, vmem_limit_bytes=60 * 1024 * 1024
            ),
            cost_estimate=pl.CostEstimate(
                flops=10_000_000, bytes_accessed=1_500_000, transcendentals=0
            ),
        )(populations, design, labels)
        adjoint, sensitivity, objective = pl.pallas_call(
            finish,
            out_shape=(
                jax.ShapeDtypeStruct((19,) + cells, F32),
                jax.ShapeDtypeStruct(cells, F32),
                jax.ShapeDtypeStruct((1,), F32),
            ),
            in_specs=[
                pl.BlockSpec(memory_space=pltpu.HBM),
                pl.BlockSpec(memory_space=pltpu.HBM),
                pl.BlockSpec(memory_space=pltpu.HBM),
            ],
            out_specs=(
                pl.BlockSpec(memory_space=pltpu.HBM),
                pl.BlockSpec(memory_space=pltpu.HBM),
                pl.BlockSpec(memory_space=pltpu.SMEM),
            ),
            scratch_shapes=[
                pltpu.VMEM(cells, F32),
                pltpu.VMEM((19,) + cells, F32),
                pltpu.SMEM((2,), F32),
                pltpu.SemaphoreType.DMA((2 * PIECES + 3,)),
            ],
            compiler_params=pltpu.CompilerParams(vmem_limit_bytes=60 * 1024 * 1024),
        )(sums, adjoint, raw)
        return adjoint, sensitivity, objective.reshape(())

    in_specs = (P(None, "gx", "gy", "gz"), P("gx", "gy", "gz"), P("gx", "gy", "gz"))
    out_specs = (P(None, "gx", "gy", "gz"), P("gx", "gy", "gz"), P())
    return jax.shard_map(body, mesh=mesh, in_specs=in_specs, out_specs=out_specs, check_vma=False)
```
